32 devices in a mesh: head: 4 (over y, x), seq: 8 (over z, core).
Axes of the slice: x: 2, y: 2, z: 4, core: 2. Of those that a mesh axis runs over, the one named last changes fastest.
Arguments:
- tokens: bfloat16 [32, 1024, 768], P('seq', 'head'), may hold values from -6 to 6
- cotangent: bfloat16 [32, 1024, 768], P('seq', 'head')
- segment_ids: int32 [32, 1024], P('seq'), may hold values from 0 to 1024, as said below
- owner_order: int32 [192], replicated, may hold values from 0 to 191, as said below
- master_blocks: float32 [192, 192, 192], P('seq')
- momentum: float32 [192, 192, 192], P('seq')
- stat_left: float32 [192, 192, 192], P('seq')
- stat_right: float32 [192, 192, 192], P('seq')
- root_left: float32 [192, 192, 192], P('seq')
- root_right: float32 [192, 192, 192], P('seq')
- vectors: float32 [9216], replicated
- vec_first: float32 [9216], replicated
- vec_second: float32 [9216], replicated, as said below
Outputs:
- output: bfloat16 [32, 1024, 768], P('seq', 'head')
- input_grad: float32 [32, 1024, 768], P('seq', 'head')
- new_momentum: float32 [192, 192, 192], P('seq')
- new_left: float32 [192, 192, 192], P('seq')
- new_right: float32 [192, 192, 192], P('seq')
- new_master: float32 [192, 192, 192], P('seq')
- new_first: float32 [9216], replicated
- new_second: float32 [9216], replicated
- new_vectors: float32 [9216], replicated
The draws below stay inside these ranges and needn't reach their ends.
Inputs may be any that keep to these rules, and one draw needn't show every extreme that they name: `segment_ids`: along each row the numbers start at 0 and rise by one from one document to the next; a document has 1 to 512 positions and some row holds one of exactly 512; every row ends in padding of one position or more, marked 1024. `owner_order`: A permutation of 0 to 191. `vec_second`: Positive.
All inputs are finite; a program needn't handle non-finite values.
Results may differ from the reference program's by a relative error of at most 0.01.
The reference program's roundings to bfloat16 on the way count: a program that leaves them out, or rounds other values in their place, can miss the bound.
Values may be sent and summed in bfloat16 or wider, within the bound.
No kernel may reach another device: no remote copies, remote signals or barrier semaphores. Data moves between devices by JAX's collectives and lax.ppermute only.
A program may use at most 256 MiB of HBM per device.

```python
import math
import jax
import jax.numpy as jnp
from jax import lax

MODEL_WIDTH = 768
HEAD_TOTAL = 12
HEAD_SIZE = 64
FF = 3072
ROW_POSITIONS = 1024
DOCUMENT_LIMIT = 512
QUERY_GROUP = 512
B = 192
STEP = 10
PACKED_ROWS = 32
NBLK = 192
VECLEN = 9216


def grad_scale():
    return 0.35 * math.sqrt(PACKED_ROWS * ROW_POSITIONS)


def vector_scale():
    factors = [0.7, 0.7, 1.0, 1.0, 0.3, 0.6, 0.7, 0.8]
    fragment_list = [jnp.full((MODEL_WIDTH,), factor, jnp.float32) for factor in factors]
    fragment_list = fragment_list + [jnp.full((FF,), 0.25, jnp.float32)]
    return jnp.concatenate(fragment_list) * math.sqrt(PACKED_ROWS * ROW_POSITIONS)


def owner_perm(key):
    return jax.random.permutation(jax.random.fold_in(key, 5), NBLK).astype(jnp.int32)


def definite(random_portion, diagonal):
    symmetric = (random_portion + jnp.transpose(random_portion, (0, 2, 1))) * (0.15 / math.sqrt(B))
    return symmetric + jnp.eye(B, dtype=jnp.float32) * diagonal[:, :, None]


def draw_owner_order(key, part):
    return owner_perm(key)


def draw_master_blocks(key, part):
    ordering = owner_perm(key)
    key = jax.random.fold_in(key, 21)
    width_blocks = MODEL_WIDTH // B
    attention_end = width_blocks * 3 * width_blocks
    output_end = attention_end + width_blocks * width_blocks
    upward_end = output_end + width_blocks * (FF // B)
    scales = jnp.where(ordering < attention_end, MODEL_WIDTH ** (-0.5), jnp.where(ordering < output_end, (MODEL_WIDTH // 8) ** (-0.5), jnp.where(ordering < upward_end, MODEL_WIDTH ** (-0.5), FF ** (-0.5))))
    random_portion = jax.random.normal(key, (NBLK, B, B), jnp.float32)
    return random_portion * scales[:, None, None].astype(jnp.float32)


def draw_momentum(key, part):
    key = jax.random.fold_in(key, 31)
    return jax.random.normal(key, (NBLK, B, B), jnp.float32) * grad_scale()


def draw_stat_left(key, part):
    key = jax.random.fold_in(key, 41)
    initial_random_key, key_number_two = jax.random.split(key)
    random_portion = jax.random.normal(initial_random_key, (NBLK, B, B), jnp.float32)
    diagonal = jax.random.uniform(key_number_two, (NBLK, B), jnp.float32, 1.0, 4.0)
    return definite(random_portion, diagonal) * (B * grad_scale() ** 2)


def draw_stat_right(key, part):
    key = jax.random.fold_in(key, 42)
    initial_random_key, key_number_two = jax.random.split(key)
    random_portion = jax.random.normal(initial_random_key, (NBLK, B, B), jnp.float32)
    diagonal = jax.random.uniform(key_number_two, (NBLK, B), jnp.float32, 1.0, 4.0)
    return definite(random_portion, diagonal) * (B * grad_scale() ** 2)


def draw_root_left(key, part):
    key = jax.random.fold_in(key, 43)
    initial_random_key, key_number_two = jax.random.split(key)
    random_portion = jax.random.normal(initial_random_key, (NBLK, B, B), jnp.float32)
    diagonal = jax.random.uniform(key_number_two, (NBLK, B), jnp.float32, 0.6, 1.2)
    return definite(random_portion, diagonal) * (B * grad_scale() ** 2) ** (-0.25)


def draw_root_right(key, part):
    key = jax.random.fold_in(key, 44)
    initial_random_key, key_number_two = jax.random.split(key)
    random_portion = jax.random.normal(initial_random_key, (NBLK, B, B), jnp.float32)
    diagonal = jax.random.uniform(key_number_two, (NBLK, B), jnp.float32, 0.6, 1.2)
    return definite(random_portion, diagonal) * (B * grad_scale() ** 2) ** (-0.25)


def draw_cotangent(key, part):
    key = jax.random.fold_in(key, 61)
    random_portion = jax.random.normal(key, (PACKED_ROWS, ROW_POSITIONS, MODEL_WIDTH), jnp.float32)
    row_place = (jnp.arange(PACKED_ROWS, dtype=jnp.float32) + 0.5) / PACKED_ROWS
    seat_location = (jnp.arange(ROW_POSITIONS, dtype=jnp.float32) + 0.5) / ROW_POSITIONS
    ramp_rows = (0.5 + 2.5 * row_place) / 1.89
    ramp_seats = (0.5 + 2.5 * seat_location) / 1.89
    return (random_portion * ramp_rows[:, None, None] * ramp_seats[None, :, None]).astype(jnp.bfloat16)


def draw_segment_ids(key, part):
    key = jax.random.fold_in(key, 11)
    initial_random_key, key_number_two, third_key, key_number_four = jax.random.split(key, 4)
    power_value = jax.random.randint(initial_random_key, (PACKED_ROWS, ROW_POSITIONS), 2, DOCUMENT_LIMIT.bit_length(), jnp.int32)
    upper_limit = jnp.left_shift(jnp.ones_like(power_value), power_value)
    document_lengths = jax.random.randint(key_number_two, (PACKED_ROWS, ROW_POSITIONS), 1, upper_limit + 1, jnp.int32)
    document_lengths = jnp.minimum(document_lengths, DOCUMENT_LIMIT)
    big_row = jax.random.randint(third_key, (), 0, PACKED_ROWS, jnp.int32)
    slot_entries = jnp.arange(ROW_POSITIONS, dtype=jnp.int32)[None, :]
    row_numbers = jnp.arange(PACKED_ROWS, dtype=jnp.int32)[:, None]
    document_lengths = jnp.where((row_numbers == big_row) & (slot_entries == 0), DOCUMENT_LIMIT, document_lengths)
    doc_ends = jnp.cumsum(document_lengths, axis=1).astype(jnp.int32)
    position_indices = jnp.arange(ROW_POSITIONS, dtype=jnp.int32)
    segment_labels = jax.vmap(lambda doc_ends_row: jnp.searchsorted(doc_ends_row, position_indices, side='right'))(doc_ends)
    segment_labels = segment_labels.astype(jnp.int32)
    remaining_length = 1 + jax.random.randint(key_number_four, (PACKED_ROWS, 1), 0, ROW_POSITIONS // 4, jnp.int32)
    usable_length = ROW_POSITIONS - remaining_length
    return jnp.where(position_indices[None, :] < usable_length, segment_labels, ROW_POSITIONS).astype(jnp.int32)


def draw_vectors(key, part):
    key = jax.random.fold_in(key, 71)
    gain_key, shift_key = jax.random.split(key)
    gain_values = jax.random.uniform(gain_key, (VECLEN,), jnp.float32, 0.7, 1.3)
    shifts = jax.random.normal(shift_key, (VECLEN,), jnp.float32) * 0.3
    position_indices = jnp.arange(VECLEN)
    is_gain = (position_indices < MODEL_WIDTH) | (position_indices >= 2 * MODEL_WIDTH) & (position_indices < 3 * MODEL_WIDTH)
    return jnp.where(is_gain, gain_values, shifts)


def draw_vec_first(key, part):
    key = jax.random.fold_in(key, 81)
    return jax.random.normal(key, (VECLEN,), jnp.float32) * (0.1 / 0.9) * vector_scale()


def draw_vec_second(key, part):
    key = jax.random.fold_in(key, 91)
    factors = jax.random.uniform(key, (VECLEN,), jnp.float32, 1.0, 4.0)
    return factors * (0.001 / 0.999) * vector_scale() ** 2


def block_scale(rng, dims, cuts, low, high):
    factor_of = 1.0
    for position, parts in cuts:
        steps = jax.random.uniform(jax.random.fold_in(jax.random.fold_in(rng, 6), position), (parts,), jnp.float32, low / len(cuts), high / len(cuts))
        factor_of = factor_of * jnp.repeat(jnp.exp(steps), dims[position] // parts).reshape((-1,) + (1,) * (len(dims) - 1 - position))
    return factor_of


def bell_draw(rng, dims, deviation, reach, cuts=(), held_as=jnp.bfloat16):
    loudness = block_scale(rng, dims, cuts, -0.22, 0.18) if cuts else 1.0
    entries = jax.random.normal(rng, dims, jnp.float32) * deviation * loudness
    return jnp.minimum(jnp.maximum(entries, -reach), reach).astype(held_as)


def setup_inputs(seed: int = 0) -> dict:
    keys = jax.random.split(jax.random.key(seed), 14)
    return {
        "tokens": bell_draw(keys[0], (PACKED_ROWS, ROW_POSITIONS, MODEL_WIDTH), 1.0, 6.0, ((0, 8), (1, 4))),
        "cotangent": draw_cotangent(jax.random.fold_in(keys[13], 71), 0),
        "segment_ids": draw_segment_ids(jax.random.fold_in(keys[13], 71), 0),
        "owner_order": draw_owner_order(jax.random.fold_in(keys[13], 71), 0),
        "master_blocks": draw_master_blocks(jax.random.fold_in(keys[13], 71), 0),
        "momentum": draw_momentum(jax.random.fold_in(keys[13], 71), 0),
        "stat_left": draw_stat_left(jax.random.fold_in(keys[13], 71), 0),
        "stat_right": draw_stat_right(jax.random.fold_in(keys[13], 71), 0),
        "root_left": draw_root_left(jax.random.fold_in(keys[13], 71), 0),
        "root_right": draw_root_right(jax.random.fold_in(keys[13], 71), 0),
        "vectors": draw_vectors(jax.random.fold_in(keys[13], 71), 0),
        "vec_first": draw_vec_first(jax.random.fold_in(keys[13], 71), 0),
        "vec_second": draw_vec_second(jax.random.fold_in(keys[13], 71), 0),
    }


@jax.custom_vjp
def reduced_precision(v):
    return lax.optimization_barrier(v.astype(jnp.bfloat16)).astype(jnp.float32)

@jax.custom_vjp
def reduced_backward(v):
    return v

def low_keep(v):
    return (reduced_precision(v), None)

def low_pass(kept, grad):
    return (grad,)

def back_keep(v):
    return (v, None)

def back_low(kept, grad):
    return (reduced_precision(grad),)
reduced_precision.defvjp(low_keep, low_pass)
reduced_backward.defvjp(back_keep, back_low)
HIGHEST_PRECISION = lax.Precision.HIGHEST
NORM_EPSILON = 1e-05
STAT_DECAY = 0.5
MOMENTUM_DECAY = 0.5
MATRIX_RATE = 1.0
WEIGHT_DECAY = 0.01
FIRST_DECAY = 0.9
SECOND_DECAY = 0.999
VECTOR_RATE = 0.3
ADAM_EPSILON = 1e-08

def matmul(left_side, right_side):
    return jnp.dot(left_side, right_side, precision=HIGHEST_PRECISION, preferred_element_type=jnp.float32)

def layer_norm(hidden, scaling, offset):
    center = hidden - lax.optimization_barrier(jnp.mean(hidden, axis=-1, keepdims=True))
    variance = lax.optimization_barrier(jnp.mean(center * center, axis=-1, keepdims=True))
    return center * lax.rsqrt(variance + NORM_EPSILON) * scaling + offset

def unpack(vectors):
    fragment_list = [vectors[number * MODEL_WIDTH:(number + 1) * MODEL_WIDTH] for number in range(8)]
    return fragment_list + [vectors[8 * MODEL_WIDTH:]]

def to_matrix(blocks, row_blocks, column_blocks):
    shaped = blocks.reshape(row_blocks, column_blocks, B, B).transpose(0, 2, 1, 3)
    return shaped.reshape(row_blocks * B, column_blocks * B)

def to_blocks(matrix):
    row_blocks = matrix.shape[0] // B
    column_blocks = matrix.shape[1] // B
    shaped = matrix.reshape(row_blocks, B, column_blocks, B).transpose(0, 2, 1, 3)
    return shaped.reshape(row_blocks * column_blocks, B, B)

def split_blocks(blocks):
    width_blocks = MODEL_WIDTH // B
    hidden_blocks = FF // B
    attention_end = width_blocks * 3 * width_blocks
    output_end = attention_end + width_blocks * width_blocks
    upward_end = output_end + width_blocks * hidden_blocks
    return (to_matrix(blocks[:attention_end], width_blocks, 3 * width_blocks), to_matrix(blocks[attention_end:output_end], width_blocks, width_blocks), to_matrix(blocks[output_end:upward_end], width_blocks, hidden_blocks), to_matrix(blocks[upward_end:], hidden_blocks, width_blocks))

def shampoo_step(grad_blocks, momentum, stat_left, stat_right, root_left, root_right, master_blocks):
    new_momentum = MOMENTUM_DECAY * momentum + (1.0 - MOMENTUM_DECAY) * grad_blocks
    new_left = STAT_DECAY * stat_left + (1.0 - STAT_DECAY) * jnp.einsum('bij,bkj->bik', grad_blocks, grad_blocks, precision=HIGHEST_PRECISION)
    new_right = STAT_DECAY * stat_right + (1.0 - STAT_DECAY) * jnp.einsum('bji,bjk->bik', grad_blocks, grad_blocks, precision=HIGHEST_PRECISION)
    leftward = jnp.einsum('bij,bjk->bik', root_left, new_momentum, precision=HIGHEST_PRECISION)
    preconditioned = jnp.einsum('bij,bjk->bik', leftward, root_right, precision=HIGHEST_PRECISION)
    new_master = master_blocks - MATRIX_RATE * (preconditioned + WEIGHT_DECAY * master_blocks)
    return (new_momentum, new_left, new_right, new_master)

def adam_step(vector_grad, vec_first, vec_second, vectors):
    new_first = FIRST_DECAY * vec_first + (1.0 - FIRST_DECAY) * vector_grad
    new_second = SECOND_DECAY * vec_second + (1.0 - SECOND_DECAY) * vector_grad * vector_grad
    corrected_first = new_first / (1.0 - FIRST_DECAY ** STEP)
    corrected_second = new_second / (1.0 - SECOND_DECAY ** STEP)
    new_vectors = vectors - VECTOR_RATE * corrected_first / (jnp.sqrt(corrected_second) + ADAM_EPSILON)
    return (new_first, new_second, new_vectors)

def forward(inputs, segment_labels, query_key_value, out_weight, up_weight, down_weight, vectors):
    first_gain, first_shift, second_gain, second_shift, query_bias, value_bias, out_bias, down_bias, up_bias = unpack(vectors)
    input_bias = jnp.concatenate([query_bias, jnp.zeros_like(query_bias), value_bias])
    projection_output = reduced_backward(reduced_precision(matmul(inputs, reduced_precision(query_key_value)) + input_bias))
    query_rows = projection_output[:, :MODEL_WIDTH].reshape(ROW_POSITIONS, HEAD_TOTAL, HEAD_SIZE)
    row_of_keys = projection_output[:, MODEL_WIDTH:2 * MODEL_WIDTH].reshape(ROW_POSITIONS, HEAD_TOTAL, HEAD_SIZE)
    row_of_values = projection_output[:, 2 * MODEL_WIDTH:].reshape(ROW_POSITIONS, HEAD_TOTAL, HEAD_SIZE)
    factor = HEAD_SIZE ** (-0.5)

    def attend(block_items):
        query_block, segment_block = block_items
        scores = reduced_backward(jnp.einsum('qhd,khd->hqk', query_block, row_of_keys, precision=HIGHEST_PRECISION) * factor)
        allowed = segment_block[:, None] == segment_labels[None, :]
        scores = jnp.where(allowed[None], scores, -1e+30)
        probabilities = jax.nn.softmax(scores, axis=-1)
        return jnp.einsum('hqk,khd->qhd', reduced_precision(probabilities), row_of_values, precision=HIGHEST_PRECISION)
    block_total = ROW_POSITIONS // QUERY_GROUP
    attended_output = lax.map(jax.checkpoint(attend), (query_rows.reshape(block_total, QUERY_GROUP, HEAD_TOTAL, HEAD_SIZE), segment_labels.reshape(block_total, QUERY_GROUP)))
    attended_output = reduced_backward(reduced_precision(attended_output.reshape(ROW_POSITIONS, MODEL_WIDTH)))
    branch = reduced_backward(matmul(attended_output, reduced_precision(out_weight)) + out_bias)
    normed = layer_norm(inputs + branch, first_gain, first_shift)
    before = reduced_backward(matmul(reduced_precision(normed), reduced_precision(up_weight)) + up_bias)
    activated = reduced_precision(jax.nn.gelu(before, approximate=False))
    feed_out = reduced_backward(matmul(activated, reduced_precision(down_weight)) + down_bias)
    return layer_norm(normed + feed_out, second_gain, second_shift)

def reference(tokens, cotangent, segment_ids, owner_order, master_blocks, momentum, stat_left, stat_right, root_left, root_right, vectors, vec_first, vec_second):
    natural = jnp.zeros_like(master_blocks).at[owner_order].set(master_blocks)
    matrices = split_blocks(natural)

    def per_row(totals, row_items):
        inputs, upstream, segment_labels = row_items

        def forward_row(inputs_row, query_key_value, out_weight, up_weight, down_weight, vector_row):
            return forward(inputs_row, segment_labels, query_key_value, out_weight, up_weight, down_weight, vector_row)
        result, backward = jax.vjp(forward_row, inputs, matrices[0], matrices[1], matrices[2], matrices[3], vectors)
        gradients = backward(upstream)
        totals = tuple((earlier + latest for earlier, latest in zip(totals, gradients[1:])))
        return (totals, (result.astype(jnp.bfloat16), gradients[0]))
    starting = tuple((jnp.zeros_like(matrix) for matrix in matrices)) + (jnp.zeros_like(vectors),)
    totals, (output, input_grad) = lax.scan(per_row, starting, (tokens.astype(jnp.float32), cotangent.astype(jnp.float32), segment_ids))
    grad_natural = jnp.concatenate([to_blocks(matrix) for matrix in totals[:4]])
    grad_blocks = grad_natural[owner_order]
    new_momentum, new_left, new_right, new_master = shampoo_step(grad_blocks, momentum, stat_left, stat_right, root_left, root_right, master_blocks)
    new_first, new_second, new_vectors = adam_step(totals[4], vec_first, vec_second, vectors)
    return (output, input_grad, new_momentum, new_left, new_right, new_master, new_first, new_second, new_vectors)
```

```python
import functools

import jax
import jax.numpy as jnp
import numpy as np
from jax import lax
from jax.experimental import pallas as pl
from jax.experimental.pallas import tpu as pltpu
from jax.sharding import PartitionSpec as P

MODEL_WIDTH = 768
HEAD_TOTAL = 12
HEAD_SIZE = 64
FF = 3072
ROW_POSITIONS = 1024
B = 192
STEP = 10
NBLK = 192
PAIRS = HEAD_TOTAL // 2
LANES = 128
REST = B * B // LANES
QUARTER = REST // 4
CHUNKS = FF // MODEL_WIDTH
MEBI = 2**20

NORM_EPSILON = 1e-05
STAT_DECAY = 0.5
MOMENTUM_DECAY = 0.5
MATRIX_RATE = 1.0
WEIGHT_DECAY = 0.01
FIRST_DECAY = 0.9
SECOND_DECAY = 0.999
VECTOR_RATE = 0.3
ADAM_EPSILON = 1e-08

F32 = jnp.float32
BF16 = jnp.bfloat16
STARTS = (0, 48, 64, 128, 192)


def panel_of_block():
    panels = []
    for block in range(NBLK):
        if block < STARTS[1]:
            panels.append((block % 12) // 4 * 4 + block // 12)
        elif block < STARTS[2]:
            panels.append(12 + (block - STARTS[1]) // 4)
        elif block < STARTS[3]:
            inner = block - STARTS[2]
            panels.append(16 + (inner % 16) // 4 * 4 + inner // 16)
        else:
            panels.append(32 + (block - STARTS[3]) // 4)
    return np.array(panels, np.int32)


def cost(flops, moved, transcendentals=0):
    return pl.CostEstimate(flops=flops, bytes_accessed=moved, transcendentals=transcendentals)


def dot(left, right, contract=((1,), (0,))):
    return lax.dot_general(left, right, (contract, ((), ())), preferred_element_type=F32)


def low_lanes(rows):
    return lax.broadcasted_iota(jnp.int32, (rows, LANES), 1) < LANES // 2


def pack_kernel(order_ref, blocks_ref, packed_ref):
    count = blocks_ref.shape[0]
    first = pl.program_id(0) * count
    half = low_lanes(B // 2)
    low = low_lanes(B)
    for slot in range(count):
        left = blocks_ref[slot, :, :LANES]
        narrow = blocks_ref[slot, :, LANES:]
        right = jnp.concatenate([narrow, narrow], axis=1)
        turned = pltpu.roll(left, LANES // 2, 1)
        odd = order_ref[first + slot] % 2 == 1
        main = jnp.where(odd, jnp.where(low, turned, right), left)
        even_rest = jnp.where(half, right[: B // 2], right[B // 2 :])
        odd_rest = jnp.where(half, left[B // 2 :], turned[: B // 2])
        packed_ref[slot, :B, :] = main.astype(BF16)
        packed_ref[slot, B:, :] = jnp.where(odd, odd_rest, even_rest).astype(BF16)


def pack_blocks(order, blocks):
    count = blocks.shape[0]
    group = max(size for size in range(1, 7) if count % size == 0)
    return pl.pallas_call(
        pack_kernel,
        grid_spec=pltpu.PrefetchScalarGridSpec(
            num_scalar_prefetch=1,
            grid=(count // group,),
            in_specs=[pl.BlockSpec((group, B, B), lambda i, *_: (i, 0, 0))],
            out_specs=pl.BlockSpec((group, REST, LANES), lambda i, *_: (i, 0, 0)),
        ),
        out_shape=jax.ShapeDtypeStruct((count, REST, LANES), BF16),
        cost_estimate=cost(0, count * B * B * 6),
        name="pack_weight_blocks",
    )(order, blocks)


def permute_xor(value, axis, mask):
    size = lax.axis_size(axis)
    return lax.ppermute(value, axis, [(i, i ^ mask) for i in range(size)])


def choose(cases, table, index):
    wanted = sorted(set(table))
    result = cases[wanted[0]]
    for case in wanted[1:]:
        match = functools.reduce(jnp.logical_or, [index == i for i, t in enumerate(table) if t == case])
        result = jnp.where(match, cases[case], result)
    return result


def gather_weights(packed, owner_order):
    heads = lax.axis_size("head")
    owners = lax.axis_size("seq")
    chips = owners // 2
    count = packed.shape[0]
    head = lax.axis_index("head")
    seq = lax.axis_index("seq")
    chip, core = seq // 2, seq % 2
    parts = heads if count % heads == 0 and heads == 4 else 1
    size = count // parts
    own = lax.dynamic_slice_in_dim(packed, head * size, size, 0) if parts > 1 else packed
    arrived = {}
    below = above = own
    for step in range(1, chips):
        below = lax.ppermute(below, "seq", [(s, s + 2) for s in range(owners - 2)])
        above = lax.ppermute(above, "seq", [(s + 2, s) for s in range(owners - 2)])
        arrived[-step], arrived[step] = below, above
    offsets = []
    for place in range(chips):
        reach = [d * s for s in range(1, chips) for d in (-1, 1)]
        offsets.append([r for r in reach if 0 <= place + r < chips])
    mine = [packed]
    sources = [chip]
    for slot in range(chips - 1):
        table = [offsets[place][slot] for place in range(chips)]
        sources.append(chip + jnp.array(table, jnp.int32)[chip])
        piece = choose(arrived, table, chip)
        if parts > 1:
            cut = size // 2
            first, second = piece[:cut], piece[cut:]
            first_x = permute_xor(first, "head", 1)
            second_y = permute_xor(second, "head", 2)
            first_y = permute_xor(first, "head", 2)
            second_x = permute_xor(second, "head", 1)
            first_xy = permute_xor(first_x, "head", 2)
            second_xy = permute_xor(second_y, "head", 1)
            piece = jnp.concatenate(
                [first, second, first_x, second_x, first_y, second_y, first_xy, second_xy]
            )
        mine.append(piece)
    other = [permute_xor(piece, "seq", 1) for piece in mine]
    place = jnp.arange(count, dtype=jnp.int32)
    mixed = place if parts == 1 else ((place // size) ^ head) * size + place % size
    numbers = []
    for which in (core, 1 - core):
        for slot, source in enumerate(sources):
            local_place = place if slot == 0 else mixed
            numbers.append(owner_order[(source * 2 + which) * count + local_place])
    return mine + other, jnp.concatenate(numbers)


def project_kernel(number_ref, panel_ref, pair_panel_ref, x_ref, vec_ref, *refs):
    sources = refs[:-6]
    projected_ref, sheet_out, sheet, rest, arrive, leave = refs[-6:]
    count = sources[0].shape[0]
    for which, source in enumerate(sources):

        def start(place, carry):
            number = number_ref[which * count + place]
            panel = panel_ref[which * count + place]
            group = (
                (number >= STARTS[1]).astype(jnp.int32)
                + (number >= STARTS[2]).astype(jnp.int32)
                + (number >= STARTS[3]).astype(jnp.int32)
            )
            row = pl.multiple_of(panel * B, B)
            lane = pl.multiple_of(((number // 2) % 2) * 384 + (number % 2) * 256, LANES)
            pltpu.make_async_copy(
                source.at[place, pl.ds(0, B), :],
                sheet.at[pl.ds(row, B), pl.ds(lane, LANES)],
                arrive.at[group],
            ).start()
            pltpu.make_async_copy(
                source.at[place, pl.ds(B, B // 2), :], rest.at[number], arrive.at[group]
            ).start()
            return carry

        lax.fori_loop(0, count, start, 0)
    half = low_lanes(B // 2)

    def merge(pair, carry):
        even, odd = rest[2 * pair].astype(F32), rest[2 * pair + 1].astype(F32)
        row = pl.multiple_of(pair_panel_ref[pair] * B, B)
        lane = pl.multiple_of((pair % 2) * 384 + LANES, LANES)
        turned = pltpu.roll(jnp.where(half, odd, even), LANES // 2, 1)
        sheet[pl.ds(row, B // 2), pl.ds(lane, LANES)] = jnp.where(half, even, odd).astype(BF16)
        sheet[pl.ds(row + B // 2, B // 2), pl.ds(lane, LANES)] = turned.astype(BF16)
        return carry

    copies = []
    for group in range(4):
        rows = pl.ds(STARTS[group] * 48, (STARTS[group + 1] - STARTS[group]) * 48)
        part = sheet.at[rows, :]
        pltpu.make_async_copy(part, part, arrive.at[group]).wait()
        lax.fori_loop(STARTS[group] // 2, STARTS[group + 1] // 2, merge, 0)
        copies.append(pltpu.make_async_copy(part, sheet_out.at[rows, :], leave.at[group]))
        copies[-1].start()
    for panel in range(3):
        weight = sheet[panel * MODEL_WIDTH : (panel + 1) * MODEL_WIDTH, :]
        for tile in range(x_ref.shape[0] // 256):
            rows = slice(tile * 256, (tile + 1) * 256)
            value = dot(x_ref[rows, :], weight)
            if panel != 1:
                value = value + vec_ref[4 + panel // 2 : 5 + panel // 2, :]
            projected_ref[rows, panel * MODEL_WIDTH : (panel + 1) * MODEL_WIDTH] = value.astype(BF16)
    for copy in copies:
        copy.wait()


def project(x, vectors, sources, numbers):
    panels = panel_of_block()
    rows = x.shape[0]
    whole = lambda shape: pl.BlockSpec(shape, lambda i, *_: (0,) * len(shape))
    anywhere = pl.BlockSpec(memory_space=pl.ANY)
    return pl.pallas_call(
        project_kernel,
        grid_spec=pltpu.PrefetchScalarGridSpec(
            num_scalar_prefetch=3,
            grid=(1,),
            in_specs=[whole(x.shape), whole(vectors.shape)] + [anywhere] * len(sources),
            out_specs=[whole((rows, 3 * MODEL_WIDTH)), anywhere],
            scratch_shapes=[
                pltpu.VMEM((NBLK * 48, MODEL_WIDTH), BF16),
                pltpu.VMEM((NBLK, B // 2, LANES), BF16),
                pltpu.SemaphoreType.DMA((4,)),
                pltpu.SemaphoreType.DMA((4,)),
            ],
        ),
        out_shape=[
            jax.ShapeDtypeStruct((rows, 3 * MODEL_WIDTH), BF16),
            jax.ShapeDtypeStruct((NBLK * 48, MODEL_WIDTH), BF16),
        ],
        compiler_params=pltpu.CompilerParams(vmem_limit_bytes=48 * MEBI),
        cost_estimate=cost(6 * rows * MODEL_WIDTH**2, 2 * NBLK * B * B * 2 + rows * MODEL_WIDTH * 8),
        name="project_and_lay_out_weights",
    )(numbers, jnp.array(panels)[numbers], jnp.array(panels[::2]), x, vectors, *sources)


KEY_TILE = 256


def key_tiles(labels, tile):
    edges = labels.reshape(-1, tile)
    first, last = edges[:, 0], edges[:, -1]
    start = jnp.sum(labels[None, :] < first[:, None], axis=1, dtype=jnp.int32) // KEY_TILE
    end = jnp.sum(labels[None, :] <= last[:, None], axis=1, dtype=jnp.int32)
    return start, (end + KEY_TILE - 1) // KEY_TILE - start


def over_tiles(tile, start_ref, count_ref, run):
    def block(index, carry):
        rows = pl.ds(pl.multiple_of(index * tile, tile), tile)
        start = pl.multiple_of(start_ref[index] * KEY_TILE, KEY_TILE)
        for count in range(1, ROW_POSITIONS // KEY_TILE + 1):
            keys = pl.ds(start, count * KEY_TILE)
            pl.when(count_ref[index] == count)(functools.partial(run, rows, keys))
        return carry

    lax.fori_loop(0, ROW_POSITIONS // tile, block, 0)


def attention_forward_kernel(
    tile, start_ref, count_ref, row_ref, column_ref, q_ref, k_ref, v_ref, out_ref, log_ref, vt_ref
):
    groups = q_ref.shape[1] // LANES
    vt_ref[...] = v_ref[...].T
    low = low_lanes(tile)

    def run(rows, keys):
        same = column_ref[keys, :] == row_ref[:, rows]
        for group in range(groups):
            lanes = slice(group * LANES, (group + 1) * LANES)
            queries = q_ref[rows, lanes] * jnp.bfloat16(HEAD_SIZE**-0.5)
            mixed = []
            for part in range(2):
                chosen = jnp.where(low if part == 0 else ~low, queries, jnp.zeros_like(queries))
                scores = dot(k_ref[keys, lanes], chosen, ((1,), (1,)))
                scores = jnp.where(same, scores, -1e30)
                peak = jnp.max(scores, axis=0, keepdims=True)
                exponents = jnp.exp(scores - peak)
                total = jnp.sum(exponents, axis=0, keepdims=True)
                probabilities = (exponents * (1.0 / total)).astype(BF16)
                first = group * LANES + part * HEAD_SIZE
                mixed.append(dot(vt_ref[first : first + HEAD_SIZE, keys], probabilities))
                log_ref[group, part : part + 1, rows] = peak + jnp.log(total)
            out_ref[rows, lanes] = jnp.concatenate(mixed, axis=0).T.astype(BF16)

    over_tiles(tile, start_ref, count_ref, run)


def attention_forward(projected, labels, tile=512, groups=2):
    start, count = key_tiles(labels, tile)
    width = groups * LANES
    steps = PAIRS // groups
    rows = ROW_POSITIONS
    return pl.pallas_call(
        functools.partial(attention_forward_kernel, tile),
        grid_spec=pltpu.PrefetchScalarGridSpec(
            num_scalar_prefetch=2,
            grid=(steps,),
            in_specs=[
                pl.BlockSpec((1, rows), lambda h, *_: (0, 0)),
                pl.BlockSpec((rows, 1), lambda h, *_: (0, 0)),
                pl.BlockSpec((rows, width), lambda h, *_: (0, h)),
                pl.BlockSpec((rows, width), lambda h, *_: (0, steps + h)),
                pl.BlockSpec((rows, width), lambda h, *_: (0, 2 * steps + h)),
            ],
            out_specs=[
                pl.BlockSpec((rows, width), lambda h, *_: (0, h)),
                pl.BlockSpec((groups, 8, rows), lambda h, *_: (h, 0, 0)),
            ],
            scratch_shapes=[pltpu.VMEM((width, rows), BF16)],
        ),
        out_shape=[
            jax.ShapeDtypeStruct((rows, MODEL_WIDTH), BF16),
            jax.ShapeDtypeStruct((PAIRS, 8, rows), F32),
        ],
        compiler_params=pltpu.CompilerParams(vmem_limit_bytes=48 * MEBI),
        cost_estimate=cost(16 * 10**9, 8 * rows * MODEL_WIDTH),
        name="attention_forward",
    )(start, count, labels.reshape(1, rows), labels.reshape(rows, 1), projected, projected, projected)


def attention_backward_kernel(
    tile,
    start_ref,
    count_ref,
    row_ref,
    column_ref,
    q_ref,
    k_ref,
    v_ref,
    d_ref,
    log_ref,
    out_ref,
    sum_ref,
    kt_ref,
    dk_ref,
    dv_ref,
):
    groups = q_ref.shape[1] // LANES
    factor = HEAD_SIZE**-0.5
    kt_ref[...] = k_ref[...].T
    dk_ref[...] = jnp.zeros_like(dk_ref)
    dv_ref[...] = jnp.zeros_like(dv_ref)
    low = low_lanes(tile)

    def run(rows, keys):
        same = column_ref[keys, :] == row_ref[:, rows]
        for group in range(groups):
            lanes = slice(group * LANES, (group + 1) * LANES)
            queries = q_ref[rows, lanes] * jnp.bfloat16(factor)
            upstream = d_ref[rows, lanes]
            d_queries = []
            d_keys = d_values = 0.0
            for part in range(2):
                mask = low if part == 0 else ~low
                chosen = jnp.where(mask, queries, jnp.zeros_like(queries))
                d_chosen = jnp.where(mask, upstream, jnp.zeros_like(upstream))
                scores = dot(k_ref[keys, lanes], chosen, ((1,), (1,)))
                exponents = jnp.exp(scores - log_ref[group, part : part + 1, rows])
                probabilities = jnp.where(same, exponents, 0.0)
                d_probs = dot(v_ref[keys, lanes], d_chosen, ((1,), (1,)))
                inner = jnp.sum(probabilities * d_probs, axis=0, keepdims=True)
                d_scores = (probabilities * (d_probs - inner)).astype(BF16)
                d_values += dot(probabilities.astype(BF16), d_chosen)
                d_keys += dot(d_scores, chosen)
                first = group * LANES + part * HEAD_SIZE
                d_queries.append(dot(kt_ref[first : first + HEAD_SIZE, keys], d_scores))
            dk_ref[keys, lanes] += d_keys
            dv_ref[keys, lanes] += d_values
            out_ref[0, rows, lanes] = (jnp.concatenate(d_queries, axis=0).T * factor).astype(BF16)

    over_tiles(tile, start_ref, count_ref, run)
    out_ref[1] = dk_ref[...].astype(BF16)
    out_ref[2] = dv_ref[...].astype(BF16)
    sum_ref[0:1, :] = jnp.sum(out_ref[0].astype(F32), axis=0, keepdims=True)
    sum_ref[1:2, :] = jnp.sum(out_ref[2].astype(F32), axis=0, keepdims=True)


def attention_backward(projected, labels, d_attended, logs, tile=256, groups=2):
    start, count = key_tiles(labels, tile)
    width = groups * LANES
    steps = PAIRS // groups
    rows = ROW_POSITIONS
    return pl.pallas_call(
        functools.partial(attention_backward_kernel, tile),
        grid_spec=pltpu.PrefetchScalarGridSpec(
            num_scalar_prefetch=2,
            grid=(steps,),
            in_specs=[
                pl.BlockSpec((1, rows), lambda h, *_: (0, 0)),
                pl.BlockSpec((rows, 1), lambda h, *_: (0, 0)),
                pl.BlockSpec((rows, width), lambda h, *_: (0, h)),
                pl.BlockSpec((rows, width), lambda h, *_: (0, steps + h)),
                pl.BlockSpec((rows, width), lambda h, *_: (0, 2 * steps + h)),
                pl.BlockSpec((rows, width), lambda h, *_: (0, h)),
                pl.BlockSpec((groups, 8, rows), lambda h, *_: (h, 0, 0)),
            ],
            out_specs=[
                pl.BlockSpec((3, rows, width), lambda h, *_: (0, 0, h)),
                pl.BlockSpec((8, width), lambda h, *_: (0, h)),
            ],
            scratch_shapes=[
                pltpu.VMEM((width, rows), BF16),
                pltpu.VMEM((rows, width), F32),
                pltpu.VMEM((rows, width), F32),
            ],
        ),
        out_shape=[
            jax.ShapeDtypeStruct((3, rows, MODEL_WIDTH), BF16),
            jax.ShapeDtypeStruct((8, MODEL_WIDTH), F32),
        ],
        compiler_params=pltpu.CompilerParams(vmem_limit_bytes=48 * MEBI),
        cost_estimate=cost(32 * 10**9, 16 * rows * MODEL_WIDTH),
        name="attention_backward",
    )(
        start,
        count,
        labels.reshape(1, rows),
        labels.reshape(rows, 1),
        projected,
        projected,
        projected,
        d_attended,
        logs,
    )


def mean(value):
    return jnp.sum(value, axis=1, keepdims=True) * (1.0 / MODEL_WIDTH)


def middle_kernel(
    attended_ref,
    x_ref,
    upstream_ref,
    vec_ref,
    out_weight,
    up_weight,
    down_weight,
    output_ref,
    normed_ref,
    activated_ref,
    d_before_ref,
    d_feed_ref,
    d_first_ref,
    d_branch_ref,
    d_attended_ref,
    sums_ref,
    slope_ref,
):
    width = MODEL_WIDTH

    @pl.when(pl.program_id(0) == 0)
    def _():
        sums_ref[...] = jnp.zeros_like(sums_ref)

    def add_up(row, value):
        sums_ref[row : row + 1, :] += jnp.sum(value, axis=0, keepdims=True)

    def vector(row):
        return vec_ref[row : row + 1, :]

    hidden = x_ref[...].astype(F32) + (dot(attended_ref[...], out_weight[...]) + vector(6))
    center = hidden - mean(hidden)
    first_scale = lax.rsqrt(mean(center * center) + NORM_EPSILON)
    first_normal = center * first_scale
    normed = first_normal * vector(0) + vector(1)
    normed_low = normed.astype(BF16)
    normed_ref[...] = normed_low
    feed_out = vector(7)
    for chunk in range(CHUNKS):
        part = slice(chunk * width, (chunk + 1) * width)
        before = dot(normed_low, up_weight[part, :]) + vector(8 + chunk)
        share = 0.5 + 0.5 * lax.erf(before * np.float32(np.sqrt(0.5)))
        density = jnp.exp(before * before * -0.5) * np.float32(1.0 / np.sqrt(2.0 * np.pi))
        slope_ref[:, part] = share + before * density
        activated = (before * share).astype(BF16)
        activated_ref[:, part] = activated
        feed_out = feed_out + dot(activated, down_weight[part, :])
    mixed = normed + feed_out
    center = mixed - mean(mixed)
    second_scale = lax.rsqrt(mean(center * center) + NORM_EPSILON)
    second_normal = center * second_scale
    output_ref[...] = (second_normal * vector(2) + vector(3)).astype(BF16)
    upstream = upstream_ref[...].astype(F32)
    add_up(2, upstream * second_normal)
    add_up(3, upstream)
    scaled = upstream * vector(2)
    d_mixed = second_scale * (scaled - mean(scaled) - second_normal * mean(scaled * second_normal))
    d_feed = d_mixed.astype(BF16)
    d_feed_ref[...] = d_feed
    add_up(7, d_feed.astype(F32))
    d_normed = d_mixed
    for chunk in range(CHUNKS):
        part = slice(chunk * width, (chunk + 1) * width)
        d_active = dot(d_feed, down_weight[part, :], ((1,), (1,)))
        d_before = (d_active * slope_ref[:, part]).astype(BF16)
        d_before_ref[:, part] = d_before
        add_up(8 + chunk, d_before.astype(F32))
        d_normed = d_normed + dot(d_before, up_weight[part, :], ((1,), (1,)))
    add_up(0, d_normed * first_normal)
    add_up(1, d_normed)
    scaled = d_normed * vector(0)
    d_first = first_scale * (scaled - mean(scaled) - first_normal * mean(scaled * first_normal))
    d_first_ref[...] = d_first
    d_branch = d_first.astype(BF16)
    d_branch_ref[...] = d_branch
    add_up(6, d_branch.astype(F32))
    d_attended_ref[...] = dot(d_branch, out_weight[...], ((1,), (1,))).astype(BF16)


def middle(attended, x, upstream, vectors, sheet, tile=256):
    rows = x.shape[0]
    width = MODEL_WIDTH
    by_tile = lambda columns: pl.BlockSpec((tile, columns), lambda i: (i, 0))
    held = lambda count, place: pl.BlockSpec(
        (count, width), lambda i: (place, 0), pipeline_mode=pl.Buffered(1)
    )
    low = lambda columns: jax.ShapeDtypeStruct((rows, columns), BF16)
    return pl.pallas_call(
        middle_kernel,
        grid=(rows // tile,),
        in_specs=[
            by_tile(width),
            by_tile(width),
            by_tile(width),
            pl.BlockSpec((12, width), lambda i: (0, 0)),
            held(width, 3),
            held(FF, 1),
            held(FF, 2),
        ],
        out_specs=[
            by_tile(width),
            by_tile(width),
            by_tile(FF),
            by_tile(FF),
            by_tile(width),
            by_tile(width),
            by_tile(width),
            by_tile(width),
            pl.BlockSpec((12, width), lambda i: (0, 0)),
        ],
        out_shape=[
            low(width),
            low(width),
            low(FF),
            low(FF),
            low(width),
            jax.ShapeDtypeStruct((rows, width), F32),
            low(width),
            low(width),
            jax.ShapeDtypeStruct((12, width), F32),
        ],
        scratch_shapes=[pltpu.VMEM((tile, FF), F32)],
        compiler_params=pltpu.CompilerParams(vmem_limit_bytes=56 * MEBI),
        cost_estimate=cost(rows * width * (FF * 8 + width * 4), rows * width * 40),
        name="layer_middle",
    )(attended, x, upstream, vectors, sheet, sheet, sheet)


def fold_blocks(value, even_ref, odd_ref, place):
    half = low_lanes(B // 2)
    center = value[:, LANES : 2 * LANES]
    top, bottom = center[: B // 2], pltpu.roll(center[B // 2 :], LANES // 2, 1)
    turned = pltpu.roll(top, LANES // 2, 1)
    even_rest = jnp.where(half, top, bottom)
    odd_rest = jnp.where(half, bottom, top)
    del turned
    for quarter in range(4):
        main = slice(quarter * 48, (quarter + 1) * 48)
        rest = slice(quarter * 24, (quarter + 1) * 24)
        even_ref[place + (quarter, slice(0, 48))] = value[main, :LANES].astype(BF16)
        even_ref[place + (quarter, slice(48, 72))] = even_rest[rest].astype(BF16)
        odd_ref[place + (quarter, slice(0, 48))] = value[main, 2 * LANES :].astype(BF16)
        odd_ref[place + (quarter, slice(48, 72))] = odd_rest[rest].astype(BF16)


def weight_gradient_kernel(left_ref, right_ref, even_ref, odd_ref):
    value = dot(left_ref[...], right_ref[...], ((0,), (0,)))
    for row in range(value.shape[0] // B):
        for pair in range(value.shape[1] // 384):
            fold_blocks(
                value[row * B : (row + 1) * B, pair * 384 : (pair + 1) * 384],
                even_ref,
                odd_ref,
                (row, pair),
            )


def weight_gradient(left, right, left_step, right_step):
    rows, height = left.shape
    width = right.shape[1]
    grid = (height // left_step, width // right_step)
    shape = jax.ShapeDtypeStruct((height // B, width // 384, 4, QUARTER, LANES), BF16)
    spec = pl.BlockSpec((left_step // B, right_step // 384, 4, QUARTER, LANES), lambda i, j: (i, j, 0, 0, 0))
    even, odd = pl.pallas_call(
        weight_gradient_kernel,
        grid=grid,
        in_specs=[
            pl.BlockSpec((rows, left_step), lambda i, j: (0, i)),
            pl.BlockSpec((rows, right_step), lambda i, j: (0, j)),
        ],
        out_specs=[spec, spec],
        out_shape=[shape, shape],
        compiler_params=pltpu.CompilerParams(vmem_limit_bytes=48 * MEBI),
        cost_estimate=cost(2 * rows * height * width, 2 * (height * width + rows * (height + width))),
        name="weight_gradient",
    )(left, right)
    flat = (height // B * (width // 384), 4, QUARTER, LANES)
    return even.reshape(flat), odd.reshape(flat)


def add_parts(*parts):
    return functools.reduce(jnp.add, [part.astype(F32) for part in parts]).astype(BF16)


def reduce_gradient(even, odd):
    owners = lax.axis_size("seq")
    chips = owners // 2
    head = lax.axis_index("head")
    seq = lax.axis_index("seq")
    chip, core = seq // 2, seq % 2
    from_odd = lax.ppermute(even, "seq", [(s + 1, s) for s in range(0, owners, 2)])
    from_even = lax.ppermute(odd, "seq", [(s, s + 1) for s in range(0, owners, 2)])
    kept = jnp.where(core == 0, add_parts(even, from_odd), add_parts(odd, from_even))
    take = lambda index: lax.dynamic_index_in_dim(kept, index, 1, keepdims=False)
    quarter = add_parts(
        take(head), *[permute_xor(take(head ^ mask), "head", mask) for mask in (1, 2, 3)]
    )
    pairs = quarter.shape[0]
    each = -(-pairs // chips)
    quarter = jnp.pad(quarter, ((0, each * chips - pairs), (0, 0), (0, 0)))
    quarter = quarter.reshape(chips, each, QUARTER, LANES)
    take = lambda index: lax.dynamic_index_in_dim(quarter, index, 0, keepdims=False)
    share = add_parts(
        take(chip), *[permute_xor(take(chip ^ mask), "seq", 2 * mask) for mask in range(1, chips)]
    )
    whole = jnp.concatenate(
        [share] + [permute_xor(share, "seq", 2 * mask) for mask in range(1, chips)]
    )
    return whole, permute_xor(whole, "seq", 1)


def pick_kernel(count, place_ref, which_ref, *refs):
    sources, out_ref, semaphore = refs[:-2], refs[-2], refs[-1]

    def start(slot, carry):
        for index, source in enumerate(sources):

            @pl.when(which_ref[slot] == index)
            def _():
                pltpu.make_async_copy(
                    source.at[place_ref[slot]], out_ref.at[slot], semaphore
                ).start()

        return carry

    lax.fori_loop(0, count, start, 0)
    pltpu.make_async_copy(out_ref, out_ref, semaphore).wait()


def pick_blocks(numbers, gathered):
    chips = lax.axis_size("seq") // 2
    seq = lax.axis_index("seq")
    chip, core = seq // 2, seq % 2
    which = jnp.zeros_like(numbers)
    place = jnp.zeros_like(numbers)
    sources = []
    for first, last, (mine, other) in gathered:
        inside = (numbers >= first) & (numbers < last)
        pair = (numbers - first) // 2
        each = mine.shape[0] // chips
        spot = ((pair // each) ^ chip) * each + pair % each
        place = jnp.where(inside, spot, place)
        which = jnp.where(inside, len(sources) + ((numbers % 2) ^ core), which)
        sources += [mine, other]
    count = numbers.shape[0]
    return pl.pallas_call(
        functools.partial(pick_kernel, count),
        grid_spec=pltpu.PrefetchScalarGridSpec(
            num_scalar_prefetch=2,
            grid=(1,),
            in_specs=[pl.BlockSpec(memory_space=pl.ANY)] * len(sources),
            out_specs=pl.BlockSpec(memory_space=pl.ANY),
            scratch_shapes=[pltpu.SemaphoreType.DMA],
        ),
        out_shape=jax.ShapeDtypeStruct((count, QUARTER, LANES), BF16),
        cost_estimate=cost(0, count * QUARTER * LANES * 4),
        name="pick_owned_blocks",
    )(place, which, *sources)


def shampoo_kernel(
    number_ref,
    quarter_ref,
    part0,
    part1,
    part2,
    part3,
    momentum_ref,
    left_ref,
    right_ref,
    root_left_ref,
    root_right_ref,
    master_ref,
    new_momentum_ref,
    new_left_ref,
    new_right_ref,
    new_master_ref,
    main_ref,
    rest_ref,
):
    count = momentum_ref.shape[0]
    first = pl.program_id(0) * count
    half = low_lanes(B // 2)
    low = low_lanes(B)
    for slot in range(count):
        for index, part in enumerate((part0, part1, part2, part3)):
            quarter = quarter_ref[index]
            value = part[slot].astype(F32)
            main_ref[pl.ds(pl.multiple_of(quarter * 48, 8), 48), :] = value[:48]
            rest_ref[pl.ds(pl.multiple_of(quarter * 24, 8), 24), :] = value[48:]
        main = main_ref[...]
        rest = rest_ref[...]
        turned = pltpu.roll(rest, LANES // 2, 1)
        odd = number_ref[first + slot] % 2 == 1
        upper = jnp.where(odd, jnp.where(half, turned, rest), jnp.where(half, rest, turned))
        lower = jnp.where(odd, jnp.where(half, rest, turned), jnp.where(half, turned, rest))
        folded = jnp.concatenate([upper, lower], axis=0)
        spun = pltpu.roll(main, LANES // 2, 1)
        left_lanes = jnp.where(odd, jnp.where(low, folded, spun), main)
        right_lanes = jnp.where(odd, spun, folded)
        gradient = jnp.concatenate([left_lanes, right_lanes[:, : LANES // 2]], axis=1)
        new_momentum = MOMENTUM_DECAY * momentum_ref[slot] + (1.0 - MOMENTUM_DECAY) * gradient
        new_momentum_ref[slot] = new_momentum
        grad_low = gradient.astype(BF16)
        new_left_ref[slot] = STAT_DECAY * left_ref[slot] + (1.0 - STAT_DECAY) * dot(
            grad_low, grad_low, ((1,), (1,))
        )
        new_right_ref[slot] = STAT_DECAY * right_ref[slot] + (1.0 - STAT_DECAY) * dot(
            grad_low, grad_low, ((0,), (0,))
        )
        leftward = dot(root_left_ref[slot].astype(BF16), new_momentum.astype(BF16))
        preconditioned = dot(leftward.astype(BF16), root_right_ref[slot].astype(BF16))
        master = master_ref[slot]
        new_master_ref[slot] = master - MATRIX_RATE * (preconditioned + WEIGHT_DECAY * master)


def shampoo(numbers, parts, states):
    count = numbers.shape[0]
    group = max(size for size in range(1, 4) if count % size == 0)
    spec = pl.BlockSpec((group, B, B), lambda i, *_: (i, 0, 0))
    part_spec = pl.BlockSpec((group, QUARTER, LANES), lambda i, *_: (i, 0, 0))
    quarters = lax.axis_index("head") ^ jnp.arange(4, dtype=jnp.int32)
    return pl.pallas_call(
        shampoo_kernel,
        grid_spec=pltpu.PrefetchScalarGridSpec(
            num_scalar_prefetch=2,
            grid=(count // group,),
            in_specs=[part_spec] * 4 + [spec] * 6,
            out_specs=[spec] * 4,
            scratch_shapes=[pltpu.VMEM((B, LANES), F32), pltpu.VMEM((B // 2, LANES), F32)],
        ),
        out_shape=[jax.ShapeDtypeStruct((count, B, B), F32)] * 4,
        compiler_params=pltpu.CompilerParams(vmem_limit_bytes=48 * MEBI),
        cost_estimate=cost(8 * count * B**3, 10 * count * B * B * 4),
        name="shampoo_blocks",
    )(numbers, quarters, *parts, *states)


def sum_everywhere(value):
    for axis in ("head", "seq"):
        mask = 1
        while mask < lax.axis_size(axis):
            value = value + permute_xor(value, axis, mask)
            mask *= 2
    return value


def adam_step(vector_grad, vec_first, vec_second, vectors):
    new_first = FIRST_DECAY * vec_first + (1.0 - FIRST_DECAY) * vector_grad
    new_second = SECOND_DECAY * vec_second + (1.0 - SECOND_DECAY) * vector_grad * vector_grad
    corrected_first = new_first / (1.0 - FIRST_DECAY**STEP)
    corrected_second = new_second / (1.0 - SECOND_DECAY**STEP)
    new_vectors = vectors - VECTOR_RATE * corrected_first / (
        jnp.sqrt(corrected_second) + ADAM_EPSILON
    )
    return (new_first, new_second, new_vectors)


def to_rows(value):
    return lax.all_to_all(value, "head", split_axis=0, concat_axis=1, tiled=True)


def to_positions(value):
    return lax.all_to_all(value, "head", split_axis=1, concat_axis=0, tiled=True)


def local(
    tokens,
    cotangent,
    segment_ids,
    owner_order,
    master_blocks,
    momentum,
    stat_left,
    stat_right,
    root_left,
    root_right,
    vectors,
    vec_first,
    vec_second,
):
    width = MODEL_WIDTH
    count = master_blocks.shape[0]
    head = lax.axis_index("head")
    numbers = lax.dynamic_slice_in_dim(owner_order, lax.axis_index("seq") * count, count, 0)
    sheet_vectors = vectors.reshape(12, width)

    packed = pack_blocks(numbers, master_blocks)
    sources, source_numbers = gather_weights(packed, owner_order)
    row_tokens = to_rows(tokens)
    own_rows = row_tokens.shape[0]
    x = row_tokens.reshape(own_rows * ROW_POSITIONS, width)
    upstream = to_rows(cotangent).reshape(x.shape)
    labels = lax.dynamic_slice_in_dim(segment_ids, head * own_rows, own_rows, 0)

    projected, sheet = project(x, sheet_vectors, sources, source_numbers)
    by_row = lambda value, row: value[row * ROW_POSITIONS : (row + 1) * ROW_POSITIONS]
    forward = [attention_forward(by_row(projected, r), labels[r]) for r in range(own_rows)]
    attended = jnp.concatenate([f[0] for f in forward])
    (
        output,
        normed_low,
        activated,
        d_before,
        d_feed,
        d_first,
        d_branch,
        d_attended,
        sums,
    ) = middle(attended, x, upstream, sheet_vectors, sheet)
    output = to_positions(output.reshape(row_tokens.shape))
    down_parts = reduce_gradient(*weight_gradient(activated, d_feed, 384, width))
    up_parts = reduce_gradient(*weight_gradient(normed_low, d_before, width, width))
    out_parts = reduce_gradient(*weight_gradient(attended, d_branch, width, width))
    backward = [
        attention_backward(by_row(projected, r), labels[r], by_row(d_attended, r), forward[r][1])
        for r in range(own_rows)
    ]
    d_projected = jnp.concatenate([b[0] for b in backward], axis=1)
    d_wide = jnp.concatenate([d_projected[part] for part in range(3)], axis=1)
    qkv_parts = reduce_gradient(*weight_gradient(x, d_wide, width, width))
    input_grad = d_first
    for part in range(3):
        input_grad = input_grad + dot(
            d_projected[part], sheet[part * width : (part + 1) * width], ((1,), (1,))
        )
    input_grad = to_positions(input_grad.astype(BF16).reshape(row_tokens.shape)).astype(F32)

    bias_sums = functools.reduce(jnp.add, [b[1] for b in backward])
    sums = sum_everywhere(sums)
    bias_sums = sum_everywhere(bias_sums[:2])
    vector_grad = jnp.concatenate([sums[:4], bias_sums, sums[6:]]).reshape(-1)
    new_first, new_second, new_vectors = adam_step(vector_grad, vec_first, vec_second, vectors)

    picked = pick_blocks(
        numbers,
        [
            (STARTS[0], STARTS[1], qkv_parts),
            (STARTS[1], STARTS[2], out_parts),
            (STARTS[2], STARTS[3], up_parts),
            (STARTS[3], STARTS[4], down_parts),
        ],
    )
    parts = [picked] + [permute_xor(picked, "head", mask) for mask in (1, 2, 3)]
    states = (momentum, stat_left, stat_right, root_left, root_right, master_blocks)
    new_momentum, new_left, new_right, new_master = shampoo(numbers, parts, states)
    return (
        output,
        input_grad,
        new_momentum,
        new_left,
        new_right,
        new_master,
        new_first,
        new_second,
        new_vectors,
    )


def solution(mesh):
    blocks = P("seq", None, None)
    positions = P("seq", "head", None)
    return jax.shard_map(
        local,
        mesh=mesh,
        in_specs=(positions, positions, P("seq", None), P()) + (blocks,) * 6 + (P(),) * 3,
        out_specs=(positions, positions) + (blocks,) * 4 + (P(),) * 3,
        check_vma=False,
    )
```

```python
import functools

import jax
import jax.numpy as jnp
import numpy as np
from jax import lax
from jax.experimental import pallas as pl
from jax.experimental.pallas import tpu as pltpu
from jax.sharding import PartitionSpec as P

MODEL_WIDTH = 768
HEAD_TOTAL = 12
HEAD_SIZE = 64
FF = 3072
ROW_POSITIONS = 1024
B = 192
STEP = 10
NBLK = 192
PAIRS = HEAD_TOTAL // 2
LANES = 128
REST = B * B // LANES
QUARTER = REST // 4
CHUNKS = FF // MODEL_WIDTH
MEBI = 2**20

NORM_EPSILON = 1e-05
STAT_DECAY = 0.5
MOMENTUM_DECAY = 0.5
MATRIX_RATE = 1.0
WEIGHT_DECAY = 0.01
FIRST_DECAY = 0.9
SECOND_DECAY = 0.999
VECTOR_RATE = 0.3
ADAM_EPSILON = 1e-08

F32 = jnp.float32
BF16 = jnp.bfloat16
STARTS = (0, 48, 64, 128, 192)


def panel_of_block():
    panels = []
    for block in range(NBLK):
        if block < STARTS[1]:
            panels.append((block % 12) // 4 * 4 + block // 12)
        elif block < STARTS[2]:
            panels.append(12 + (block - STARTS[1]) // 4)
        elif block < STARTS[3]:
            inner = block - STARTS[2]
            panels.append(16 + (inner % 16) // 4 * 4 + inner // 16)
        else:
            panels.append(32 + (block - STARTS[3]) // 4)
    return np.array(panels, np.int32)


def cost(flops, moved, transcendentals=0):
    return pl.CostEstimate(flops=flops, bytes_accessed=moved, transcendentals=transcendentals)


def dot(left, right, contract=((1,), (0,))):
    return lax.dot_general(left, right, (contract, ((), ())), preferred_element_type=F32)


def low_lanes(rows):
    return lax.broadcasted_iota(jnp.int32, (rows, LANES), 1) < LANES // 2


def pack_kernel(order_ref, blocks_ref, packed_ref):
    count = blocks_ref.shape[0]
    first = pl.program_id(0) * count
    half = low_lanes(B // 2)
    low = low_lanes(B)
    for slot in range(count):
        left = blocks_ref[slot, :, :LANES]
        narrow = blocks_ref[slot, :, LANES:]
        right = jnp.concatenate([narrow, narrow], axis=1)
        turned = pltpu.roll(left, LANES // 2, 1)
        odd = order_ref[first + slot] % 2 == 1
        main = jnp.where(odd, jnp.where(low, turned, right), left)
        even_rest = jnp.where(half, right[: B // 2], right[B // 2 :])
        odd_rest = jnp.where(half, left[B // 2 :], turned[: B // 2])
        packed_ref[slot, :B, :] = main.astype(BF16)
        packed_ref[slot, B:, :] = jnp.where(odd, odd_rest, even_rest).astype(BF16)


def pack_blocks(order, blocks):
    count = blocks.shape[0]
    group = max(size for size in range(1, 7) if count % size == 0)
    return pl.pallas_call(
        pack_kernel,
        grid_spec=pltpu.PrefetchScalarGridSpec(
            num_scalar_prefetch=1,
            grid=(count // group,),
            in_specs=[pl.BlockSpec((group, B, B), lambda i, *_: (i, 0, 0))],
            out_specs=pl.BlockSpec((group, REST, LANES), lambda i, *_: (i, 0, 0)),
        ),
        out_shape=jax.ShapeDtypeStruct((count, REST, LANES), BF16),
        cost_estimate=cost(0, count * B * B * 6),
        name="pack_weight_blocks",
    )(order, blocks)


def permute_xor(value, axis, mask):
    size = lax.axis_size(axis)
    return lax.ppermute(value, axis, [(i, i ^ mask) for i in range(size)])


def after(value, *others):
    return lax.optimization_barrier((value,) + others)[0]


def gather_weights(packed, owner_order):
    heads = lax.axis_size("head")
    chips = lax.axis_size("seq") // 2
    count = packed.shape[0]
    head = lax.axis_index("head")
    seq = lax.axis_index("seq")
    chip, core = seq // 2, seq % 2
    place = jnp.arange(count, dtype=jnp.int32)
    if count % (2 * heads) or chips != 4:
        return [lax.all_gather(packed, "seq", axis=0, tiled=True)], owner_order
    size = count // heads
    cut = size // 2
    own = lax.dynamic_slice_in_dim(packed, head * size, size, 0)
    halves = own[:cut], own[cut:]
    over_z = lambda half, mask: permute_xor(half, "seq", 2 * mask)
    near = [over_z(half, 1) for half in halves]
    middle_halves = [over_z(halves[0], 2), over_z(halves[0], 3)]
    last = after(halves[1], near[0])
    last_halves = [over_z(last, 2), over_z(last, 3)]
    groups = [
        (near, ((1, 0), (1, 1))),
        (middle_halves, ((2, 0), (3, 0))),
        (last_halves, ((2, 1), (3, 1))),
    ]
    mine = [packed]
    origins = [chip * count + place]
    for (first, second), kinds in groups:
        first_x = permute_xor(first, "head", 1)
        second_y = permute_xor(second, "head", 2)
        first_y = permute_xor(first, "head", 2)
        second_x = permute_xor(second, "head", 1)
        first_xy = permute_xor(first_x, "head", 2)
        second_xy = permute_xor(second_y, "head", 1)
        mine += [first, second, first_x, second_x, first_y, second_y, first_xy, second_xy]
        for mask in range(heads):
            for chip_mask, half in kinds:
                begin = (chip ^ chip_mask) * count + (head ^ mask) * size + half * cut
                origins.append(begin + jnp.arange(cut, dtype=jnp.int32))
    other = [permute_xor(piece, "seq", 1) for piece in mine]
    origins = jnp.concatenate(origins)
    slots = jnp.concatenate([origins, origins])
    cores = jnp.repeat(jnp.stack([core, 1 - core]), NBLK // 2)
    owner_slot = (slots // count * 2 + cores) * count + slots % count
    return mine + other, owner_order[owner_slot]


LOW_GROUP = (STARTS[0], STARTS[1])
HIGH_GROUP = (STARTS[1], STARTS[4])


def fetch_blocks(number_ref, sources, blocks, arrive, group):
    low, high = group
    first = 0
    for source in sources:

        def start(place, carry, source=source, first=first):
            number = number_ref[first + place]

            @pl.when((number >= low) & (number < high))
            def _():
                pltpu.make_async_copy(source.at[place], blocks.at[number - low], arrive).start()

            return carry

        count = source.shape[0]
        if count <= 6:
            for place in range(count):
                start(place, 0)
        else:
            lax.fori_loop(0, count, start, 0)
        first += count


def lay_out_blocks(panel_ref, blocks, sheet, group, begin, end):
    low = group[0]
    half = low_lanes(B // 2)

    def lay_out(index, carry):
        pair = low // 2 + index
        row = pl.multiple_of((panel_ref[pair] - low // 4) * B, B)
        lane = pl.multiple_of((pair % 2) * 384, LANES)
        even, odd = 2 * index, 2 * index + 1
        sheet[pl.ds(row, B), pl.ds(lane, LANES)] = blocks[even, :B, :]
        sheet[pl.ds(row, B), pl.ds(lane + 2 * LANES, LANES)] = blocks[odd, :B, :]
        even_rest = blocks[even, B:, :].astype(F32)
        odd_rest = blocks[odd, B:, :].astype(F32)
        turned = pltpu.roll(jnp.where(half, odd_rest, even_rest), LANES // 2, 1)
        center = jnp.concatenate([jnp.where(half, even_rest, odd_rest), turned], axis=0)
        sheet[pl.ds(row, B), pl.ds(lane + LANES, LANES)] = center.astype(BF16)
        return carry

    lax.fori_loop(begin, end, lay_out, 0, unroll=4)


def group_scratch(group):
    count = group[1] - group[0]
    return [
        pltpu.VMEM((count * 48, MODEL_WIDTH), BF16),
        pltpu.VMEM((count, REST, LANES), BF16),
        pltpu.SemaphoreType.DMA,
        pltpu.SemaphoreType.DMA,
    ]


def project_kernel(number_ref, panel_ref, x_ref, vec_ref, *refs):
    sources = refs[:-6]
    projected_ref, sheet_out, sheet, blocks, arrive, leave = refs[-6:]
    fetch_blocks(number_ref, sources, blocks, arrive, LOW_GROUP)
    pltpu.make_async_copy(blocks, blocks, arrive).wait()
    lay_out_blocks(panel_ref, blocks, sheet, LOW_GROUP, 0, blocks.shape[0] // 2)
    copy = pltpu.make_async_copy(sheet, sheet_out, leave)
    copy.start()
    for panel in range(3):
        weight = sheet[panel * MODEL_WIDTH : (panel + 1) * MODEL_WIDTH, :]
        for tile in range(x_ref.shape[0] // 512):
            rows = slice(tile * 512, (tile + 1) * 512)
            value = dot(x_ref[rows, :], weight)
            if panel != 1:
                value = value + vec_ref[4 + panel // 2 : 5 + panel // 2, :]
            projected_ref[rows, panel * MODEL_WIDTH : (panel + 1) * MODEL_WIDTH] = value.astype(BF16)
    copy.wait()


def project(x, vectors, sources, numbers):
    rows = x.shape[0]
    whole = lambda shape: pl.BlockSpec(shape, lambda i, *_: (0,) * len(shape))
    anywhere = pl.BlockSpec(memory_space=pl.ANY)
    return pl.pallas_call(
        project_kernel,
        grid_spec=pltpu.PrefetchScalarGridSpec(
            num_scalar_prefetch=2,
            grid=(1,),
            in_specs=[whole(x.shape), whole(vectors.shape)] + [anywhere] * len(sources),
            out_specs=[whole((rows, 3 * MODEL_WIDTH)), anywhere],
            scratch_shapes=group_scratch(LOW_GROUP),
        ),
        out_shape=[
            jax.ShapeDtypeStruct((rows, 3 * MODEL_WIDTH), BF16),
            jax.ShapeDtypeStruct((STARTS[1] * 48, MODEL_WIDTH), BF16),
        ],
        compiler_params=pltpu.CompilerParams(vmem_limit_bytes=48 * MEBI),
        cost_estimate=cost(6 * rows * MODEL_WIDTH**2, 16 * MEBI),
        name="project_queries_keys_values",
    )(numbers, jnp.array(panel_of_block()[::2]), x, vectors, *sources)


KEY_TILE = 256


def key_tiles(labels, tile):
    edges = labels.reshape(-1, tile)
    first, last = edges[:, 0], edges[:, -1]
    start = jnp.sum(labels[None, :] < first[:, None], axis=1, dtype=jnp.int32) // KEY_TILE
    end = jnp.sum(labels[None, :] <= last[:, None], axis=1, dtype=jnp.int32)
    return start, (end + KEY_TILE - 1) // KEY_TILE - start


def over_tiles(tile, start_ref, count_ref, run):
    def block(index, carry):
        rows = pl.ds(pl.multiple_of(index * tile, tile), tile)
        start = pl.multiple_of(start_ref[index] * KEY_TILE, KEY_TILE)
        for count in range(1, ROW_POSITIONS // KEY_TILE + 1):
            keys = pl.ds(start, count * KEY_TILE)
            pl.when(count_ref[index] == count)(functools.partial(run, rows, keys))
        return carry

    lax.fori_loop(0, ROW_POSITIONS // tile, block, 0)


def attention_forward_kernel(
    tile, start_ref, count_ref, number_ref, panel_ref, row_ref, column_ref, q_ref, k_ref, v_ref, *refs
):
    sources = refs[:-8]
    out_ref, log_ref, sheet_out, vt_ref, sheet, blocks, arrive, leave = refs[-8:]
    groups = q_ref.shape[1] // LANES
    step, last = pl.program_id(0), pl.num_programs(0) - 1

    @pl.when(step == 0)
    def _():
        fetch_blocks(number_ref, sources, blocks, arrive, HIGH_GROUP)

    @pl.when(step == 1)
    def _():
        pltpu.make_async_copy(blocks, blocks, arrive).wait()
        lay_out_blocks(panel_ref, blocks, sheet, HIGH_GROUP, 0, blocks.shape[0] // 2)
        pltpu.make_async_copy(sheet, sheet_out, leave).start()

    vt_ref[...] = v_ref[...].T
    low = low_lanes(tile)

    def run(rows, keys):
        same = column_ref[keys, :] == row_ref[:, rows]
        for group in range(groups):
            lanes = slice(group * LANES, (group + 1) * LANES)
            queries = q_ref[rows, lanes] * jnp.bfloat16(HEAD_SIZE**-0.5)
            mixed = []
            for part in range(2):
                chosen = jnp.where(low if part == 0 else ~low, queries, jnp.zeros_like(queries))
                scores = dot(k_ref[keys, lanes], chosen, ((1,), (1,)))
                scores = jnp.where(same, scores, -1e30)
                peak = jnp.max(scores, axis=0, keepdims=True)
                exponents = jnp.exp(scores - peak)
                total = jnp.sum(exponents, axis=0, keepdims=True)
                probabilities = (exponents * (1.0 / total)).astype(BF16)
                first = group * LANES + part * HEAD_SIZE
                mixed.append(dot(vt_ref[first : first + HEAD_SIZE, keys], probabilities))
                log_ref[group, part : part + 1, rows] = peak + jnp.log(total)
            out_ref[rows, lanes] = jnp.concatenate(mixed, axis=0).T.astype(BF16)

    over_tiles(tile, start_ref, count_ref, run)

    @pl.when(step == last)
    def _():
        pltpu.make_async_copy(sheet, sheet_out, leave).wait()


def attention_forward(projected, labels, sources, numbers, tile=512, groups=2):
    start, count = key_tiles(labels, tile)
    width = groups * LANES
    steps = PAIRS // groups
    rows = ROW_POSITIONS
    anywhere = pl.BlockSpec(memory_space=pl.ANY)
    return pl.pallas_call(
        functools.partial(attention_forward_kernel, tile),
        grid_spec=pltpu.PrefetchScalarGridSpec(
            num_scalar_prefetch=4,
            grid=(steps,),
            in_specs=[
                pl.BlockSpec((1, rows), lambda h, *_: (0, 0)),
                pl.BlockSpec((rows, 1), lambda h, *_: (0, 0)),
                pl.BlockSpec((rows, width), lambda h, *_: (0, h)),
                pl.BlockSpec((rows, width), lambda h, *_: (0, steps + h)),
                pl.BlockSpec((rows, width), lambda h, *_: (0, 2 * steps + h)),
            ]
            + [anywhere] * len(sources),
            out_specs=[
                pl.BlockSpec((rows, width), lambda h, *_: (0, h)),
                pl.BlockSpec((groups, 8, rows), lambda h, *_: (h, 0, 0)),
                anywhere,
            ],
            scratch_shapes=[pltpu.VMEM((width, rows), BF16)] + group_scratch(HIGH_GROUP),
        ),
        out_shape=[
            jax.ShapeDtypeStruct((rows, MODEL_WIDTH), BF16),
            jax.ShapeDtypeStruct((PAIRS, 8, rows), F32),
            jax.ShapeDtypeStruct(((NBLK - STARTS[1]) * 48, MODEL_WIDTH), BF16),
        ],
        compiler_params=pltpu.CompilerParams(vmem_limit_bytes=56 * MEBI),
        cost_estimate=cost(16 * 10**9, 30 * MEBI),
        name="attention_forward",
    )(
        start,
        count,
        numbers,
        jnp.array(panel_of_block()[::2]),
        labels.reshape(1, rows),
        labels.reshape(rows, 1),
        projected,
        projected,
        projected,
        *sources,
    )


def attention_backward_kernel(
    tile,
    start_ref,
    count_ref,
    row_ref,
    column_ref,
    q_ref,
    k_ref,
    v_ref,
    d_ref,
    log_ref,
    out_ref,
    sum_ref,
    kt_ref,
    dk_ref,
    dv_ref,
):
    groups = q_ref.shape[1] // LANES
    factor = HEAD_SIZE**-0.5
    kt_ref[...] = k_ref[...].T
    dk_ref[...] = jnp.zeros_like(dk_ref)
    dv_ref[...] = jnp.zeros_like(dv_ref)
    low = low_lanes(tile)

    def run(rows, keys):
        same = column_ref[keys, :] == row_ref[:, rows]
        for group in range(groups):
            lanes = slice(group * LANES, (group + 1) * LANES)
            queries = q_ref[rows, lanes] * jnp.bfloat16(factor)
            upstream = d_ref[rows, lanes]
            d_queries = []
            d_keys = d_values = 0.0
            for part in range(2):
                mask = low if part == 0 else ~low
                chosen = jnp.where(mask, queries, jnp.zeros_like(queries))
                d_chosen = jnp.where(mask, upstream, jnp.zeros_like(upstream))
                scores = dot(k_ref[keys, lanes], chosen, ((1,), (1,)))
                exponents = jnp.exp(scores - log_ref[group, part : part + 1, rows])
                probabilities = jnp.where(same, exponents, 0.0)
                d_probs = dot(v_ref[keys, lanes], d_chosen, ((1,), (1,)))
                inner = jnp.sum(probabilities * d_probs, axis=0, keepdims=True)
                d_scores = (probabilities * (d_probs - inner)).astype(BF16)
                d_values += dot(probabilities.astype(BF16), d_chosen)
                d_keys += dot(d_scores, chosen)
                first = group * LANES + part * HEAD_SIZE
                d_queries.append(dot(kt_ref[first : first + HEAD_SIZE, keys], d_scores))
            dk_ref[keys, lanes] += d_keys
            dv_ref[keys, lanes] += d_values
            out_ref[0, rows, lanes] = (jnp.concatenate(d_queries, axis=0).T * factor).astype(BF16)

    over_tiles(tile, start_ref, count_ref, run)
    out_ref[1] = dk_ref[...].astype(BF16)
    out_ref[2] = dv_ref[...].astype(BF16)
    sum_ref[0:1, :] = jnp.sum(out_ref[0].astype(F32), axis=0, keepdims=True)
    sum_ref[1:2, :] = jnp.sum(out_ref[2].astype(F32), axis=0, keepdims=True)


def attention_backward(projected, tiles, labels, d_attended, logs, first, tile=256, groups=2):
    start, count = tiles
    width = groups * LANES
    steps = PAIRS // groups
    rows = ROW_POSITIONS
    return pl.pallas_call(
        functools.partial(attention_backward_kernel, tile),
        grid_spec=pltpu.PrefetchScalarGridSpec(
            num_scalar_prefetch=2,
            grid=(1,),
            in_specs=[
                pl.BlockSpec((1, rows), lambda h, *_: (0, 0)),
                pl.BlockSpec((rows, 1), lambda h, *_: (0, 0)),
                pl.BlockSpec((rows, width), lambda h, *_: (0, first)),
                pl.BlockSpec((rows, width), lambda h, *_: (0, steps + first)),
                pl.BlockSpec((rows, width), lambda h, *_: (0, 2 * steps + first)),
                pl.BlockSpec((rows, width), lambda h, *_: (0, first)),
                pl.BlockSpec((groups, 8, rows), lambda h, *_: (first, 0, 0)),
            ],
            out_specs=[
                pl.BlockSpec((3, rows, width), lambda h, *_: (0, 0, 0)),
                pl.BlockSpec((8, width), lambda h, *_: (0, 0)),
            ],
            scratch_shapes=[
                pltpu.VMEM((width, rows), BF16),
                pltpu.VMEM((rows, width), F32),
                pltpu.VMEM((rows, width), F32),
            ],
        ),
        out_shape=[
            jax.ShapeDtypeStruct((3, rows, width), BF16),
            jax.ShapeDtypeStruct((8, width), F32),
        ],
        compiler_params=pltpu.CompilerParams(vmem_limit_bytes=48 * MEBI),
        cost_estimate=cost(11 * 10**9, 6 * rows * MODEL_WIDTH),
        name="attention_backward",
    )(
        start,
        count,
        labels.reshape(1, rows),
        labels.reshape(rows, 1),
        projected,
        projected,
        projected,
        d_attended,
        logs,
    )


def mean(value):
    return jnp.sum(value, axis=1, keepdims=True) * (1.0 / MODEL_WIDTH)


def load_once(step, pairs, semaphores):
    copies = [pltpu.make_async_copy(source, held, semaphores.at[i]) for i, (source, held) in enumerate(pairs)]

    @pl.when(step == 0)
    def _():
        for copy in copies:
            copy.start()

    def wait(index):
        pl.when(step == 0)(copies[index].wait)

    return wait


def feed_forward_kernel(
    attended_ref,
    x_ref,
    upstream_ref,
    vec_ref,
    sheet_ref,
    output_ref,
    normed_ref,
    normal_ref,
    scale_ref,
    activated_ref,
    slope_ref,
    d_mixed_ref,
    d_feed_ref,
    sums_ref,
    out_weight,
    up_weight,
    down_weight,
    semaphores,
):
    width = MODEL_WIDTH
    step = pl.program_id(0)
    wait = load_once(
        step,
        [
            (sheet_ref.at[pl.ds(0, width), :], out_weight),
            (sheet_ref.at[pl.ds(width, FF), :], up_weight),
            (sheet_ref.at[pl.ds(width + FF, FF), :], down_weight),
        ],
        semaphores,
    )

    @pl.when(step == 0)
    def _():
        sums_ref[...] = jnp.zeros_like(sums_ref)

    def add_up(row, value):
        sums_ref[row : row + 1, :] += jnp.sum(value, axis=0, keepdims=True)

    def vector(row):
        return vec_ref[row : row + 1, :]

    wait(0)
    hidden = x_ref[...].astype(F32) + (dot(attended_ref[...], out_weight[...]) + vector(6))
    center = hidden - mean(hidden)
    first_scale = lax.rsqrt(mean(center * center) + NORM_EPSILON)
    first_normal = center * first_scale
    normal_ref[...] = first_normal
    scale_ref[...] = first_scale
    normed = first_normal * vector(0) + vector(1)
    normed_low = normed.astype(BF16)
    normed_ref[...] = normed_low
    wait(1)
    wait(2)
    feed_out = vector(7)
    for chunk in range(CHUNKS):
        part = slice(chunk * width, (chunk + 1) * width)
        before = dot(normed_low, up_weight[part, :]) + vector(8 + chunk)
        share = 0.5 + 0.5 * lax.erf(before * np.float32(np.sqrt(0.5)))
        density = jnp.exp(before * before * -0.5) * np.float32(1.0 / np.sqrt(2.0 * np.pi))
        slope_ref[:, part] = share + before * density
        activated = (before * share).astype(BF16)
        activated_ref[:, part] = activated
        feed_out = feed_out + dot(activated, down_weight[part, :])
    mixed = normed + feed_out
    center = mixed - mean(mixed)
    second_scale = lax.rsqrt(mean(center * center) + NORM_EPSILON)
    second_normal = center * second_scale
    output_ref[...] = (second_normal * vector(2) + vector(3)).astype(BF16)
    upstream = upstream_ref[...].astype(F32)
    add_up(2, upstream * second_normal)
    add_up(3, upstream)
    scaled = upstream * vector(2)
    d_mixed = second_scale * (scaled - mean(scaled) - second_normal * mean(scaled * second_normal))
    d_mixed_ref[...] = d_mixed
    d_feed = d_mixed.astype(BF16)
    d_feed_ref[...] = d_feed
    add_up(7, d_feed.astype(F32))


def feed_backward_kernel(
    normal_ref,
    scale_ref,
    slope_ref,
    d_mixed_ref,
    d_feed_ref,
    vec_ref,
    sheet_ref,
    d_before_ref,
    d_first_ref,
    d_branch_ref,
    d_attended_ref,
    sums_ref,
    out_weight,
    up_weight,
    down_weight,
    semaphores,
):
    width = MODEL_WIDTH
    step = pl.program_id(0)
    wait = load_once(
        step,
        [
            (sheet_ref.at[pl.ds(width + FF, FF), :], down_weight),
            (sheet_ref.at[pl.ds(width, FF), :], up_weight),
            (sheet_ref.at[pl.ds(0, width), :], out_weight),
        ],
        semaphores,
    )

    @pl.when(step == 0)
    def _():
        sums_ref[...] = jnp.zeros_like(sums_ref)

    def add_up(row, value):
        sums_ref[row : row + 1, :] += jnp.sum(value, axis=0, keepdims=True)

    wait(0)
    wait(1)
    wait(2)
    d_feed = d_feed_ref[...]
    d_normed = d_mixed_ref[...]
    for chunk in range(CHUNKS):
        part = slice(chunk * width, (chunk + 1) * width)
        d_active = dot(d_feed, down_weight[part, :], ((1,), (1,)))
        d_before = (d_active * slope_ref[:, part]).astype(BF16)
        d_before_ref[:, part] = d_before
        add_up(8 + chunk, d_before.astype(F32))
        d_normed = d_normed + dot(d_before, up_weight[part, :], ((1,), (1,)))
    first_normal = normal_ref[...]
    add_up(0, d_normed * first_normal)
    add_up(1, d_normed)
    scaled = d_normed * vec_ref[0:1, :]
    d_first = scale_ref[...] * (scaled - mean(scaled) - first_normal * mean(scaled * first_normal))
    d_first_ref[...] = d_first
    d_branch = d_first.astype(BF16)
    d_branch_ref[...] = d_branch
    add_up(6, d_branch.astype(F32))
    d_attended_ref[...] = dot(d_branch, out_weight[...], ((1,), (1,))).astype(BF16)


FEED_TILE = 256


def feed_call(kernel, name, rows, ins, outs, flops, values):
    tile = FEED_TILE
    width = MODEL_WIDTH
    by_tile = lambda columns: pl.BlockSpec((tile, columns), lambda i: (i, 0))
    fixed = pl.BlockSpec((12, width), lambda i: (0, 0))
    return pl.pallas_call(
        kernel,
        grid=(rows // tile,),
        in_specs=[by_tile(columns) for columns in ins] + [fixed, pl.BlockSpec(memory_space=pl.ANY)],
        out_specs=[by_tile(columns) for columns, _ in outs] + [fixed],
        out_shape=[jax.ShapeDtypeStruct((rows, columns), dtype) for columns, dtype in outs]
        + [jax.ShapeDtypeStruct((12, width), F32)],
        scratch_shapes=[
            pltpu.VMEM((width, width), BF16),
            pltpu.VMEM((FF, width), BF16),
            pltpu.VMEM((FF, width), BF16),
            pltpu.SemaphoreType.DMA((3,)),
        ],
        compiler_params=pltpu.CompilerParams(vmem_limit_bytes=58 * MEBI),
        cost_estimate=cost(flops, rows * width * 40),
        name=name,
    )(*values)


def feed_forward(attended, x, upstream, vectors, sheet):
    rows, width = x.shape
    return feed_call(
        feed_forward_kernel,
        "feed_forward",
        rows,
        [width] * 3,
        [(width, BF16), (width, BF16), (width, F32), (1, F32), (FF, BF16), (FF, F32), (width, F32), (width, BF16)],
        rows * width * (FF * 4 + width * 2),
        (attended, x, upstream, vectors, sheet),
    )


def feed_backward(normal, scale, slope, d_mixed, d_feed, vectors, sheet):
    rows, width = normal.shape
    return feed_call(
        feed_backward_kernel,
        "feed_backward",
        rows,
        [width, 1, FF, width, width],
        [(FF, BF16), (width, F32), (width, BF16), (width, BF16)],
        rows * width * (FF * 4 + width * 2),
        (normal, scale, slope, d_mixed, d_feed, vectors, sheet),
    )


def store_panels(value, core, kept_ref, sent_ref):
    for kept_parity in range(2):

        @pl.when(core == kept_parity)
        def _():
            for panel in range(4):
                ref = kept_ref if panel % 2 == kept_parity else sent_ref
                for quarter in range(4):
                    first = panel * B + quarter * 48
                    ref[quarter, panel // 2] = value[first : first + 48].astype(BF16)


def gradient_kernel(pairs, core_ref, *refs):
    kept_ref, sent_ref = refs[-2:]
    step = pl.program_id(0)
    for low, high, left, right in pairs:

        def run(left=refs[left], right=refs[right]):
            right = right[0] if len(right.shape) == 3 else right[...]
            store_panels(dot(left[...], right, ((0,), (0,))), core_ref[0], kept_ref, sent_ref)

        if low == 0 and high == CHUNKS:
            run()
        else:
            pl.when((step >= low) & (step < high))(run)


def gradient_call(pairs, specs, values, name):
    core = (lax.axis_index("seq") % 2).reshape(1).astype(jnp.int32)
    shape = jax.ShapeDtypeStruct((4, 2 * CHUNKS, 48, MODEL_WIDTH), BF16)
    spec = pl.BlockSpec((4, 2, 48, MODEL_WIDTH), lambda i, *_: (0, i, 0, 0))
    return pl.pallas_call(
        functools.partial(gradient_kernel, pairs),
        grid_spec=pltpu.PrefetchScalarGridSpec(
            num_scalar_prefetch=1, grid=(CHUNKS,), in_specs=specs, out_specs=[spec, spec]
        ),
        out_shape=[shape, shape],
        compiler_params=pltpu.CompilerParams(vmem_limit_bytes=48 * MEBI),
        cost_estimate=cost(2 * ROW_POSITIONS * CHUNKS * MODEL_WIDTH**2, 16 * MEBI),
        name=name,
    )(core, *values)


FIXED_ROWS = pl.BlockSpec((ROW_POSITIONS, MODEL_WIDTH), lambda i, *_: (0, 0))
MOVING_ROWS = pl.BlockSpec((ROW_POSITIONS, MODEL_WIDTH), lambda i, *_: (0, i))


def down_gradient(activated, d_feed):
    pairs = [(0, CHUNKS, 0, 1)]
    return gradient_call(pairs, [MOVING_ROWS, FIXED_ROWS], (activated, d_feed), "down_gradient")


def up_gradient(normed_low, d_before):
    pairs = [(0, CHUNKS, 0, 1)]
    return gradient_call(pairs, [FIXED_ROWS, MOVING_ROWS], (normed_low, d_before), "up_gradient")


def attention_gradients(x, d_projected, attended, d_branch):
    pairs = [(0, 3, 0, 1), (3, 4, 2, 3)]
    third = pl.BlockSpec(
        (1, ROW_POSITIONS, MODEL_WIDTH), lambda i, *_: (jnp.minimum(i, 2), 0, 0)
    )
    return gradient_call(
        pairs,
        [FIXED_ROWS, third, FIXED_ROWS, FIXED_ROWS],
        (x, d_projected, attended, d_branch),
        "attention_gradients",
    )


def input_gradient_kernel(d_ref, sheet_ref, d_first_ref, out_ref):
    value = d_first_ref[...]
    for part in range(3):
        weight = sheet_ref[part * MODEL_WIDTH : (part + 1) * MODEL_WIDTH, :]
        value = value + dot(d_ref[part], weight, ((1,), (1,)))
    out_ref[...] = value.astype(BF16)


def input_gradient(d_projected, sheet, d_first, tile=256):
    rows = d_first.shape[0]
    return pl.pallas_call(
        input_gradient_kernel,
        grid=(rows // tile,),
        in_specs=[
            pl.BlockSpec((3, tile, MODEL_WIDTH), lambda i: (0, i, 0)),
            pl.BlockSpec((3 * MODEL_WIDTH, MODEL_WIDTH), lambda i: (0, 0), pipeline_mode=pl.Buffered(1)),
            pl.BlockSpec((tile, MODEL_WIDTH), lambda i: (i, 0)),
        ],
        out_specs=pl.BlockSpec((tile, MODEL_WIDTH), lambda i: (i, 0)),
        out_shape=jax.ShapeDtypeStruct((rows, MODEL_WIDTH), BF16),
        compiler_params=pltpu.CompilerParams(vmem_limit_bytes=48 * MEBI),
        cost_estimate=cost(6 * rows * MODEL_WIDTH**2, 14 * MEBI),
        name="input_gradient",
    )(d_projected, sheet, d_first)


def add_parts(*parts):
    return functools.reduce(jnp.add, [part.astype(F32) for part in parts]).astype(BF16)


def pick(value, index, axis=0):
    return lax.dynamic_index_in_dim(value, index, axis, keepdims=False)


def head_first_sum(kept):
    head = lax.axis_index("head")
    x, y = head % 2, head // 2
    cut = kept.shape[1] // 2
    square = kept.reshape((2, 2) + kept.shape[1:])
    first, second = square[:, :, :cut], square[:, :, cut:]
    first_x = permute_xor(pick(first, 1 - x, 1), "head", 1)
    second_y = permute_xor(pick(second, 1 - y, 0), "head", 2)
    return add_parts(pick(first, x, 1), first_x), add_parts(pick(second, y, 0), second_y)


def head_second_sum(first, second):
    head = lax.axis_index("head")
    x, y = head % 2, head // 2
    first_y = permute_xor(pick(first, 1 - y), "head", 2)
    second_x = permute_xor(pick(second, 1 - x), "head", 1)
    return jnp.concatenate(
        [add_parts(pick(first, y), first_y), add_parts(pick(second, x), second_x)]
    )


def chip_sum(quarter):
    chips = lax.axis_size("seq") // 2
    chip = lax.axis_index("seq") // 2
    panels = quarter.shape[0]
    if panels % chips:
        groups = [list(range(core, 2 * chips, 2)) for core in range(2)]
        return lax.psum(quarter.astype(F32), "seq", axis_index_groups=groups).astype(BF16)
    quarter = quarter.reshape((chips, panels // chips) + quarter.shape[1:])
    return add_parts(
        pick(quarter, chip),
        *[permute_xor(pick(quarter, chip ^ mask), "seq", 2 * mask) for mask in range(1, chips)],
    )


def chip_gather(share, panels):
    if share.shape[0] == panels:
        return share
    chips = lax.axis_size("seq") // 2
    return jnp.concatenate(
        [share] + [permute_xor(share, "seq", 2 * mask) for mask in range(1, chips)]
    )


def exchange_cores(kept, sent):
    return add_parts(kept, permute_xor(sent, "seq", 1))


def pick_kernel(count, row_ref, lane_ref, which_ref, odd_ref, *refs):
    sources, out_ref, parts, semaphore = refs[:-3], refs[-3], refs[-2], refs[-1]

    def start(slot, carry):
        row = row_ref[slot]
        lane = pl.multiple_of(lane_ref[slot], LANES)
        main = pl.multiple_of(lane + odd_ref[slot] * 2 * LANES, LANES)
        center = pl.multiple_of(lane + LANES, LANES)
        for index, source in enumerate(sources):

            @pl.when(which_ref[slot] == index)
            def _():
                for half, begin in enumerate((main, center)):
                    pltpu.make_async_copy(
                        source.at[row, :, pl.ds(begin, LANES)],
                        parts.at[slot, pl.ds(half * 48, 48), :],
                        semaphore,
                    ).start()

        return carry

    lax.fori_loop(0, count, start, 0)
    pltpu.make_async_copy(parts, parts, semaphore).wait()
    half = low_lanes(24)

    def fold(slot, carry):
        center = parts[slot, 48:, :].astype(F32)
        top, bottom = center[:24], pltpu.roll(center[24:], LANES // 2, 1)
        rest = jnp.where(half == (odd_ref[slot] == 0), top, bottom)
        out_ref[slot, :48, :] = parts[slot, :48, :]
        out_ref[slot, 48:, :] = rest.astype(BF16)
        return carry

    lax.fori_loop(0, count, fold, 0)


def pick_blocks(numbers, gathered):
    chips = lax.axis_size("seq") // 2
    seq = lax.axis_index("seq")
    chip, core = seq // 2, seq % 2
    panels = jnp.array(panel_of_block())[numbers]
    which = jnp.zeros_like(numbers)
    row = jnp.zeros_like(numbers)
    sources = []
    for first, last, (mine, other) in gathered:
        inside = (panels >= first) & (panels < last)
        local = panels - first
        pieces = chips if mine.shape[0] % chips == 0 else 1
        each = mine.shape[0] // pieces
        spot = ((local // 2 // each) ^ (chip % pieces)) * each + local // 2 % each
        row = jnp.where(inside, spot, row)
        which = jnp.where(inside, len(sources) + ((local % 2) ^ core), which)
        sources += [mine, other]
    count = numbers.shape[0]
    return pl.pallas_call(
        functools.partial(pick_kernel, count),
        grid_spec=pltpu.PrefetchScalarGridSpec(
            num_scalar_prefetch=4,
            grid=(1,),
            in_specs=[pl.BlockSpec(memory_space=pl.ANY)] * len(sources),
            out_specs=pl.BlockSpec((count, QUARTER, LANES), lambda i, *_: (0, 0, 0)),
            scratch_shapes=[pltpu.VMEM((count, 96, LANES), BF16), pltpu.SemaphoreType.DMA],
        ),
        out_shape=jax.ShapeDtypeStruct((count, QUARTER, LANES), BF16),
        cost_estimate=cost(0, count * QUARTER * LANES * 4),
        name="pick_owned_blocks",
    )(row, numbers // 2 % 2 * 384, which, numbers % 2, *sources)


def shampoo_kernel(
    number_ref,
    quarter_ref,
    part0,
    part1,
    part2,
    part3,
    momentum_ref,
    left_ref,
    right_ref,
    root_left_ref,
    root_right_ref,
    master_ref,
    new_momentum_ref,
    new_left_ref,
    new_right_ref,
    new_master_ref,
    main_ref,
    rest_ref,
):
    count = momentum_ref.shape[0]
    first = pl.program_id(0) * count
    low = low_lanes(B)
    for slot in range(count):
        for index, part in enumerate((part0, part1, part2, part3)):
            first_row = pl.multiple_of(quarter_ref[index] * 48, 8)
            value = part[slot].astype(F32)
            main_ref[pl.ds(first_row, 48), :] = value[:48]
            rest_ref[pl.ds(first_row, 24), :] = value[48:]
            rest_ref[pl.ds(first_row + 24, 24), :] = pltpu.roll(value[48:], LANES // 2, 1)
        main = main_ref[...]
        rest = rest_ref[...]
        odd = number_ref[first + slot] % 2 == 1
        spun = pltpu.roll(main, LANES // 2, 1)
        left_lanes = jnp.where(odd, jnp.where(low, pltpu.roll(rest, LANES // 2, 1), spun), main)
        right_lanes = jnp.where(odd, spun, rest)
        gradient = jnp.concatenate([left_lanes, right_lanes[:, : LANES // 2]], axis=1)
        new_momentum = MOMENTUM_DECAY * momentum_ref[slot] + (1.0 - MOMENTUM_DECAY) * gradient
        new_momentum_ref[slot] = new_momentum
        grad_low = gradient.astype(BF16)
        new_left_ref[slot] = STAT_DECAY * left_ref[slot] + (1.0 - STAT_DECAY) * dot(
            grad_low, grad_low, ((1,), (1,))
        )
        new_right_ref[slot] = STAT_DECAY * right_ref[slot] + (1.0 - STAT_DECAY) * dot(
            grad_low, grad_low, ((0,), (0,))
        )
        leftward = dot(root_left_ref[slot].astype(BF16), new_momentum.astype(BF16))
        preconditioned = dot(leftward.astype(BF16), root_right_ref[slot].astype(BF16))
        master = master_ref[slot]
        new_master_ref[slot] = master - MATRIX_RATE * (preconditioned + WEIGHT_DECAY * master)


def shampoo(numbers, parts, states):
    count = numbers.shape[0]
    group = max(size for size in range(1, 4) if count % size == 0)
    spec = pl.BlockSpec((group, B, B), lambda i, *_: (i, 0, 0))
    part_spec = pl.BlockSpec((group, QUARTER, LANES), lambda i, *_: (i, 0, 0))
    quarters = lax.axis_index("head") ^ jnp.arange(4, dtype=jnp.int32)
    return pl.pallas_call(
        shampoo_kernel,
        grid_spec=pltpu.PrefetchScalarGridSpec(
            num_scalar_prefetch=2,
            grid=(count // group,),
            in_specs=[part_spec] * 4 + [spec] * 6,
            out_specs=[spec] * 4,
            scratch_shapes=[pltpu.VMEM((B, LANES), F32), pltpu.VMEM((B, LANES), F32)],
        ),
        out_shape=[jax.ShapeDtypeStruct((count, B, B), F32)] * 4,
        compiler_params=pltpu.CompilerParams(vmem_limit_bytes=48 * MEBI),
        cost_estimate=cost(8 * count * B**3, 10 * count * B * B * 4),
        name="shampoo_blocks",
    )(numbers, quarters, *parts, *states)


def sum_everywhere(value):
    for axis in ("head", "seq"):
        mask = 1
        while mask < lax.axis_size(axis):
            value = value + permute_xor(value, axis, mask)
            mask *= 2
    return value


def adam_step(vector_grad, vec_first, vec_second, vectors):
    new_first = FIRST_DECAY * vec_first + (1.0 - FIRST_DECAY) * vector_grad
    new_second = SECOND_DECAY * vec_second + (1.0 - SECOND_DECAY) * vector_grad * vector_grad
    corrected_first = new_first / (1.0 - FIRST_DECAY**STEP)
    corrected_second = new_second / (1.0 - SECOND_DECAY**STEP)
    new_vectors = vectors - VECTOR_RATE * corrected_first / (
        jnp.sqrt(corrected_second) + ADAM_EPSILON
    )
    return (new_first, new_second, new_vectors)


def exchange_rows(value):
    return lax.all_to_all(value, "head", split_axis=0, concat_axis=0, tiled=True)


def local(
    tokens,
    cotangent,
    segment_ids,
    owner_order,
    master_blocks,
    momentum,
    stat_left,
    stat_right,
    root_left,
    root_right,
    vectors,
    vec_first,
    vec_second,
):
    width = MODEL_WIDTH
    count = master_blocks.shape[0]
    head = lax.axis_index("head")
    numbers = lax.dynamic_slice_in_dim(owner_order, lax.axis_index("seq") * count, count, 0)
    sheet_vectors = vectors.reshape(12, width)

    packed = pack_blocks(numbers, master_blocks)
    sources, source_numbers = gather_weights(packed, owner_order)
    x = exchange_rows(tokens).reshape(ROW_POSITIONS, width)
    upstream = exchange_rows(cotangent).reshape(ROW_POSITIONS, width)
    labels = lax.dynamic_index_in_dim(segment_ids, head, 0, keepdims=False)

    projected, input_sheet = project(x, sheet_vectors, sources, source_numbers)
    attended, logs, sheet = attention_forward(projected, labels, sources, source_numbers)
    output, normed_low, normal, scale, activated, slope, d_mixed, d_feed, sums = feed_forward(
        attended, x, upstream, sheet_vectors, sheet
    )
    half_panels = 2 * CHUNKS
    output = exchange_rows(output.reshape(tokens.shape))
    down = down_gradient(activated, d_feed)
    d_mixed = after(d_mixed, *down)
    d_before, d_first, d_branch, d_attended, more_sums = feed_backward(
        normal, scale, slope, d_mixed, d_feed, sheet_vectors, sheet
    )
    down = exchange_cores(*down)
    d_before = after(d_before, down, output)
    up = up_gradient(normed_low, d_before)
    tiles = key_tiles(labels, KEY_TILE)
    backward = lambda part, d_rows: attention_backward(projected, tiles, labels, d_rows, logs, part)
    parts = [backward(0, after(d_attended, *up))]
    down = head_first_sum(down)
    up = exchange_cores(*up)
    parts.append(backward(1, after(d_attended, up, *down, *parts[0])))
    down = head_second_sum(*down)
    parts.append(backward(2, after(d_attended, down, *parts[1])))
    up = head_first_sum(up)
    down = chip_sum(down)
    d_projected = jnp.concatenate([part[0] for part in parts], axis=2)
    bias_sums = jnp.concatenate([part[1] for part in parts], axis=1)
    rest = attention_gradients(x, after(d_projected, down, *up), attended, d_branch)
    up = head_second_sum(*up)
    down = chip_gather(down, half_panels)
    rest = exchange_cores(*rest)
    input_grad = input_gradient(after(d_projected, rest, up, down), input_sheet, d_first)
    up = chip_sum(up)
    rest = head_first_sum(rest)
    up = chip_gather(up, half_panels)
    rest = head_second_sum(*rest)
    input_grad = after(input_grad, rest, up).reshape(tokens.shape)
    input_grad = exchange_rows(input_grad).astype(F32)
    rest = chip_gather(chip_sum(rest), half_panels)
    rest, up, down = [(mine, permute_xor(mine, "seq", 1)) for mine in (rest, up, down)]

    sums = sums + more_sums
    sums = sum_everywhere(jnp.concatenate([sums[:4], bias_sums[:2], sums[6:]]))
    new_first, new_second, new_vectors = adam_step(sums.reshape(-1), vec_first, vec_second, vectors)

    picked = pick_blocks(numbers, [(0, 16, rest), (16, 32, up), (32, 48, down)])
    parts = [picked] + [permute_xor(picked, "head", mask) for mask in (1, 2, 3)]
    states = (momentum, stat_left, stat_right, root_left, root_right, master_blocks)
    new_momentum, new_left, new_right, new_master = shampoo(numbers, parts, states)
    return (
        output,
        input_grad,
        new_momentum,
        new_left,
        new_right,
        new_master,
        new_first,
        new_second,
        new_vectors,
    )


def solution(mesh):
    blocks = P("seq", None, None)
    positions = P("seq", "head", None)
    return jax.shard_map(
        local,
        mesh=mesh,
        in_specs=(positions, positions, P("seq", None), P()) + (blocks,) * 6 + (P(),) * 3,
        out_specs=(positions, positions) + (blocks,) * 4 + (P(),) * 3,
        check_vma=False,
    )
```

```python
import functools

import jax
import jax.numpy as jnp
import numpy as np
from jax import lax
from jax.experimental import pallas as pl
from jax.experimental.pallas import tpu as pltpu
from jax.sharding import PartitionSpec as P

MODEL_WIDTH = 768
HEAD_TOTAL = 12
HEAD_SIZE = 64
FF = 3072
ROW_POSITIONS = 1024
B = 192
STEP = 10
NBLK = 192
PAIRS = HEAD_TOTAL // 2
LANES = 128
REST = B * B // LANES
QUARTER = REST // 4
CHUNKS = FF // MODEL_WIDTH
MEBI = 2**20

NORM_EPSILON = 1e-05
STAT_DECAY = 0.5
MOMENTUM_DECAY = 0.5
MATRIX_RATE = 1.0
WEIGHT_DECAY = 0.01
FIRST_DECAY = 0.9
SECOND_DECAY = 0.999
VECTOR_RATE = 0.3
ADAM_EPSILON = 1e-08

F32 = jnp.float32
BF16 = jnp.bfloat16
STARTS = (0, 48, 64, 128, 192)


def panel_of_block():
    panels = []
    for block in range(NBLK):
        if block < STARTS[1]:
            panels.append((block % 12) // 4 * 4 + block // 12)
        elif block < STARTS[2]:
            panels.append(12 + (block - STARTS[1]) // 4)
        elif block < STARTS[3]:
            inner = block - STARTS[2]
            panels.append(16 + (inner % 16) // 4 * 4 + inner // 16)
        else:
            panels.append(32 + (block - STARTS[3]) // 4)
    return np.array(panels, np.int32)


def cost(flops, moved, transcendentals=0):
    return pl.CostEstimate(flops=flops, bytes_accessed=moved, transcendentals=transcendentals)


def dot(left, right, contract=((1,), (0,))):
    return lax.dot_general(left, right, (contract, ((), ())), preferred_element_type=F32)


def low_lanes(rows):
    return lax.broadcasted_iota(jnp.int32, (rows, LANES), 1) < LANES // 2


def pack_kernel(order_ref, blocks_ref, packed_ref):
    count = blocks_ref.shape[0]
    first = pl.program_id(0) * count
    half = low_lanes(B // 2)
    low = low_lanes(B)
    for slot in range(count):
        left = blocks_ref[slot, :, :LANES]
        narrow = blocks_ref[slot, :, LANES:]
        right = jnp.concatenate([narrow, narrow], axis=1)
        turned = pltpu.roll(left, LANES // 2, 1)
        odd = order_ref[first + slot] % 2 == 1
        main = jnp.where(odd, jnp.where(low, turned, right), left)
        even_rest = jnp.where(half, right[: B // 2], right[B // 2 :])
        odd_rest = jnp.where(half, left[B // 2 :], turned[: B // 2])
        packed_ref[slot, :B, :] = main.astype(BF16)
        packed_ref[slot, B:, :] = jnp.where(odd, odd_rest, even_rest).astype(BF16)


def pack_blocks(order, blocks):
    count = blocks.shape[0]
    group = max(size for size in range(1, 7) if count % size == 0)
    return pl.pallas_call(
        pack_kernel,
        grid_spec=pltpu.PrefetchScalarGridSpec(
            num_scalar_prefetch=1,
            grid=(count // group,),
            in_specs=[pl.BlockSpec((group, B, B), lambda i, *_: (i, 0, 0))],
            out_specs=pl.BlockSpec((group, REST, LANES), lambda i, *_: (i, 0, 0)),
        ),
        out_shape=jax.ShapeDtypeStruct((count, REST, LANES), BF16),
        cost_estimate=cost(0, count * B * B * 6),
        name="pack_weight_blocks",
    )(order, blocks)


def permute_xor(value, axis, mask):
    size = lax.axis_size(axis)
    return lax.ppermute(value, axis, [(i, i ^ mask) for i in range(size)])


def gate_kernel(*refs):
    del refs


def gate(values, others):
    flat = list(values)
    shapes = [jax.ShapeDtypeStruct(value.shape, value.dtype) for value in flat]
    return pl.pallas_call(
        gate_kernel,
        in_specs=[ANYWHERE] * (len(flat) + len(others)),
        out_specs=[ANYWHERE] * len(flat),
        out_shape=shapes,
        input_output_aliases={i: i for i in range(len(flat))},
        cost_estimate=cost(0, 0),
        name="gate",
    )(*flat, *others)


ANYWHERE = pl.BlockSpec(memory_space=pl.ANY)


def gathered_slots(heads, chips, count):
    size, cut = count // heads, count // heads // 2
    slots = np.zeros((heads, chips, 2, NBLK), np.int32)
    for head in range(heads):
        for chip in range(chips):
            places = [(chip, slot) for slot in range(count)]
            for kinds in GROUP_KINDS:
                for mask in range(heads):
                    for chip_mask, half in kinds:
                        begin = (head ^ mask) * size + half * cut
                        places += [(chip ^ chip_mask, begin + slot) for slot in range(cut)]
            for core in range(2):
                slots[head, chip, core] = [
                    (c * 2 + which) * count + slot for which in (core, 1 - core) for c, slot in places
                ]
    return slots


GROUP_KINDS = (((1, 0), (1, 1)), ((2, 0), (3, 0)), ((2, 1), (3, 1)))


def gather_weights(packed, owner_order, early):
    heads = lax.axis_size("head")
    chips = lax.axis_size("seq") // 2
    count = packed.shape[0]
    head = lax.axis_index("head")
    seq = lax.axis_index("seq")
    chip, core = seq // 2, seq % 2
    if count % (2 * heads) or chips != 4:
        return [lax.all_gather(packed, "seq", axis=0, tiled=True)], owner_order, early
    size = count // heads
    cut = size // 2
    slots = jnp.asarray(gathered_slots(heads, chips, count).reshape(-1, NBLK))
    slots = lax.dynamic_index_in_dim(slots, (head * chips + chip) * 2 + core, 0, keepdims=False)
    whole = jnp.arange(NBLK, dtype=jnp.int32)
    numbers = jnp.sum(jnp.where(slots[:, None] == whole[None, :], owner_order[None, :], 0), axis=1)
    own = lax.dynamic_slice_in_dim(packed, head * size, size, 0)
    halves = own[:cut], own[cut:]
    over_z = lambda half, mask: permute_xor(half, "seq", 2 * mask)
    near = [over_z(half, 1) for half in halves]
    halfway = [over_z(halves[0], 2), over_z(halves[0], 3)]
    halves = [halves[0], *gate([halves[1]], near)]
    last = [over_z(halves[1], 2), over_z(halves[1], 3)]
    near = gate(near, [numbers, *early[:-1]])

    def first_hop(first, second):
        return [
            permute_xor(first, "head", 1),
            permute_xor(second, "head", 2),
            permute_xor(second, "head", 1),
            permute_xor(first, "head", 2),
        ]

    def second_hop(first_x, second_y, *_):
        return [permute_xor(first_x, "head", 2), permute_xor(second_y, "head", 1)]

    def swap_cores(pieces):
        return [permute_xor(piece, "seq", 1) for piece in pieces]

    def arranged(pieces, one, two):
        first_x, second_y, second_x, first_y = one
        return [*pieces, first_x, second_x, first_y, second_y, *two]

    near_one = first_hop(*near)
    halfway_one = first_hop(*halfway)
    near_two = second_hop(*near_one)
    last = gate(last, [*halfway_one, early[-1]])
    halfway_two = second_hop(*halfway_one)
    last_one = first_hop(*last)
    last_two = second_hop(*last_one)
    mine = [
        packed,
        jnp.concatenate(arranged(near, near_one, near_two)),
        jnp.concatenate(arranged(halfway, halfway_one, halfway_two)),
        jnp.concatenate(arranged(last, last_one, ())),
        *last_two,
    ]
    return mine + swap_cores(mine), numbers, early


LOW_GROUP = (STARTS[0], STARTS[1])
HIGH_GROUP = (STARTS[1], STARTS[4])


def fetch_blocks(number_ref, sources, blocks, arrive, group):
    low, high = group
    first = 0
    for source in sources:

        def start(place, carry, source=source, first=first):
            number = number_ref[first + place]

            @pl.when((number >= low) & (number < high))
            def _():
                pltpu.make_async_copy(source.at[place], blocks.at[number - low], arrive).start()

            return carry

        count = source.shape[0]
        lax.fori_loop(0, count, start, 0, unroll=min(count, 4))
        first += count


def lay_out_blocks(panel_ref, blocks, sheet, group, begin, end):
    low = group[0]
    half = low_lanes(B // 2)

    def lay_out(index, carry):
        pair = low // 2 + index
        row = pl.multiple_of((panel_ref[pair] - low // 4) * B, B)
        lane = pl.multiple_of((pair % 2) * 384, LANES)
        even, odd = 2 * index, 2 * index + 1
        sheet[pl.ds(row, B), pl.ds(lane, LANES)] = blocks[even, :B, :]
        sheet[pl.ds(row, B), pl.ds(lane + 2 * LANES, LANES)] = blocks[odd, :B, :]
        even_rest = blocks[even, B:, :].astype(F32)
        odd_rest = blocks[odd, B:, :].astype(F32)
        turned = pltpu.roll(jnp.where(half, odd_rest, even_rest), LANES // 2, 1)
        center = jnp.concatenate([jnp.where(half, even_rest, odd_rest), turned], axis=0)
        sheet[pl.ds(row, B), pl.ds(lane + LANES, LANES)] = center.astype(BF16)
        return carry

    lax.fori_loop(begin, end, lay_out, 0, unroll=4)


def group_scratch(group):
    count = group[1] - group[0]
    return [
        pltpu.VMEM((count * 48, MODEL_WIDTH), BF16),
        pltpu.VMEM((count, REST, LANES), BF16),
        pltpu.SemaphoreType.DMA,
        pltpu.SemaphoreType.DMA,
    ]


def project_kernel(
    number_ref, panel_ref, x_ref, vec_ref, *refs
):
    sources = refs[:-6]
    projected_ref, sheet_out, sheet, blocks, arrive, leave = refs[-6:]
    fetch_blocks(number_ref, sources, blocks, arrive, LOW_GROUP)
    pltpu.make_async_copy(blocks, blocks, arrive).wait()
    lay_out_blocks(panel_ref, blocks, sheet, LOW_GROUP, 0, blocks.shape[0] // 2)
    copy = pltpu.make_async_copy(sheet, sheet_out, leave)
    copy.start()
    for panel in range(3):
        weight = sheet[panel * MODEL_WIDTH : (panel + 1) * MODEL_WIDTH, :]
        for tile in range(x_ref.shape[0] // 512):
            rows = slice(tile * 512, (tile + 1) * 512)
            value = dot(x_ref[rows, :], weight)
            if panel != 1:
                value = value + vec_ref[4 + panel // 2 : 5 + panel // 2, :]
            projected_ref[rows, panel * MODEL_WIDTH : (panel + 1) * MODEL_WIDTH] = value.astype(BF16)
    copy.wait()


def project(x, vectors, sources, numbers):
    rows = x.shape[0]
    whole = lambda shape: pl.BlockSpec(shape, lambda i, *_: (0,) * len(shape))
    anywhere = pl.BlockSpec(memory_space=pl.ANY)
    return pl.pallas_call(
        project_kernel,
        grid_spec=pltpu.PrefetchScalarGridSpec(
            num_scalar_prefetch=2,
            grid=(1,),
            in_specs=[whole(x.shape), whole(vectors.shape)] + [anywhere] * len(sources),
            out_specs=[whole((rows, 3 * MODEL_WIDTH)), anywhere],
            scratch_shapes=group_scratch(LOW_GROUP),
        ),
        out_shape=[
            jax.ShapeDtypeStruct((rows, 3 * MODEL_WIDTH), BF16),
            jax.ShapeDtypeStruct((STARTS[1] * 48, MODEL_WIDTH), BF16),
        ],
        compiler_params=pltpu.CompilerParams(vmem_limit_bytes=48 * MEBI),
        cost_estimate=cost(6 * rows * MODEL_WIDTH**2, 16 * MEBI),
        name="project_queries_keys_values",
    )(numbers, jnp.array(panel_of_block()[::2]), x, vectors, *sources)


KEY_TILE = 256


def key_tiles(labels, tile):
    edges = labels.reshape(-1, tile)
    first, last = edges[:, 0], edges[:, -1]
    start = jnp.sum(labels[None, :] < first[:, None], axis=1, dtype=jnp.int32) // KEY_TILE
    end = jnp.sum(labels[None, :] <= last[:, None], axis=1, dtype=jnp.int32)
    return start, (end + KEY_TILE - 1) // KEY_TILE - start


def over_tiles(tile, start_ref, count_ref, run):
    def block(index, carry):
        rows = pl.ds(pl.multiple_of(index * tile, tile), tile)
        start = pl.multiple_of(start_ref[index] * KEY_TILE, KEY_TILE)
        for count in range(1, ROW_POSITIONS // KEY_TILE + 1):
            keys = pl.ds(start, count * KEY_TILE)
            pl.when(count_ref[index] == count)(functools.partial(run, rows, keys))
        return carry

    lax.fori_loop(0, ROW_POSITIONS // tile, block, 0)


def attention_forward_kernel(
    tile, start_ref, count_ref, number_ref, panel_ref, row_ref, column_ref, q_ref, k_ref, v_ref, *refs
):
    sources = refs[:-8]
    out_ref, log_ref, sheet_out, vt_ref, sheet, blocks, arrive, leave = refs[-8:]
    groups = q_ref.shape[1] // LANES
    step, last = pl.program_id(0), pl.num_programs(0) - 1

    @pl.when(step == 0)
    def _():
        fetch_blocks(number_ref, sources, blocks, arrive, HIGH_GROUP)

    @pl.when(step == 1)
    def _():
        pltpu.make_async_copy(blocks, blocks, arrive).wait()
        lay_out_blocks(panel_ref, blocks, sheet, HIGH_GROUP, 0, blocks.shape[0] // 2)
        pltpu.make_async_copy(sheet, sheet_out, leave).start()

    vt_ref[...] = v_ref[...].T
    low = low_lanes(tile)

    def run(rows, keys):
        same = column_ref[keys, :] == row_ref[:, rows]
        for group in range(groups):
            lanes = slice(group * LANES, (group + 1) * LANES)
            queries = q_ref[rows, lanes] * jnp.bfloat16(HEAD_SIZE**-0.5)
            mixed = []
            for part in range(2):
                chosen = jnp.where(low if part == 0 else ~low, queries, jnp.zeros_like(queries))
                scores = dot(k_ref[keys, lanes], chosen, ((1,), (1,)))
                scores = jnp.where(same, scores, -1e30)
                peak = jnp.max(scores, axis=0, keepdims=True)
                exponents = jnp.exp(scores - peak)
                total = jnp.sum(exponents, axis=0, keepdims=True)
                probabilities = (exponents * (1.0 / total)).astype(BF16)
                first = group * LANES + part * HEAD_SIZE
                mixed.append(dot(vt_ref[first : first + HEAD_SIZE, keys], probabilities))
                log_ref[group, part : part + 1, rows] = peak + jnp.log(total)
            out_ref[rows, lanes] = jnp.concatenate(mixed, axis=0).T.astype(BF16)

    over_tiles(tile, start_ref, count_ref, run)

    @pl.when(step == last)
    def _():
        pltpu.make_async_copy(sheet, sheet_out, leave).wait()


def attention_forward(projected, tiles, label_row, label_column, sources, numbers, tile=512, groups=2):
    start, count = tiles
    width = groups * LANES
    steps = PAIRS // groups
    rows = ROW_POSITIONS
    anywhere = pl.BlockSpec(memory_space=pl.ANY)
    return pl.pallas_call(
        functools.partial(attention_forward_kernel, tile),
        grid_spec=pltpu.PrefetchScalarGridSpec(
            num_scalar_prefetch=4,
            grid=(steps,),
            in_specs=[
                pl.BlockSpec((1, rows), lambda h, *_: (0, 0)),
                pl.BlockSpec((rows, 1), lambda h, *_: (0, 0)),
                pl.BlockSpec((rows, width), lambda h, *_: (0, h)),
                pl.BlockSpec((rows, width), lambda h, *_: (0, steps + h)),
                pl.BlockSpec((rows, width), lambda h, *_: (0, 2 * steps + h)),
            ]
            + [anywhere] * len(sources),
            out_specs=[
                pl.BlockSpec((rows, width), lambda h, *_: (0, h)),
                pl.BlockSpec((groups, 8, rows), lambda h, *_: (h, 0, 0)),
                anywhere,
            ],
            scratch_shapes=[pltpu.VMEM((width, rows), BF16)] + group_scratch(HIGH_GROUP),
        ),
        out_shape=[
            jax.ShapeDtypeStruct((rows, MODEL_WIDTH), BF16),
            jax.ShapeDtypeStruct((PAIRS, 8, rows), F32),
            jax.ShapeDtypeStruct(((NBLK - STARTS[1]) * 48, MODEL_WIDTH), BF16),
        ],
        compiler_params=pltpu.CompilerParams(vmem_limit_bytes=56 * MEBI),
        cost_estimate=cost(16 * 10**9, 30 * MEBI),
        name="attention_forward",
    )(
        start,
        count,
        numbers,
        jnp.array(panel_of_block()[::2]),
        label_row,
        label_column,
        projected,
        projected,
        projected,
        *sources,
    )


def attention_backward_kernel(
    tile,
    start_ref,
    count_ref,
    row_ref,
    column_ref,
    q_ref,
    k_ref,
    v_ref,
    d_ref,
    log_ref,
    *refs,
):
    out_ref, sum_ref, kt_ref, dk_ref, dv_ref = refs[-5:]
    groups = q_ref.shape[1] // LANES
    factor = HEAD_SIZE**-0.5
    kt_ref[...] = k_ref[...].T
    dk_ref[...] = jnp.zeros_like(dk_ref)
    dv_ref[...] = jnp.zeros_like(dv_ref)
    low = low_lanes(tile)

    def run(rows, keys):
        same = column_ref[keys, :] == row_ref[:, rows]
        for group in range(groups):
            lanes = slice(group * LANES, (group + 1) * LANES)
            queries = q_ref[rows, lanes] * jnp.bfloat16(factor)
            upstream = d_ref[rows, lanes]
            d_queries = []
            d_keys = d_values = 0.0
            for part in range(2):
                mask = low if part == 0 else ~low
                chosen = jnp.where(mask, queries, jnp.zeros_like(queries))
                d_chosen = jnp.where(mask, upstream, jnp.zeros_like(upstream))
                scores = dot(k_ref[keys, lanes], chosen, ((1,), (1,)))
                exponents = jnp.exp(scores - log_ref[group, part : part + 1, rows])
                probabilities = jnp.where(same, exponents, 0.0)
                d_probs = dot(v_ref[keys, lanes], d_chosen, ((1,), (1,)))
                inner = jnp.sum(probabilities * d_probs, axis=0, keepdims=True)
                d_scores = (probabilities * (d_probs - inner)).astype(BF16)
                d_values += dot(probabilities.astype(BF16), d_chosen)
                d_keys += dot(d_scores, chosen)
                first = group * LANES + part * HEAD_SIZE
                d_queries.append(dot(kt_ref[first : first + HEAD_SIZE, keys], d_scores))
            dk_ref[keys, lanes] += d_keys
            dv_ref[keys, lanes] += d_values
            out_ref[0, rows, lanes] = (jnp.concatenate(d_queries, axis=0).T * factor).astype(BF16)

    over_tiles(tile, start_ref, count_ref, run)
    out_ref[1] = dk_ref[...].astype(BF16)
    out_ref[2] = dv_ref[...].astype(BF16)
    sum_ref[0:1, :] = jnp.sum(out_ref[0].astype(F32), axis=0, keepdims=True)
    sum_ref[1:2, :] = jnp.sum(out_ref[2].astype(F32), axis=0, keepdims=True)


def attention_backward(projected, tiles, label_row, label_column, d_attended, logs, first, others, tile=256, groups=2):
    start, count = tiles
    width = groups * LANES
    steps = PAIRS // groups
    rows = ROW_POSITIONS
    return pl.pallas_call(
        functools.partial(attention_backward_kernel, tile),
        grid_spec=pltpu.PrefetchScalarGridSpec(
            num_scalar_prefetch=2,
            grid=(1,),
            in_specs=[
                pl.BlockSpec((1, rows), lambda h, *_: (0, 0)),
                pl.BlockSpec((rows, 1), lambda h, *_: (0, 0)),
                pl.BlockSpec((rows, width), lambda h, *_: (0, first)),
                pl.BlockSpec((rows, width), lambda h, *_: (0, steps + first)),
                pl.BlockSpec((rows, width), lambda h, *_: (0, 2 * steps + first)),
                pl.BlockSpec((rows, width), lambda h, *_: (0, first)),
                pl.BlockSpec((groups, 8, rows), lambda h, *_: (first, 0, 0)),
            ]
            + [ANYWHERE] * len(others),
            out_specs=[
                pl.BlockSpec((3, rows, width), lambda h, *_: (0, 0, 0)),
                pl.BlockSpec((8, width), lambda h, *_: (0, 0)),
            ],
            scratch_shapes=[
                pltpu.VMEM((width, rows), BF16),
                pltpu.VMEM((rows, width), F32),
                pltpu.VMEM((rows, width), F32),
            ],
        ),
        out_shape=[
            jax.ShapeDtypeStruct((3, rows, width), BF16),
            jax.ShapeDtypeStruct((8, width), F32),
        ],
        compiler_params=pltpu.CompilerParams(vmem_limit_bytes=48 * MEBI),
        cost_estimate=cost(11 * 10**9, 6 * rows * MODEL_WIDTH),
        name="attention_backward",
    )(
        start,
        count,
        label_row,
        label_column,
        projected,
        projected,
        projected,
        d_attended,
        logs,
        *others,
    )


def mean(value):
    return jnp.sum(value, axis=1, keepdims=True) * (1.0 / MODEL_WIDTH)


def load_once(step, pairs, semaphores):
    copies = [pltpu.make_async_copy(source, held, semaphores.at[i]) for i, (source, held) in enumerate(pairs)]

    @pl.when(step == 0)
    def _():
        for copy in copies:
            copy.start()

    def wait(index):
        pl.when(step == 0)(copies[index].wait)

    return wait


def middle_kernel(
    attended_ref,
    x_ref,
    upstream_ref,
    vec_ref,
    sheet_ref,
    output_ref,
    normed_ref,
    activated_ref,
    d_before_ref,
    d_feed_ref,
    d_first_ref,
    d_branch_ref,
    d_attended_ref,
    sums_ref,
    out_weight,
    up_weight,
    down_weight,
    slope_ref,
    semaphores,
):
    width = MODEL_WIDTH
    step = pl.program_id(0)
    wait = load_once(
        step,
        [
            (sheet_ref.at[pl.ds(0, width), :], out_weight),
            (sheet_ref.at[pl.ds(width, FF), :], up_weight),
            (sheet_ref.at[pl.ds(width + FF, FF), :], down_weight),
        ],
        semaphores,
    )

    @pl.when(step == 0)
    def _():
        sums_ref[...] = jnp.zeros_like(sums_ref)

    def add_up(row, value):
        sums_ref[row : row + 1, :] += jnp.sum(value, axis=0, keepdims=True)

    def vector(row):
        return vec_ref[row : row + 1, :]

    wait(0)
    hidden = x_ref[...].astype(F32) + (dot(attended_ref[...], out_weight[...]) + vector(6))
    center = hidden - mean(hidden)
    first_scale = lax.rsqrt(mean(center * center) + NORM_EPSILON)
    first_normal = center * first_scale
    normed = first_normal * vector(0) + vector(1)
    normed_low = normed.astype(BF16)
    normed_ref[...] = normed_low
    wait(1)
    wait(2)
    feed_out = vector(7)
    for chunk in range(CHUNKS):
        part = slice(chunk * width, (chunk + 1) * width)
        before = dot(normed_low, up_weight[part, :]) + vector(8 + chunk)
        share = 0.5 + 0.5 * lax.erf(before * np.float32(np.sqrt(0.5)))
        density = jnp.exp(before * before * -0.5) * np.float32(1.0 / np.sqrt(2.0 * np.pi))
        slope_ref[:, part] = share + before * density
        activated = (before * share).astype(BF16)
        activated_ref[:, part] = activated
        feed_out = feed_out + dot(activated, down_weight[part, :])
    mixed = normed + feed_out
    center = mixed - mean(mixed)
    second_scale = lax.rsqrt(mean(center * center) + NORM_EPSILON)
    second_normal = center * second_scale
    output_ref[...] = (second_normal * vector(2) + vector(3)).astype(BF16)
    upstream = upstream_ref[...].astype(F32)
    add_up(2, upstream * second_normal)
    add_up(3, upstream)
    scaled = upstream * vector(2)
    d_mixed = second_scale * (scaled - mean(scaled) - second_normal * mean(scaled * second_normal))
    d_feed = d_mixed.astype(BF16)
    d_feed_ref[...] = d_feed
    add_up(7, d_feed.astype(F32))
    d_normed = d_mixed
    for chunk in range(CHUNKS):
        part = slice(chunk * width, (chunk + 1) * width)
        d_active = dot(d_feed, down_weight[part, :], ((1,), (1,)))
        d_before = (d_active * slope_ref[:, part]).astype(BF16)
        d_before_ref[:, part] = d_before
        add_up(8 + chunk, d_before.astype(F32))
        d_normed = d_normed + dot(d_before, up_weight[part, :], ((1,), (1,)))
    add_up(0, d_normed * first_normal)
    add_up(1, d_normed)
    scaled = d_normed * vector(0)
    d_first = first_scale * (scaled - mean(scaled) - first_normal * mean(scaled * first_normal))
    d_first_ref[...] = d_first
    d_branch = d_first.astype(BF16)
    d_branch_ref[...] = d_branch
    add_up(6, d_branch.astype(F32))
    d_attended_ref[...] = dot(d_branch, out_weight[...], ((1,), (1,))).astype(BF16)


def middle(attended, x, upstream, vectors, sheet, tile=256):
    rows, width = x.shape
    by_tile = lambda columns: pl.BlockSpec((tile, columns), lambda i: (i, 0))
    fixed = pl.BlockSpec((12, width), lambda i: (0, 0))
    outs = [(width, BF16), (width, BF16), (FF, BF16), (FF, BF16), (width, BF16), (width, F32)]
    outs += [(width, BF16), (width, BF16)]
    return pl.pallas_call(
        middle_kernel,
        grid=(rows // tile,),
        in_specs=[by_tile(width)] * 3 + [fixed, pl.BlockSpec(memory_space=pl.ANY)],
        out_specs=[by_tile(columns) for columns, _ in outs] + [fixed],
        out_shape=[jax.ShapeDtypeStruct((rows, columns), dtype) for columns, dtype in outs]
        + [jax.ShapeDtypeStruct((12, width), F32)],
        scratch_shapes=[
            pltpu.VMEM((width, width), BF16),
            pltpu.VMEM((FF, width), BF16),
            pltpu.VMEM((FF, width), BF16),
            pltpu.VMEM((tile, FF), F32),
            pltpu.SemaphoreType.DMA((3,)),
        ],
        compiler_params=pltpu.CompilerParams(vmem_limit_bytes=56 * MEBI),
        cost_estimate=cost(rows * width * (FF * 8 + width * 4), rows * width * 40),
        name="layer_middle",
    )(attended, x, upstream, vectors, sheet)


def store_panels(value, core, kept_ref, sent_ref):
    for own in range(2):

        @pl.when(core == own)
        def _():
            for ref, half in ((kept_ref, own), (sent_ref, 1 - own)):
                for pair in range(2):
                    for quarter in range(4):
                        first = 2 * pair * B + quarter * 48 + half * 24
                        rows = [value[first : first + 24], value[first + B : first + B + 24]]
                        ref[quarter, pair] = jnp.concatenate(rows, axis=0).astype(BF16)


def gradient_kernel(pairs, core_ref, *refs):
    kept_ref, sent_ref = refs[-2:]
    step = pl.program_id(0)
    for low, high, left, rights in pairs:

        def run(left=refs[left], rights=[refs[right] for right in rights]):
            if len(rights) == 1:
                right = rights[0][...]
            else:
                right = jnp.concatenate([part[0] for part in rights], axis=1)
            store_panels(dot(left[...], right, ((0,), (0,))), core_ref[0], kept_ref, sent_ref)

        if low == 0 and high == CHUNKS:
            run()
        else:
            pl.when((step >= low) & (step < high))(run)


def gradient_call(pairs, specs, values, name, others=()):
    core = (lax.axis_index("seq") % 2).reshape(1).astype(jnp.int32)
    shape = jax.ShapeDtypeStruct((4, 2 * CHUNKS, 48, MODEL_WIDTH), BF16)
    spec = pl.BlockSpec((4, 2, 48, MODEL_WIDTH), lambda i, *_: (0, i, 0, 0))
    return pl.pallas_call(
        functools.partial(gradient_kernel, pairs),
        grid_spec=pltpu.PrefetchScalarGridSpec(
            num_scalar_prefetch=1,
            grid=(CHUNKS,),
            in_specs=specs + [ANYWHERE] * len(others),
            out_specs=[spec, spec],
        ),
        out_shape=[shape, shape],
        compiler_params=pltpu.CompilerParams(vmem_limit_bytes=48 * MEBI),
        cost_estimate=cost(2 * ROW_POSITIONS * CHUNKS * MODEL_WIDTH**2, 16 * MEBI),
        name=name,
    )(core, *values, *others)


FIXED_ROWS = pl.BlockSpec((ROW_POSITIONS, MODEL_WIDTH), lambda i, *_: (0, 0))
MOVING_ROWS = pl.BlockSpec((ROW_POSITIONS, MODEL_WIDTH), lambda i, *_: (0, i))


def down_gradient(activated, d_feed):
    pairs = [(0, CHUNKS, 0, [1])]
    return gradient_call(pairs, [MOVING_ROWS, FIXED_ROWS], (activated, d_feed), "down_gradient")


def up_gradient(normed_low, d_before, others):
    pairs = [(0, CHUNKS, 0, [1])]
    values = (normed_low, d_before)
    return gradient_call(pairs, [FIXED_ROWS, MOVING_ROWS], values, "up_gradient", others)


def attention_gradients(x, attended, d_branch, d_projected, others):
    count = len(d_projected)
    pairs = [(0, 3, 0, list(range(3, 3 + count))), (3, 4, 1, [2])]
    third = lambda part: pl.BlockSpec(
        (1,) + part.shape[1:], lambda i, *_: (jnp.minimum(i, 2), 0, 0)
    )
    return gradient_call(
        pairs,
        [FIXED_ROWS] * 3 + [third(part) for part in d_projected],
        (x, attended, d_branch) + tuple(d_projected),
        "attention_gradients",
        others,
    )


def input_gradient_kernel(count, sheet_ref, d_first_ref, output_ref, *refs):
    parts, out_ref = refs[:count], refs[-1]
    value = d_first_ref[...]
    for third in range(3):
        weight = sheet_ref[third * MODEL_WIDTH : (third + 1) * MODEL_WIDTH, :]
        d_rows = jnp.concatenate([part[third] for part in parts], axis=1)
        value = value + dot(d_rows, weight, ((1,), (1,)))
    out_ref[:, :MODEL_WIDTH] = output_ref[...]
    out_ref[:, MODEL_WIDTH:] = value.astype(BF16)


def input_gradient(d_projected, sheet, d_first, output, others, tile=512):
    rows = d_first.shape[0]
    by_tile = lambda width: pl.BlockSpec((tile, width), lambda i: (i, 0))
    return pl.pallas_call(
        functools.partial(input_gradient_kernel, len(d_projected)),
        grid=(rows // tile,),
        in_specs=[
            pl.BlockSpec((3 * MODEL_WIDTH, MODEL_WIDTH), lambda i: (0, 0), pipeline_mode=pl.Buffered(1)),
            by_tile(MODEL_WIDTH),
            by_tile(MODEL_WIDTH),
        ]
        + [pl.BlockSpec((3, tile, part.shape[2]), lambda i: (0, i, 0)) for part in d_projected]
        + [ANYWHERE] * len(others),
        out_specs=by_tile(2 * MODEL_WIDTH),
        out_shape=jax.ShapeDtypeStruct((rows, 2 * MODEL_WIDTH), BF16),
        compiler_params=pltpu.CompilerParams(vmem_limit_bytes=48 * MEBI),
        cost_estimate=cost(6 * rows * MODEL_WIDTH**2, 14 * MEBI),
        name="input_gradient",
    )(sheet, d_first, output, *d_projected, *others)


def add_parts(*parts):
    return functools.reduce(jnp.add, [part.astype(F32) for part in parts]).astype(BF16)


def pick(value, index, axis=0):
    return lax.dynamic_index_in_dim(value, index, axis, keepdims=False)


def head_first_parts(kept):
    head = lax.axis_index("head")
    x, y = head % 2, head // 2
    cut = kept.shape[1] // 2
    square = kept.reshape((2, 2) + kept.shape[1:])
    first, second = square[:, :, :cut], square[:, :, cut:]
    sent = pick(first, 1 - x, 1), pick(second, 1 - y, 0)
    return sent, (pick(first, x, 1), pick(second, y, 0))


def head_first_send(sent):
    return permute_xor(sent[0], "head", 1), permute_xor(sent[1], "head", 2)


def head_second_parts(first, second):
    head = lax.axis_index("head")
    x, y = head % 2, head // 2
    sent = pick(first, 1 - y), pick(second, 1 - x)
    return sent, (pick(first, y), pick(second, x))


def head_second_send(sent):
    return permute_xor(sent[0], "head", 2), permute_xor(sent[1], "head", 1)


def add_pairs(kept, arrived):
    return [add_parts(one, two) for one, two in zip(kept, arrived)]


TOGETHER = 4
BUNDLE = TOGETHER * 36


def owned_kernel(panel_ref, lane_ref, odd_ref, sheet_ref, carried_ref, out_ref, carried_out):
    del carried_ref, carried_out
    first = pl.program_id(0) * out_ref.shape[0] * TOGETHER
    half = low_lanes(24)

    def bundle(place, carry):
        mains, rests = [], []
        for index in range(TOGETHER):
            slot = first + place * TOGETHER + index
            panel, odd = panel_ref[slot], odd_ref[slot] == 1
            pair = panel // 2
            lane = pl.multiple_of(lane_ref[slot], LANES)
            main_lane = pl.multiple_of(lane + jnp.where(odd, 2 * LANES, 0), LANES)
            values = []
            for begin in (main_lane, pl.multiple_of(lane + LANES, LANES)):
                value = sheet_ref[pair, :, pl.ds(begin, LANES)].astype(F32)
                values.append(jnp.where(panel % 2 == 1, value[24:], value[:24]))
            mains.append(values[0])
            turn = odd if index % 2 == 0 else jnp.logical_not(odd)
            rests.append(jnp.where(turn, pltpu.roll(values[1], LANES // 2, 1), values[1]))
        rests = [jnp.where(half, rests[i], rests[i + 1]) for i in range(0, TOGETHER, 2)]
        out_ref[place] = jnp.concatenate(mains + rests, axis=0).astype(BF16)
        return carry

    lax.fori_loop(0, out_ref.shape[0], bundle, 0)


def by_owner(sheet_gradient, owner_order, carried):
    owners = lax.axis_size("seq")
    count = NBLK // owners
    bundles = -(-count // TOGETHER)
    slots = jnp.pad(owner_order.reshape(owners, count), ((0, 0), (0, bundles * TOGETHER - count)))
    slots = slots.reshape(-1)
    steps = 4 if owners * bundles % 4 == 0 else 1
    each = owners * bundles // steps
    panels = jnp.asarray(panel_of_block())
    whole = jnp.arange(NBLK, dtype=jnp.int32)
    panels = jnp.sum(jnp.where(slots[:, None] == whole[None, :], panels[None, :], 0), axis=1)
    gathered, carried = pl.pallas_call(
        owned_kernel,
        grid_spec=pltpu.PrefetchScalarGridSpec(
            num_scalar_prefetch=3,
            grid=(steps,),
            in_specs=[pl.BlockSpec(sheet_gradient.shape, lambda i, *_: (0, 0, 0)), ANYWHERE],
            out_specs=[pl.BlockSpec((each, BUNDLE, LANES), lambda i, *_: (i, 0, 0)), ANYWHERE],
        ),
        out_shape=[
            jax.ShapeDtypeStruct((owners * bundles, BUNDLE, LANES), BF16),
            jax.ShapeDtypeStruct(carried.shape, carried.dtype),
        ],
        input_output_aliases={4: 1},
        compiler_params=pltpu.CompilerParams(vmem_limit_bytes=24 * MEBI),
        cost_estimate=cost(0, 4 * MEBI),
        name="gradients_by_owner",
    )(panels, slots // 2 % 2 * 384, slots % 2, sheet_gradient, carried)
    return gathered.reshape(owners // 2, 2, bundles, BUNDLE, LANES), carried


def add_tree(terms):
    while len(terms) > 1:
        terms = [one + two for one, two in zip(terms[::2], terms[1::2])]
    return terms[0]


def two_parts(value):
    high = lax.reduce_precision(value, 8, 7)
    return high, lax.reduce_precision(value - high, 8, 7)


def sum_to_owners(parts, sums):
    chips = lax.axis_size("seq") // 2
    seq = lax.axis_index("seq")
    chip, core = seq // 2, seq % 2
    shape = parts.shape[2:]
    flat = lambda value: value.reshape((-1,) + shape[1:])

    def with_sums(value, total):
        high, low = two_parts(total)
        both = jnp.concatenate([high, low]).astype(BF16)
        return jnp.concatenate([flat(value), flat(both)])

    def split_sums(value):
        high, low = value[-1].astype(F32).reshape((2,) + sums.shape)
        return value[:-1], high + low

    packed = flat if sums is None else functools.partial(with_sums, total=sums)
    arrived = [packed(pick(parts, chip))]
    for mask in range(1, chips):
        arrived.append(permute_xor(packed(pick(parts, chip ^ mask)), "seq", 2 * mask))
    if sums is not None:
        split = [split_sums(value) for value in arrived]
        arrived = [value for value, _ in split]
        sums = add_tree([total for _, total in split])
    mine = add_parts(*arrived).reshape((2,) + shape)
    packed = flat if sums is None else functools.partial(with_sums, total=sums)
    other = permute_xor(packed(pick(mine, 1 - core)), "seq", 1)
    if sums is not None:
        other, total = split_sums(other)
        high, low = two_parts(sums)
        sums = (high + low) + total
    return jnp.stack([pick(mine, core), other.reshape(shape)]), sums


def shampoo_kernel(
    base,
    held,
    number_ref,
    place_ref,
    part0,
    part1,
    part2,
    part3,
    momentum_ref,
    left_ref,
    right_ref,
    root_left_ref,
    root_right_ref,
    master_ref,
    *refs,
):
    new_momentum_ref, new_left_ref, new_right_ref, new_master_ref, main_ref, rest_ref = refs[held:]
    count = momentum_ref.shape[0]
    first = (base + pl.program_id(0)) * count
    low = low_lanes(B)
    half = low_lanes(24)
    core = place_ref[4]
    for slot in range(count):
        odd = number_ref[first + slot] % 2 == 1
        for index, part in enumerate((part0, part1, part2, part3)):
            for which in range(2):
                row = pl.multiple_of(place_ref[index] * 48 + (which ^ core) * 24, 8)
                bundle = part[which, slot // TOGETHER].astype(F32)
                inside = slot % TOGETHER
                main_ref[pl.ds(row, 24), :] = bundle[inside * 24 : inside * 24 + 24]
                begin = TOGETHER * 24 + inside // 2 * 24
                rest_ref[pl.ds(row, 24), :] = bundle[begin : begin + 24]
        main = main_ref[...]
        rest = rest_ref[...]
        spun = pltpu.roll(main, LANES // 2, 1)
        rest_low = rest if slot % 2 == 0 else pltpu.roll(rest, LANES // 2, 1)
        left_lanes = jnp.where(odd, jnp.where(low, rest_low, spun), main)
        right_lanes = jnp.where(odd, spun, rest_low)
        gradient = jnp.concatenate([left_lanes, right_lanes[:, : LANES // 2]], axis=1)
        new_momentum = MOMENTUM_DECAY * momentum_ref[slot] + (1.0 - MOMENTUM_DECAY) * gradient
        new_momentum_ref[slot] = new_momentum
        grad_low = gradient.astype(BF16)
        new_left_ref[slot] = STAT_DECAY * left_ref[slot] + (1.0 - STAT_DECAY) * dot(
            grad_low, grad_low, ((1,), (1,))
        )
        new_right_ref[slot] = STAT_DECAY * right_ref[slot] + (1.0 - STAT_DECAY) * dot(
            grad_low, grad_low, ((0,), (0,))
        )
        leftward = dot(root_left_ref[slot].astype(BF16), new_momentum.astype(BF16))
        preconditioned = dot(leftward.astype(BF16), root_right_ref[slot].astype(BF16))
        master = master_ref[slot]
        new_master_ref[slot] = master - MATRIX_RATE * (preconditioned + WEIGHT_DECAY * master)


def shampoo(numbers, parts, states, first, earlier, others):
    group = TOGETHER if numbers.shape[0] % TOGETHER == 0 else numbers.shape[0]
    steps = parts[0].shape[1]
    base = first // group
    spec = pl.BlockSpec((group, B, B), lambda i, *_: (base + i, 0, 0))
    part_spec = pl.BlockSpec((2, 1, BUNDLE, LANES), lambda i, *_: (0, i, 0, 0))
    places = lax.axis_index("head") ^ jnp.arange(4, dtype=jnp.int32)
    places = jnp.concatenate([places, (lax.axis_index("seq") % 2).reshape(1).astype(jnp.int32)])
    return pl.pallas_call(
        functools.partial(shampoo_kernel, base, len(earlier) + len(others)),
        grid_spec=pltpu.PrefetchScalarGridSpec(
            num_scalar_prefetch=2,
            grid=(steps,),
            in_specs=[part_spec] * 4
            + [spec] * 6
            + [ANYWHERE] * (len(earlier) + len(others)),
            out_specs=[spec] * 4,
            scratch_shapes=[pltpu.VMEM((B, LANES), F32), pltpu.VMEM((B, LANES), F32)],
        ),
        out_shape=[jax.ShapeDtypeStruct((numbers.shape[0], B, B), F32)] * 4,
        input_output_aliases={12 + i: i for i in range(len(earlier))},
        compiler_params=pltpu.CompilerParams(vmem_limit_bytes=48 * MEBI),
        cost_estimate=cost(8 * steps * group * B**3, 10 * steps * group * B * B * 4),
        name="shampoo_blocks",
    )(numbers, places, *parts, *states, *earlier, *others)


def adam_step(vector_grad, vec_first, vec_second, vectors):
    new_first = FIRST_DECAY * vec_first + (1.0 - FIRST_DECAY) * vector_grad
    new_second = SECOND_DECAY * vec_second + (1.0 - SECOND_DECAY) * vector_grad * vector_grad
    corrected_first = new_first / (1.0 - FIRST_DECAY**STEP)
    corrected_second = new_second / (1.0 - SECOND_DECAY**STEP)
    new_vectors = vectors - VECTOR_RATE * corrected_first / (
        jnp.sqrt(corrected_second) + ADAM_EPSILON
    )
    return (new_first, new_second, new_vectors)


def exchange_rows(value):
    return lax.all_to_all(value, "head", split_axis=0, concat_axis=0, tiled=True)


def local(
    tokens,
    cotangent,
    segment_ids,
    owner_order,
    master_blocks,
    momentum,
    stat_left,
    stat_right,
    root_left,
    root_right,
    vectors,
    vec_first,
    vec_second,
):
    width = MODEL_WIDTH
    count = master_blocks.shape[0]
    head = lax.axis_index("head")
    numbers = lax.dynamic_slice_in_dim(owner_order, lax.axis_index("seq") * count, count, 0)
    sheet_vectors = vectors.reshape(12, width)

    labels = lax.dynamic_index_in_dim(segment_ids, head, 0, keepdims=False)
    early = [sheet_vectors, labels.reshape(1, -1), labels.reshape(-1, 1)]
    early += [*key_tiles(labels, 512), *key_tiles(labels, KEY_TILE)]
    early += [exchange_rows(tokens).reshape(ROW_POSITIONS, width)]
    packed = pack_blocks(numbers, master_blocks)
    blocks, source_numbers, early = gather_weights(packed, owner_order, early)
    sheet_vectors, label_row, label_column = early[:3]
    wide_tiles, tiles, x = early[3:5], early[5:7], early[7]
    upstream = exchange_rows(cotangent).reshape(ROW_POSITIONS, width)

    projected, input_sheet = project(x, sheet_vectors, blocks, source_numbers)
    attended, logs, sheet = attention_forward(
        projected, wide_tiles, label_row, label_column, blocks, source_numbers
    )
    (
        output,
        normed_low,
        activated,
        d_before,
        d_feed,
        d_first,
        d_branch,
        d_attended,
        sums,
    ) = middle(attended, x, upstream, sheet_vectors, sheet)
    def backward(index, *others):
        return attention_backward(
            projected, tiles, label_row, label_column, d_attended, logs, index, others
        )

    down, down_sent = down_gradient(activated, d_feed)
    up, up_sent = up_gradient(normed_low, d_before, [down])
    down_sent = permute_xor(down_sent, "seq", 1)
    down = add_parts(down, down_sent)
    down_sent, down = head_first_parts(down)
    parts = [backward(0, up, *down_sent)]
    down_sent = head_first_send(down_sent)
    up_sent = permute_xor(up_sent, "seq", 1)
    down = add_pairs(down, down_sent)
    up = add_parts(up, up_sent)
    down_sent, down = head_second_parts(*down)
    parts.append(backward(1, parts[0][0], *down_sent))
    down_sent = head_second_send(down_sent)
    down = jnp.concatenate(add_pairs(down, down_sent))
    up_sent, up = head_first_parts(up)
    parts.append(backward(2, parts[1][0], *up_sent))
    up_sent = head_first_send(up_sent)
    up = add_pairs(up, up_sent)
    up_sent, up = head_second_parts(*up)
    d_projected = [part[0] for part in parts]
    rest, rest_sent = attention_gradients(x, attended, d_branch, d_projected, up_sent)
    up_sent = head_second_send(up_sent)
    up = jnp.concatenate(add_pairs(up, up_sent))
    rest = add_parts(rest, permute_xor(rest_sent, "seq", 1))
    rest_sent, rest = head_first_parts(rest)
    bias_sums = jnp.concatenate([part[1] for part in parts], axis=1)
    sums = jnp.concatenate([sums[:4], bias_sums[:2], sums[6:]])
    both = input_gradient(d_projected, input_sheet, d_first, output, rest_sent)
    rest_sent = head_first_send(rest_sent)
    sums_sent = [permute_xor(sums, "head", mask) for mask in (1, 2, 3)]
    sums = add_tree([sums, *sums_sent])
    rest = add_pairs(rest, rest_sent)
    rest_sent, rest = head_second_parts(*rest)
    rest = jnp.concatenate(add_pairs(rest, head_second_send(rest_sent)))
    owned, both = by_owner(jnp.concatenate([rest, up, down]), owner_order, both)
    both = exchange_rows(both.reshape(tokens.shape[:2] + (2 * width,)))
    output, input_grad = both[:, :, :width], both[:, :, width:].astype(F32)
    bundles = owned.shape[2]
    halves = 2 if bundles % 2 == 0 else 1
    each = bundles // halves
    states = (momentum, stat_left, stat_right, root_left, root_right, master_blocks)
    blocks = ()
    for half in range(halves):
        part, total = sum_to_owners(
            owned[:, :, half * each : (half + 1) * each], sums if half == halves - 1 else None
        )
        quarters = [part] + [permute_xor(part, "head", mask) for mask in (1, 2, 3)]
        others = [output, input_grad] if half == halves - 1 else []
        blocks = shampoo(numbers, quarters, states, half * each * TOGETHER, blocks, others)
    new_first, new_second, new_vectors = adam_step(total.reshape(-1), vec_first, vec_second, vectors)

    new_momentum, new_left, new_right, new_master = blocks
    return (
        output,
        input_grad,
        new_momentum,
        new_left,
        new_right,
        new_master,
        new_first,
        new_second,
        new_vectors,
    )


def solution(mesh):
    blocks = P("seq", None, None)
    positions = P("seq", "head", None)
    return jax.shard_map(
        local,
        mesh=mesh,
        in_specs=(positions, positions, P("seq", None), P()) + (blocks,) * 6 + (P(),) * 3,
        out_specs=(positions, positions) + (blocks,) * 4 + (P(),) * 3,
        check_vma=False,
    )
```

```python
import functools

import jax
import jax.numpy as jnp
import numpy as np
from jax import lax
from jax.experimental import pallas as pl
from jax.experimental.pallas import tpu as pltpu
from jax.sharding import PartitionSpec as P

MODEL_WIDTH = 768
HEAD_TOTAL = 12
HEAD_SIZE = 64
FF = 3072
ROW_POSITIONS = 1024
B = 192
STEP = 10
NBLK = 192
PAIRS = HEAD_TOTAL // 2
LANES = 128
REST = B * B // LANES
QUARTER = REST // 4
CHUNKS = FF // MODEL_WIDTH
MEBI = 2**20

NORM_EPSILON = 1e-05
STAT_DECAY = 0.5
MOMENTUM_DECAY = 0.5
MATRIX_RATE = 1.0
WEIGHT_DECAY = 0.01
FIRST_DECAY = 0.9
SECOND_DECAY = 0.999
VECTOR_RATE = 0.3
ADAM_EPSILON = 1e-08

F32 = jnp.float32
BF16 = jnp.bfloat16
STARTS = (0, 48, 64, 128, 192)


def panel_of_block():
    panels = []
    for block in range(NBLK):
        if block < STARTS[1]:
            panels.append((block % 12) // 4 * 4 + block // 12)
        elif block < STARTS[2]:
            panels.append(12 + (block - STARTS[1]) // 4)
        elif block < STARTS[3]:
            inner = block - STARTS[2]
            panels.append(16 + (inner % 16) // 4 * 4 + inner // 16)
        else:
            panels.append(32 + (block - STARTS[3]) // 4)
    return np.array(panels, np.int32)


def cost(flops, moved, transcendentals=0):
    return pl.CostEstimate(flops=flops, bytes_accessed=moved, transcendentals=transcendentals)


def dot(left, right, contract=((1,), (0,))):
    return lax.dot_general(left, right, (contract, ((), ())), preferred_element_type=F32)


def low_lanes(rows):
    return lax.broadcasted_iota(jnp.int32, (rows, LANES), 1) < LANES // 2


def pack_kernel(order_ref, blocks_ref, packed_ref):
    count = blocks_ref.shape[0]
    first = pl.program_id(0) * count
    half = low_lanes(B // 2)
    low = low_lanes(B)
    for slot in range(count):
        left = blocks_ref[slot, :, :LANES]
        narrow = blocks_ref[slot, :, LANES:]
        right = jnp.concatenate([narrow, narrow], axis=1)
        turned = pltpu.roll(left, LANES // 2, 1)
        odd = order_ref[first + slot] % 2 == 1
        main = jnp.where(odd, jnp.where(low, turned, right), left)
        even_rest = jnp.where(half, right[: B // 2], right[B // 2 :])
        odd_rest = jnp.where(half, left[B // 2 :], turned[: B // 2])
        packed_ref[slot, :B, :] = main.astype(BF16)
        packed_ref[slot, B:, :] = jnp.where(odd, odd_rest, even_rest).astype(BF16)


def pack_blocks(order, blocks):
    count = blocks.shape[0]
    group = max(size for size in range(1, 7) if count % size == 0)
    return pl.pallas_call(
        pack_kernel,
        grid_spec=pltpu.PrefetchScalarGridSpec(
            num_scalar_prefetch=1,
            grid=(count // group,),
            in_specs=[pl.BlockSpec((group, B, B), lambda i, *_: (i, 0, 0))],
            out_specs=pl.BlockSpec((group, REST, LANES), lambda i, *_: (i, 0, 0)),
        ),
        out_shape=jax.ShapeDtypeStruct((count, REST, LANES), BF16),
        cost_estimate=cost(0, count * B * B * 6),
        name="pack_weight_blocks",
    )(order, blocks)


def permute_xor(value, axis, mask):
    size = lax.axis_size(axis)
    return lax.ppermute(value, axis, [(i, i ^ mask) for i in range(size)])


def gate_kernel(*refs):
    del refs


def gate(values, others):
    flat = list(values)
    shapes = [jax.ShapeDtypeStruct(value.shape, value.dtype) for value in flat]
    return pl.pallas_call(
        gate_kernel,
        in_specs=[ANYWHERE] * (len(flat) + len(others)),
        out_specs=[ANYWHERE] * len(flat),
        out_shape=shapes,
        input_output_aliases={i: i for i in range(len(flat))},
        cost_estimate=cost(0, 0),
        name="gate",
    )(*flat, *others)


ANYWHERE = pl.BlockSpec(memory_space=pl.ANY)


def gathered_slots(heads, chips, count):
    size, cut = count // heads, count // heads // 2
    slots = np.zeros((heads, chips, 2, NBLK), np.int32)
    for head in range(heads):
        for chip in range(chips):
            places = [(chip, slot) for slot in range(count)]
            for kinds in GROUP_KINDS:
                for mask in range(heads):
                    for chip_mask, half in kinds:
                        begin = (head ^ mask) * size + half * cut
                        places += [(chip ^ chip_mask, begin + slot) for slot in range(cut)]
            for core in range(2):
                slots[head, chip, core] = [
                    (c * 2 + which) * count + slot for which in (core, 1 - core) for c, slot in places
                ]
    return slots


GROUP_KINDS = (((1, 0), (1, 1)), ((2, 0), (3, 0)), ((2, 1), (3, 1)))


def gather_weights(packed, owner_order, early):
    heads = lax.axis_size("head")
    chips = lax.axis_size("seq") // 2
    count = packed.shape[0]
    head = lax.axis_index("head")
    seq = lax.axis_index("seq")
    chip, core = seq // 2, seq % 2
    if count % (2 * heads) or chips != 4:
        return [lax.all_gather(packed, "seq", axis=0, tiled=True)], owner_order, early
    size = count // heads
    cut = size // 2
    slots = jnp.asarray(gathered_slots(heads, chips, count).reshape(-1, NBLK))
    slots = lax.dynamic_index_in_dim(slots, (head * chips + chip) * 2 + core, 0, keepdims=False)
    whole = jnp.arange(NBLK, dtype=jnp.int32)
    numbers = jnp.sum(jnp.where(slots[:, None] == whole[None, :], owner_order[None, :], 0), axis=1)
    own = lax.dynamic_slice_in_dim(packed, head * size, size, 0)
    halves = own[:cut], own[cut:]
    over_z = lambda half, mask: permute_xor(half, "seq", 2 * mask)
    def first_hop(first, second):
        return [
            permute_xor(first, "head", 1),
            permute_xor(second, "head", 2),
            permute_xor(second, "head", 1),
            permute_xor(first, "head", 2),
        ]

    def second_hop(first_x, second_y, *_):
        return [permute_xor(first_x, "head", 2), permute_xor(second_y, "head", 1)]

    def swap_cores(pieces):
        return [permute_xor(piece, "seq", 1) for piece in pieces]

    def arranged(pieces, one, two):
        first_x, second_y, second_x, first_y = one
        return [*pieces, first_x, second_x, first_y, second_y, *two]

    near = [over_z(half, 1) for half in halves]
    halfway = [over_z(halves[0], 2), over_z(halves[0], 3)]
    swapped = swap_cores([packed])
    *near, late = gate([*near, halves[1]], [*swapped, numbers, *early[:-1]])
    near_one = first_hop(*near)
    last = [over_z(late, 2), over_z(late, 3)]
    gated = gate([*near_one[:2], *halfway], near_one[2:])
    near_one[:2], halfway = gated[:2], gated[2:]
    near_two = second_hop(*near_one)
    halfway_one = first_hop(*halfway)
    gated = gate([*halfway_one[:2], *last], [*halfway_one[2:], *near_two, early[-1]])
    halfway_one[:2], last = gated[:2], gated[2:]
    halfway_two = second_hop(*halfway_one)
    last_one = first_hop(*last)
    last_one[:2] = gate(last_one[:2], [*last_one[2:], *halfway_two])
    last_two = second_hop(*last_one)
    mine = [
        jnp.concatenate(arranged(near, near_one, near_two)),
        jnp.concatenate(arranged(halfway, halfway_one, halfway_two)),
        jnp.concatenate(arranged(last, last_one, ())),
        *last_two,
    ]
    return [packed, *mine, *swapped, *swap_cores(mine)], numbers, early


LOW_GROUP = (STARTS[0], STARTS[1])
HIGH_GROUP = (STARTS[1], STARTS[4])


def fetch_blocks(number_ref, sources, blocks, arrive, group):
    low, high = group
    first = 0
    for source in sources:

        def start(place, carry, source=source, first=first):
            number = number_ref[first + place]

            @pl.when((number >= low) & (number < high))
            def _():
                pltpu.make_async_copy(source.at[place], blocks.at[number - low], arrive).start()

            return carry

        count = source.shape[0]
        lax.fori_loop(0, count, start, 0, unroll=min(count, 4))
        first += count


def lay_out_blocks(panel_ref, blocks, sheet, group, begin, end):
    low = group[0]
    half = low_lanes(B // 2)

    def lay_out(index, carry):
        pair = low // 2 + index
        row = pl.multiple_of((panel_ref[pair] - low // 4) * B, B)
        lane = pl.multiple_of((pair % 2) * 384, LANES)
        even, odd = 2 * index, 2 * index + 1
        sheet[pl.ds(row, B), pl.ds(lane, LANES)] = blocks[even, :B, :]
        sheet[pl.ds(row, B), pl.ds(lane + 2 * LANES, LANES)] = blocks[odd, :B, :]
        even_rest = blocks[even, B:, :].astype(F32)
        odd_rest = blocks[odd, B:, :].astype(F32)
        turned = pltpu.roll(jnp.where(half, odd_rest, even_rest), LANES // 2, 1)
        center = jnp.concatenate([jnp.where(half, even_rest, odd_rest), turned], axis=0)
        sheet[pl.ds(row, B), pl.ds(lane + LANES, LANES)] = center.astype(BF16)
        return carry

    lax.fori_loop(begin, end, lay_out, 0, unroll=4)


def group_scratch(group):
    count = group[1] - group[0]
    return [
        pltpu.VMEM((count * 48, MODEL_WIDTH), BF16),
        pltpu.VMEM((count, REST, LANES), BF16),
        pltpu.SemaphoreType.DMA,
        pltpu.SemaphoreType.DMA,
    ]


def project_kernel(
    number_ref, panel_ref, x_ref, vec_ref, *refs
):
    sources = refs[:-6]
    projected_ref, sheet_out, sheet, blocks, arrive, leave = refs[-6:]
    fetch_blocks(number_ref, sources, blocks, arrive, LOW_GROUP)
    pltpu.make_async_copy(blocks, blocks, arrive).wait()
    lay_out_blocks(panel_ref, blocks, sheet, LOW_GROUP, 0, blocks.shape[0] // 2)
    copy = pltpu.make_async_copy(sheet, sheet_out, leave)
    copy.start()
    for panel in range(3):
        weight = sheet[panel * MODEL_WIDTH : (panel + 1) * MODEL_WIDTH, :]
        for tile in range(x_ref.shape[0] // 512):
            rows = slice(tile * 512, (tile + 1) * 512)
            value = dot(x_ref[rows, :], weight)
            if panel != 1:
                value = value + vec_ref[4 + panel // 2 : 5 + panel // 2, :]
            projected_ref[rows, panel * MODEL_WIDTH : (panel + 1) * MODEL_WIDTH] = value.astype(BF16)
    copy.wait()


def project(x, vectors, sources, numbers):
    rows = x.shape[0]
    whole = lambda shape: pl.BlockSpec(shape, lambda i, *_: (0,) * len(shape))
    anywhere = pl.BlockSpec(memory_space=pl.ANY)
    return pl.pallas_call(
        project_kernel,
        grid_spec=pltpu.PrefetchScalarGridSpec(
            num_scalar_prefetch=2,
            grid=(1,),
            in_specs=[whole(x.shape), whole(vectors.shape)] + [anywhere] * len(sources),
            out_specs=[whole((rows, 3 * MODEL_WIDTH)), anywhere],
            scratch_shapes=group_scratch(LOW_GROUP),
        ),
        out_shape=[
            jax.ShapeDtypeStruct((rows, 3 * MODEL_WIDTH), BF16),
            jax.ShapeDtypeStruct((STARTS[1] * 48, MODEL_WIDTH), BF16),
        ],
        compiler_params=pltpu.CompilerParams(vmem_limit_bytes=48 * MEBI),
        cost_estimate=cost(6 * rows * MODEL_WIDTH**2, 16 * MEBI),
        name="project_queries_keys_values",
    )(numbers, jnp.array(panel_of_block()[::2]), x, vectors, *sources)


FORWARD_TILES = (512, 256)
BACKWARD_TILES = (256, 128)


def key_tiles(labels, tile, key_tile):
    edges = labels.reshape(-1, tile)
    first, last = edges[:, 0], edges[:, -1]
    start = jnp.sum(labels[None, :] < first[:, None], axis=1, dtype=jnp.int32) // key_tile
    end = jnp.sum(labels[None, :] <= last[:, None], axis=1, dtype=jnp.int32)
    return start, (end + key_tile - 1) // key_tile - start


def over_tiles(tile, key_tile, start_ref, count_ref, run):
    def block(index, carry):
        rows = pl.ds(pl.multiple_of(index * tile, tile), tile)
        start = pl.multiple_of(start_ref[index] * key_tile, key_tile)
        for count in range(1, ROW_POSITIONS // key_tile + 1):
            keys = pl.ds(start, count * key_tile)
            pl.when(count_ref[index] == count)(functools.partial(run, rows, keys))
        return carry

    lax.fori_loop(0, ROW_POSITIONS // tile, block, 0)


def attention_forward_kernel(
    tile, key_tile, start_ref, count_ref, number_ref, panel_ref, row_ref, column_ref, q_ref, k_ref, v_ref, *refs
):
    sources = refs[:-8]
    out_ref, log_ref, sheet_out, vt_ref, sheet, blocks, arrive, leave = refs[-8:]
    groups = q_ref.shape[1] // LANES
    step, last = pl.program_id(0), pl.num_programs(0) - 1

    @pl.when(step == 0)
    def _():
        fetch_blocks(number_ref, sources, blocks, arrive, HIGH_GROUP)

    @pl.when(step == 1)
    def _():
        pltpu.make_async_copy(blocks, blocks, arrive).wait()
        lay_out_blocks(panel_ref, blocks, sheet, HIGH_GROUP, 0, blocks.shape[0] // 2)
        pltpu.make_async_copy(sheet, sheet_out, leave).start()

    vt_ref[...] = v_ref[...].T
    low = low_lanes(tile)

    def run(rows, keys):
        same = column_ref[keys, :] == row_ref[:, rows]
        for group in range(groups):
            lanes = slice(group * LANES, (group + 1) * LANES)
            queries = q_ref[rows, lanes] * jnp.bfloat16(HEAD_SIZE**-0.5)
            mixed = []
            for part in range(2):
                chosen = jnp.where(low if part == 0 else ~low, queries, jnp.zeros_like(queries))
                scores = dot(k_ref[keys, lanes], chosen, ((1,), (1,)))
                scores = jnp.where(same, scores, -1e30)
                peak = jnp.max(scores, axis=0, keepdims=True)
                exponents = jnp.exp(scores - peak)
                total = jnp.sum(exponents, axis=0, keepdims=True)
                probabilities = (exponents * (1.0 / total)).astype(BF16)
                first = group * LANES + part * HEAD_SIZE
                mixed.append(dot(vt_ref[first : first + HEAD_SIZE, keys], probabilities))
                log_ref[group, part : part + 1, rows] = peak + jnp.log(total)
            out_ref[rows, lanes] = jnp.concatenate(mixed, axis=0).T.astype(BF16)

    over_tiles(tile, key_tile, start_ref, count_ref, run)

    @pl.when(step == last)
    def _():
        pltpu.make_async_copy(sheet, sheet_out, leave).wait()


def attention_forward(projected, tiles, label_row, label_column, sources, numbers, groups=2):
    start, count = tiles
    width = groups * LANES
    steps = PAIRS // groups
    rows = ROW_POSITIONS
    anywhere = pl.BlockSpec(memory_space=pl.ANY)
    return pl.pallas_call(
        functools.partial(attention_forward_kernel, *FORWARD_TILES),
        grid_spec=pltpu.PrefetchScalarGridSpec(
            num_scalar_prefetch=4,
            grid=(steps,),
            in_specs=[
                pl.BlockSpec((1, rows), lambda h, *_: (0, 0)),
                pl.BlockSpec((rows, 1), lambda h, *_: (0, 0)),
                pl.BlockSpec((rows, width), lambda h, *_: (0, h)),
                pl.BlockSpec((rows, width), lambda h, *_: (0, steps + h)),
                pl.BlockSpec((rows, width), lambda h, *_: (0, 2 * steps + h)),
            ]
            + [anywhere] * len(sources),
            out_specs=[
                pl.BlockSpec((rows, width), lambda h, *_: (0, h)),
                pl.BlockSpec((groups, 8, rows), lambda h, *_: (h, 0, 0)),
                anywhere,
            ],
            scratch_shapes=[pltpu.VMEM((width, rows), BF16)] + group_scratch(HIGH_GROUP),
        ),
        out_shape=[
            jax.ShapeDtypeStruct((rows, MODEL_WIDTH), BF16),
            jax.ShapeDtypeStruct((PAIRS, 8, rows), F32),
            jax.ShapeDtypeStruct(((NBLK - STARTS[1]) * 48, MODEL_WIDTH), BF16),
        ],
        compiler_params=pltpu.CompilerParams(vmem_limit_bytes=56 * MEBI),
        cost_estimate=cost(16 * 10**9, 30 * MEBI),
        name="attention_forward",
    )(
        start,
        count,
        numbers,
        jnp.array(panel_of_block()[::2]),
        label_row,
        label_column,
        projected,
        projected,
        projected,
        *sources,
    )


def attention_backward_kernel(
    tile,
    key_tile,
    start_ref,
    count_ref,
    row_ref,
    column_ref,
    q_ref,
    k_ref,
    v_ref,
    d_ref,
    log_ref,
    *refs,
):
    out_ref, sum_ref, kt_ref, dk_ref, dv_ref = refs[-5:]
    groups = q_ref.shape[1] // LANES
    factor = HEAD_SIZE**-0.5
    kt_ref[...] = k_ref[...].T
    dk_ref[...] = jnp.zeros_like(dk_ref)
    dv_ref[...] = jnp.zeros_like(dv_ref)
    low = low_lanes(tile)

    def run(rows, keys):
        same = column_ref[keys, :] == row_ref[:, rows]
        for group in range(groups):
            lanes = slice(group * LANES, (group + 1) * LANES)
            queries = q_ref[rows, lanes] * jnp.bfloat16(factor)
            upstream = d_ref[rows, lanes]
            d_queries = []
            d_keys = d_values = 0.0
            for part in range(2):
                mask = low if part == 0 else ~low
                chosen = jnp.where(mask, queries, jnp.zeros_like(queries))
                d_chosen = jnp.where(mask, upstream, jnp.zeros_like(upstream))
                scores = dot(k_ref[keys, lanes], chosen, ((1,), (1,)))
                exponents = jnp.exp(scores - log_ref[group, part : part + 1, rows])
                probabilities = jnp.where(same, exponents, 0.0)
                d_probs = dot(v_ref[keys, lanes], d_chosen, ((1,), (1,)))
                inner = jnp.sum(probabilities * d_probs, axis=0, keepdims=True)
                d_scores = (probabilities * (d_probs - inner)).astype(BF16)
                d_values += dot(probabilities.astype(BF16), d_chosen)
                d_keys += dot(d_scores, chosen)
                first = group * LANES + part * HEAD_SIZE
                d_queries.append(dot(kt_ref[first : first + HEAD_SIZE, keys], d_scores))
            dk_ref[keys, lanes] += d_keys
            dv_ref[keys, lanes] += d_values
            out_ref[0, rows, lanes] = (jnp.concatenate(d_queries, axis=0).T * factor).astype(BF16)

    over_tiles(tile, key_tile, start_ref, count_ref, run)
    out_ref[1] = dk_ref[...].astype(BF16)
    out_ref[2] = dv_ref[...].astype(BF16)
    sum_ref[0:1, :] = jnp.sum(out_ref[0].astype(F32), axis=0, keepdims=True)
    sum_ref[1:2, :] = jnp.sum(out_ref[2].astype(F32), axis=0, keepdims=True)


def attention_backward(projected, tiles, label_row, label_column, d_attended, logs, first, others, groups=2):
    start, count = tiles
    width = groups * LANES
    steps = PAIRS // groups
    rows = ROW_POSITIONS
    return pl.pallas_call(
        functools.partial(attention_backward_kernel, *BACKWARD_TILES),
        grid_spec=pltpu.PrefetchScalarGridSpec(
            num_scalar_prefetch=2,
            grid=(1,),
            in_specs=[
                pl.BlockSpec((1, rows), lambda h, *_: (0, 0)),
                pl.BlockSpec((rows, 1), lambda h, *_: (0, 0)),
                pl.BlockSpec((rows, width), lambda h, *_: (0, first)),
                pl.BlockSpec((rows, width), lambda h, *_: (0, steps + first)),
                pl.BlockSpec((rows, width), lambda h, *_: (0, 2 * steps + first)),
                pl.BlockSpec((rows, width), lambda h, *_: (0, first)),
                pl.BlockSpec((groups, 8, rows), lambda h, *_: (first, 0, 0)),
            ]
            + [ANYWHERE] * len(others),
            out_specs=[
                pl.BlockSpec((3, rows, width), lambda h, *_: (0, 0, 0)),
                pl.BlockSpec((8, width), lambda h, *_: (0, 0)),
            ],
            scratch_shapes=[
                pltpu.VMEM((width, rows), BF16),
                pltpu.VMEM((rows, width), F32),
                pltpu.VMEM((rows, width), F32),
            ],
        ),
        out_shape=[
            jax.ShapeDtypeStruct((3, rows, width), BF16),
            jax.ShapeDtypeStruct((8, width), F32),
        ],
        compiler_params=pltpu.CompilerParams(vmem_limit_bytes=48 * MEBI),
        cost_estimate=cost(11 * 10**9, 6 * rows * MODEL_WIDTH),
        name="attention_backward",
    )(
        start,
        count,
        label_row,
        label_column,
        projected,
        projected,
        projected,
        d_attended,
        logs,
        *others,
    )


def mean(value):
    return jnp.sum(value, axis=1, keepdims=True) * (1.0 / MODEL_WIDTH)


def load_once(step, pairs, semaphores):
    copies = [pltpu.make_async_copy(source, held, semaphores.at[i]) for i, (source, held) in enumerate(pairs)]

    @pl.when(step == 0)
    def _():
        for copy in copies:
            copy.start()

    def wait(index):
        pl.when(step == 0)(copies[index].wait)

    return wait


def middle_kernel(
    head_ref,
    attended_ref,
    x_ref,
    piece0,
    piece1,
    piece2,
    piece3,
    vec_ref,
    sheet_ref,
    output_ref,
    normed_ref,
    activated_ref,
    d_before_ref,
    d_feed_ref,
    d_first_ref,
    d_branch_ref,
    d_attended_ref,
    sums_ref,
    out_weight,
    up_weight,
    down_weight,
    slope_ref,
    semaphores,
):
    width = MODEL_WIDTH
    step = pl.program_id(0)
    wait = load_once(
        step,
        [
            (sheet_ref.at[pl.ds(0, width), :], out_weight),
            (sheet_ref.at[pl.ds(width, FF), :], up_weight),
            (sheet_ref.at[pl.ds(width + FF, FF), :], down_weight),
        ],
        semaphores,
    )

    @pl.when(step == 0)
    def _():
        sums_ref[...] = jnp.zeros_like(sums_ref)

    def add_up(row, value):
        sums_ref[row : row + 1, :] += jnp.sum(value, axis=0, keepdims=True)

    def vector(row):
        return vec_ref[row : row + 1, :]

    wait(0)
    hidden = x_ref[...].astype(F32) + (dot(attended_ref[...], out_weight[...]) + vector(6))
    center = hidden - mean(hidden)
    first_scale = lax.rsqrt(mean(center * center) + NORM_EPSILON)
    first_normal = center * first_scale
    normed = first_normal * vector(0) + vector(1)
    normed_low = normed.astype(BF16)
    normed_ref[...] = normed_low
    wait(1)
    wait(2)
    feed_out = vector(7)
    for chunk in range(CHUNKS):
        part = slice(chunk * width, (chunk + 1) * width)
        before = dot(normed_low, up_weight[part, :]) + vector(8 + chunk)
        share = 0.5 + 0.5 * lax.erf(before * np.float32(np.sqrt(0.5)))
        density = jnp.exp(before * before * -0.5) * np.float32(1.0 / np.sqrt(2.0 * np.pi))
        slope_ref[:, part] = share + before * density
        activated = (before * share).astype(BF16)
        activated_ref[:, part] = activated
        feed_out = feed_out + dot(activated, down_weight[part, :])
    mixed = normed + feed_out
    center = mixed - mean(mixed)
    second_scale = lax.rsqrt(mean(center * center) + NORM_EPSILON)
    second_normal = center * second_scale
    output_ref[...] = (second_normal * vector(2) + vector(3)).astype(BF16)
    source = step ^ head_ref[0]
    upstream = jnp.where(source % 2 == 0, piece0[...], piece1[...])
    upstream = jnp.where(source < 2, upstream, jnp.where(source % 2 == 0, piece2[...], piece3[...]))
    upstream = upstream.astype(F32)
    add_up(2, upstream * second_normal)
    add_up(3, upstream)
    scaled = upstream * vector(2)
    d_mixed = second_scale * (scaled - mean(scaled) - second_normal * mean(scaled * second_normal))
    d_feed = d_mixed.astype(BF16)
    d_feed_ref[...] = d_feed
    add_up(7, d_feed.astype(F32))
    d_normed = d_mixed
    for chunk in range(CHUNKS):
        part = slice(chunk * width, (chunk + 1) * width)
        d_active = dot(d_feed, down_weight[part, :], ((1,), (1,)))
        d_before = (d_active * slope_ref[:, part]).astype(BF16)
        d_before_ref[:, part] = d_before
        add_up(8 + chunk, d_before.astype(F32))
        d_normed = d_normed + dot(d_before, up_weight[part, :], ((1,), (1,)))
    add_up(0, d_normed * first_normal)
    add_up(1, d_normed)
    scaled = d_normed * vector(0)
    d_first = first_scale * (scaled - mean(scaled) - first_normal * mean(scaled * first_normal))
    d_first_ref[...] = d_first
    d_branch = d_first.astype(BF16)
    d_branch_ref[...] = d_branch
    add_up(6, d_branch.astype(F32))
    d_attended_ref[...] = dot(d_branch, out_weight[...], ((1,), (1,))).astype(BF16)


def middle(attended, x, pieces, vectors, sheet):
    rows, width = x.shape
    tile = pieces[0].shape[0]
    by_tile = lambda columns: pl.BlockSpec((tile, columns), lambda i, *_: (i, 0))
    fixed = lambda count: pl.BlockSpec((count, width), lambda i, *_: (0, 0))
    outs = [(width, BF16), (width, BF16), (FF, BF16), (FF, BF16), (width, BF16), (width, F32)]
    outs += [(width, BF16), (width, BF16)]
    head = lax.axis_index("head").reshape(1).astype(jnp.int32)
    return pl.pallas_call(
        middle_kernel,
        grid_spec=pltpu.PrefetchScalarGridSpec(
            num_scalar_prefetch=1,
            grid=(rows // tile,),
            in_specs=[by_tile(width)] * 2 + [fixed(tile)] * 4 + [fixed(12), ANYWHERE],
            out_specs=[by_tile(columns) for columns, _ in outs] + [fixed(12)],
            scratch_shapes=[
                pltpu.VMEM((width, width), BF16),
                pltpu.VMEM((FF, width), BF16),
                pltpu.VMEM((FF, width), BF16),
                pltpu.VMEM((tile, FF), F32),
                pltpu.SemaphoreType.DMA((3,)),
            ],
        ),
        out_shape=[jax.ShapeDtypeStruct((rows, columns), dtype) for columns, dtype in outs]
        + [jax.ShapeDtypeStruct((12, width), F32)],
        compiler_params=pltpu.CompilerParams(vmem_limit_bytes=56 * MEBI),
        cost_estimate=cost(rows * width * (FF * 8 + width * 4), rows * width * 40),
        name="layer_middle",
    )(head, attended, x, *pieces, vectors, sheet)


def store_panels(value, core, kept_ref, sent_ref):
    for own in range(2):

        @pl.when(core == own)
        def _():
            for ref, half in ((kept_ref, own), (sent_ref, 1 - own)):
                for pair in range(2):
                    for quarter in range(4):
                        first = 2 * pair * B + quarter * 48 + half * 24
                        rows = [value[first : first + 24], value[first + B : first + B + 24]]
                        ref[quarter, pair] = jnp.concatenate(rows, axis=0).astype(BF16)


def gradient_kernel(pairs, core_ref, *refs):
    kept_ref, sent_ref = refs[-2:]
    step = pl.program_id(0)
    for low, high, left, rights in pairs:

        def run(left=refs[left], rights=[refs[right] for right in rights]):
            if len(rights) == 1:
                right = rights[0][...]
            else:
                right = jnp.concatenate([part[0] for part in rights], axis=1)
            store_panels(dot(left[...], right, ((0,), (0,))), core_ref[0], kept_ref, sent_ref)

        pl.when((step >= low) & (step < high))(run)


def gradient_call(steps, pairs, specs, values, name, others=()):
    core = (lax.axis_index("seq") % 2).reshape(1).astype(jnp.int32)
    shape = jax.ShapeDtypeStruct((4, 2 * steps, 48, MODEL_WIDTH), BF16)
    spec = pl.BlockSpec((4, 2, 48, MODEL_WIDTH), lambda i, *_: (0, i, 0, 0))
    return pl.pallas_call(
        functools.partial(gradient_kernel, pairs),
        grid_spec=pltpu.PrefetchScalarGridSpec(
            num_scalar_prefetch=1,
            grid=(steps,),
            in_specs=specs + [ANYWHERE] * len(others),
            out_specs=[spec, spec],
        ),
        out_shape=[shape, shape],
        compiler_params=pltpu.CompilerParams(vmem_limit_bytes=48 * MEBI),
        cost_estimate=cost(2 * ROW_POSITIONS * steps * MODEL_WIDTH**2, 4 * steps * MEBI),
        name=name,
    )(core, *values, *others)


FIXED_ROWS = pl.BlockSpec((ROW_POSITIONS, MODEL_WIDTH), lambda i, *_: (0, 0))
def feed_gradients(normed_low, d_before, activated, d_feed, others):
    pairs = [(0, CHUNKS, 0, [1]), (CHUNKS, 2 * CHUNKS, 2, [3])]
    moving = lambda first: pl.BlockSpec(
        (ROW_POSITIONS, MODEL_WIDTH), lambda i, *_: (0, jnp.clip(i - first, 0, CHUNKS - 1))
    )
    return gradient_call(
        2 * CHUNKS,
        pairs,
        [FIXED_ROWS, moving(0), moving(CHUNKS), FIXED_ROWS],
        (normed_low, d_before, activated, d_feed),
        "feed_gradients",
        others,
    )


def attention_gradients(x, attended, d_branch, d_projected, others):
    count = len(d_projected)
    pairs = [(0, 3, 0, list(range(3, 3 + count))), (3, 4, 1, [2])]
    third = lambda part: pl.BlockSpec(
        (1,) + part.shape[1:], lambda i, *_: (jnp.minimum(i, 2), 0, 0)
    )
    return gradient_call(
        CHUNKS,
        pairs,
        [FIXED_ROWS] * 3 + [third(part) for part in d_projected],
        (x, attended, d_branch) + tuple(d_projected),
        "attention_gradients",
        others,
    )


def input_gradient_kernel(count, sheet_ref, d_first_ref, *refs):
    parts, out_ref = refs[:count], refs[-1]
    value = d_first_ref[...]
    for third in range(3):
        weight = sheet_ref[third * MODEL_WIDTH : (third + 1) * MODEL_WIDTH, :]
        d_rows = jnp.concatenate([part[third] for part in parts], axis=1)
        value = value + dot(d_rows, weight, ((1,), (1,)))
    out_ref[...] = value.astype(BF16)


def input_gradient(d_projected, sheet, d_first, others, tile=512):
    rows = d_first.shape[0]
    by_tile = pl.BlockSpec((tile, MODEL_WIDTH), lambda i: (i, 0))
    return pl.pallas_call(
        functools.partial(input_gradient_kernel, len(d_projected)),
        grid=(rows // tile,),
        in_specs=[
            pl.BlockSpec((3 * MODEL_WIDTH, MODEL_WIDTH), lambda i: (0, 0), pipeline_mode=pl.Buffered(1)),
            by_tile,
        ]
        + [pl.BlockSpec((3, tile, part.shape[2]), lambda i: (0, i, 0)) for part in d_projected]
        + [ANYWHERE] * len(others),
        out_specs=by_tile,
        out_shape=jax.ShapeDtypeStruct((rows, MODEL_WIDTH), BF16),
        compiler_params=pltpu.CompilerParams(vmem_limit_bytes=48 * MEBI),
        cost_estimate=cost(6 * rows * MODEL_WIDTH**2, 14 * MEBI),
        name="input_gradient",
    )(sheet, d_first, *d_projected, *others)


def add_parts(*parts):
    return functools.reduce(jnp.add, [part.astype(F32) for part in parts]).astype(BF16)


def pick(value, index, axis=0):
    return lax.dynamic_index_in_dim(value, index, axis, keepdims=False)


def head_first_parts(kept):
    head = lax.axis_index("head")
    x, y = head % 2, head // 2
    cut = kept.shape[1] // 2
    square = kept.reshape((2, 2) + kept.shape[1:])
    first, second = square[:, :, :cut], square[:, :, cut:]
    sent = pick(first, 1 - x, 1), pick(second, 1 - y, 0)
    return sent, (pick(first, x, 1), pick(second, y, 0))


def head_first_send(sent):
    return permute_xor(sent[0], "head", 1), permute_xor(sent[1], "head", 2)


def head_second_parts(first, second):
    head = lax.axis_index("head")
    x, y = head % 2, head // 2
    sent = pick(first, 1 - y), pick(second, 1 - x)
    return sent, (pick(first, y), pick(second, x))


def head_second_send(sent):
    return permute_xor(sent[0], "head", 2), permute_xor(sent[1], "head", 1)


def add_pairs(kept, arrived):
    return [add_parts(one, two) for one, two in zip(kept, arrived)]


TOGETHER = 4
BUNDLE = TOGETHER * 36


def owned_kernel(panel_ref, lane_ref, odd_ref, sheet_ref, carried_ref, out_ref, carried_out):
    del carried_ref, carried_out
    first = pl.program_id(0) * out_ref.shape[0] * TOGETHER
    half = low_lanes(24)

    def bundle(place, carry):
        mains, rests = [], []
        for index in range(TOGETHER):
            slot = first + place * TOGETHER + index
            panel, odd = panel_ref[slot], odd_ref[slot] == 1
            pair = panel // 2
            lane = pl.multiple_of(lane_ref[slot], LANES)
            main_lane = pl.multiple_of(lane + jnp.where(odd, 2 * LANES, 0), LANES)
            values = []
            for begin in (main_lane, pl.multiple_of(lane + LANES, LANES)):
                value = sheet_ref[pair, :, pl.ds(begin, LANES)].astype(F32)
                values.append(jnp.where(panel % 2 == 1, value[24:], value[:24]))
            mains.append(values[0])
            turn = odd if index % 2 == 0 else jnp.logical_not(odd)
            rests.append(jnp.where(turn, pltpu.roll(values[1], LANES // 2, 1), values[1]))
        rests = [jnp.where(half, rests[i], rests[i + 1]) for i in range(0, TOGETHER, 2)]
        out_ref[place] = jnp.concatenate(mains + rests, axis=0).astype(BF16)
        return carry

    lax.fori_loop(0, out_ref.shape[0], bundle, 0)


def by_owner(sheet_gradient, owner_order, carried):
    owners = lax.axis_size("seq")
    count = NBLK // owners
    bundles = -(-count // TOGETHER)
    slots = jnp.pad(owner_order.reshape(owners, count), ((0, 0), (0, bundles * TOGETHER - count)))
    slots = slots.reshape(-1)
    steps = 4 if owners * bundles % 4 == 0 else 1
    each = owners * bundles // steps
    panels = jnp.asarray(panel_of_block())
    whole = jnp.arange(NBLK, dtype=jnp.int32)
    panels = jnp.sum(jnp.where(slots[:, None] == whole[None, :], panels[None, :], 0), axis=1)
    gathered, carried = pl.pallas_call(
        owned_kernel,
        grid_spec=pltpu.PrefetchScalarGridSpec(
            num_scalar_prefetch=3,
            grid=(steps,),
            in_specs=[pl.BlockSpec(sheet_gradient.shape, lambda i, *_: (0, 0, 0)), ANYWHERE],
            out_specs=[pl.BlockSpec((each, BUNDLE, LANES), lambda i, *_: (i, 0, 0)), ANYWHERE],
        ),
        out_shape=[
            jax.ShapeDtypeStruct((owners * bundles, BUNDLE, LANES), BF16),
            jax.ShapeDtypeStruct(carried.shape, carried.dtype),
        ],
        input_output_aliases={4: 1},
        compiler_params=pltpu.CompilerParams(vmem_limit_bytes=24 * MEBI),
        cost_estimate=cost(0, 4 * MEBI),
        name="gradients_by_owner",
    )(panels, slots // 2 % 2 * 384, slots % 2, sheet_gradient, carried)
    return gathered.reshape(owners // 2, 2, bundles, BUNDLE, LANES), carried


def add_tree(terms):
    while len(terms) > 1:
        terms = [one + two for one, two in zip(terms[::2], terms[1::2])]
    return terms[0]


def two_parts(value):
    high = lax.reduce_precision(value, 8, 7)
    return high, lax.reduce_precision(value - high, 8, 7)


def sum_to_owners(parts, sums, others):
    chips = lax.axis_size("seq") // 2
    seq = lax.axis_index("seq")
    chip, core = seq // 2, seq % 2
    shape = parts.shape[2:]
    flat = lambda value: value.reshape((-1,) + shape[1:])

    def with_sums(value, total):
        high, low = two_parts(total)
        both = jnp.concatenate([high, low]).astype(BF16)
        return jnp.concatenate([flat(value), flat(both)])

    def split_sums(value):
        high, low = value[-1].astype(F32).reshape((2,) + sums.shape)
        return value[:-1], high + low

    packed = flat if sums is None else functools.partial(with_sums, total=sums)
    arrived = [packed(pick(parts, chip))]
    for mask in range(1, chips):
        arrived.append(permute_xor(packed(pick(parts, chip ^ mask)), "seq", 2 * mask))
    if others:
        arrived[1:] = gate(arrived[1:], others)
    if sums is not None:
        split = [split_sums(value) for value in arrived]
        arrived = [value for value, _ in split]
        sums = add_tree([total for _, total in split])
    mine = add_parts(*arrived).reshape((2,) + shape)
    packed = flat if sums is None else functools.partial(with_sums, total=sums)
    other = permute_xor(packed(pick(mine, 1 - core)), "seq", 1)
    if sums is not None:
        other, total = split_sums(other)
        high, low = two_parts(sums)
        sums = (high + low) + total
    return jnp.stack([pick(mine, core), other.reshape(shape)]), sums


def gather_quarters(part):
    return [part] + [permute_xor(part, "head", mask) for mask in (1, 2, 3)]


def shampoo_kernel(
    base,
    held,
    number_ref,
    place_ref,
    part0,
    part1,
    part2,
    part3,
    momentum_ref,
    left_ref,
    right_ref,
    root_left_ref,
    root_right_ref,
    master_ref,
    *refs,
):
    new_momentum_ref, new_left_ref, new_right_ref, new_master_ref, main_ref, rest_ref = refs[held:]
    count = momentum_ref.shape[0]
    first = (base + pl.program_id(0)) * count
    low = low_lanes(B)
    half = low_lanes(24)
    core = place_ref[4]
    for slot in range(count):
        odd = number_ref[first + slot] % 2 == 1
        for index, part in enumerate((part0, part1, part2, part3)):
            for which in range(2):
                row = pl.multiple_of(place_ref[index] * 48 + (which ^ core) * 24, 8)
                bundle = part[which, slot // TOGETHER].astype(F32)
                inside = slot % TOGETHER
                main_ref[pl.ds(row, 24), :] = bundle[inside * 24 : inside * 24 + 24]
                begin = TOGETHER * 24 + inside // 2 * 24
                rest_ref[pl.ds(row, 24), :] = bundle[begin : begin + 24]
        main = main_ref[...]
        rest = rest_ref[...]
        spun = pltpu.roll(main, LANES // 2, 1)
        rest_low = rest if slot % 2 == 0 else pltpu.roll(rest, LANES // 2, 1)
        left_lanes = jnp.where(odd, jnp.where(low, rest_low, spun), main)
        right_lanes = jnp.where(odd, spun, rest_low)
        gradient = jnp.concatenate([left_lanes, right_lanes[:, : LANES // 2]], axis=1)
        new_momentum = MOMENTUM_DECAY * momentum_ref[slot] + (1.0 - MOMENTUM_DECAY) * gradient
        new_momentum_ref[slot] = new_momentum
        grad_low = gradient.astype(BF16)
        new_left_ref[slot] = STAT_DECAY * left_ref[slot] + (1.0 - STAT_DECAY) * dot(
            grad_low, grad_low, ((1,), (1,))
        )
        new_right_ref[slot] = STAT_DECAY * right_ref[slot] + (1.0 - STAT_DECAY) * dot(
            grad_low, grad_low, ((0,), (0,))
        )
        leftward = dot(root_left_ref[slot].astype(BF16), new_momentum.astype(BF16))
        preconditioned = dot(leftward.astype(BF16), root_right_ref[slot].astype(BF16))
        master = master_ref[slot]
        new_master_ref[slot] = master - MATRIX_RATE * (preconditioned + WEIGHT_DECAY * master)


def shampoo(numbers, parts, states, first, earlier, others):
    group = TOGETHER if numbers.shape[0] % TOGETHER == 0 else numbers.shape[0]
    steps = parts[0].shape[1]
    base = first // group
    spec = pl.BlockSpec((group, B, B), lambda i, *_: (base + i, 0, 0))
    part_spec = pl.BlockSpec((2, 1, BUNDLE, LANES), lambda i, *_: (0, i, 0, 0))
    places = lax.axis_index("head") ^ jnp.arange(4, dtype=jnp.int32)
    places = jnp.concatenate([places, (lax.axis_index("seq") % 2).reshape(1).astype(jnp.int32)])
    return pl.pallas_call(
        functools.partial(shampoo_kernel, base, len(earlier) + len(others)),
        grid_spec=pltpu.PrefetchScalarGridSpec(
            num_scalar_prefetch=2,
            grid=(steps,),
            in_specs=[part_spec] * 4
            + [spec] * 6
            + [ANYWHERE] * (len(earlier) + len(others)),
            out_specs=[spec] * 4,
            scratch_shapes=[pltpu.VMEM((B, LANES), F32), pltpu.VMEM((B, LANES), F32)],
        ),
        out_shape=[jax.ShapeDtypeStruct((numbers.shape[0], B, B), F32)] * 4,
        input_output_aliases={12 + i: i for i in range(len(earlier))},
        compiler_params=pltpu.CompilerParams(vmem_limit_bytes=48 * MEBI),
        cost_estimate=cost(8 * steps * group * B**3, 10 * steps * group * B * B * 4),
        name="shampoo_blocks",
    )(numbers, places, *parts, *states, *earlier, *others)


def adam_step(vector_grad, vec_first, vec_second, vectors):
    new_first = FIRST_DECAY * vec_first + (1.0 - FIRST_DECAY) * vector_grad
    new_second = SECOND_DECAY * vec_second + (1.0 - SECOND_DECAY) * vector_grad * vector_grad
    corrected_first = new_first / (1.0 - FIRST_DECAY**STEP)
    corrected_second = new_second / (1.0 - SECOND_DECAY**STEP)
    new_vectors = vectors - VECTOR_RATE * corrected_first / (
        jnp.sqrt(corrected_second) + ADAM_EPSILON
    )
    return (new_first, new_second, new_vectors)


def exchange_rows(value):
    return lax.all_to_all(value, "head", split_axis=0, concat_axis=0, tiled=True)


def parts_to_send(value):
    head = lax.axis_index("head")
    return [pick(value, head ^ mask) for mask in (1, 2, 3)]


def send_rows(parts):
    return [permute_xor(part, "head", mask) for mask, part in enumerate(parts, 1)]


def arrange_rows(value, arrived):
    head = lax.axis_index("head")
    result = value
    for mask, piece in enumerate(arrived, 1):
        result = lax.dynamic_update_index_in_dim(result, piece, head ^ mask, 0)
    return result


def local(
    tokens,
    cotangent,
    segment_ids,
    owner_order,
    master_blocks,
    momentum,
    stat_left,
    stat_right,
    root_left,
    root_right,
    vectors,
    vec_first,
    vec_second,
):
    width = MODEL_WIDTH
    count = master_blocks.shape[0]
    head = lax.axis_index("head")
    numbers = lax.dynamic_slice_in_dim(owner_order, lax.axis_index("seq") * count, count, 0)
    sheet_vectors = vectors.reshape(12, width)

    labels = lax.dynamic_index_in_dim(segment_ids, head, 0, keepdims=False)
    early = [sheet_vectors, labels.reshape(1, -1), labels.reshape(-1, 1)]
    early += [*key_tiles(labels, *FORWARD_TILES), *key_tiles(labels, *BACKWARD_TILES)]
    early += [exchange_rows(tokens).reshape(ROW_POSITIONS, width)]
    packed = pack_blocks(numbers, master_blocks)
    blocks, source_numbers, early = gather_weights(packed, owner_order, early)
    sheet_vectors, label_row, label_column = early[:3]
    wide_tiles, tiles, x = early[3:5], early[5:7], early[7]
    upstream = [pick(cotangent, head), *send_rows(parts_to_send(cotangent))]

    projected, input_sheet = project(x, sheet_vectors, blocks, source_numbers)
    attended, logs, sheet = attention_forward(
        projected, wide_tiles, label_row, label_column, blocks, source_numbers
    )
    upstream[1:] = gate(upstream[1:], [attended])
    (
        output,
        normed_low,
        activated,
        d_before,
        d_feed,
        d_first,
        d_branch,
        d_attended,
        sums,
    ) = middle(attended, x, upstream, sheet_vectors, sheet)
    def backward(index, *others):
        return attention_backward(
            projected, tiles, label_row, label_column, d_attended, logs, index, others
        )

    output = output.reshape(tokens.shape)
    output_sent = parts_to_send(output)
    feed, feed_sent = feed_gradients(normed_low, d_before, activated, d_feed, [])
    parts = [backward(0, feed, feed_sent, *output_sent)]
    feed = add_parts(feed, *gate([permute_xor(feed_sent, "seq", 1)], parts[0][:1]))
    feed_sent, feed = head_first_parts(feed)
    output_arrived = gate(send_rows(output_sent), feed_sent)
    parts.append(backward(1, parts[0][0], *feed_sent, *output_arrived))
    parts.append(backward(2, parts[1][0]))
    feed = add_pairs(feed, gate(head_first_send(feed_sent), parts[2][:1]))
    feed_sent, feed = head_second_parts(*feed)
    d_projected = [part[0] for part in parts]
    rest, rest_sent = attention_gradients(x, attended, d_branch, d_projected, feed_sent)
    feed = jnp.concatenate(add_pairs(feed, gate(head_second_send(feed_sent), [rest])))
    rest = add_parts(rest, *gate([permute_xor(rest_sent, "seq", 1)], [feed]))
    rest_sent, rest = head_first_parts(rest)
    bias_sums = jnp.concatenate([part[1] for part in parts], axis=1)
    sums = jnp.concatenate([sums[:4], bias_sums[:2], sums[6:]])
    input_grad = input_gradient(d_projected, input_sheet, d_first, rest_sent)
    arrived = [permute_xor(sums, "head", mask) for mask in (1, 2, 3)]
    sums = add_tree([sums, *gate(arrived, [input_grad])])
    rest = add_pairs(rest, gate(head_first_send(rest_sent), [input_grad]))
    rest_sent, rest = head_second_parts(*rest)
    rest = jnp.concatenate(add_pairs(rest, head_second_send(rest_sent)))
    owned, input_grad = by_owner(jnp.concatenate([rest, feed]), owner_order, input_grad)
    input_grad = exchange_rows(input_grad.reshape(tokens.shape))
    output = arrange_rows(output, output_arrived)
    bundles = owned.shape[2]
    halves = 2 if bundles % 2 == 0 else 1
    each = bundles // halves
    states = (momentum, stat_left, stat_right, root_left, root_right, master_blocks)
    if halves == 1:
        part, total = sum_to_owners(owned, sums, [])
        blocks = shampoo(numbers, gather_quarters(part), states, 0, (), [])
        input_grad = input_grad.astype(F32)
    else:
        part, _ = sum_to_owners(owned[:, :, :each], None, [])
        quarters = gather_quarters(part)
        part, total = sum_to_owners(owned[:, :, each:], sums, [*quarters[1:], input_grad])
        input_grad = input_grad.astype(F32)
        blocks = shampoo(numbers, quarters, states, 0, (), [part])
        quarters = gather_quarters(part)
        blocks = shampoo(numbers, quarters, states, each * TOGETHER, blocks, [input_grad, output])
    new_first, new_second, new_vectors = adam_step(total.reshape(-1), vec_first, vec_second, vectors)

    new_momentum, new_left, new_right, new_master = blocks
    return (
        output,
        input_grad,
        new_momentum,
        new_left,
        new_right,
        new_master,
        new_first,
        new_second,
        new_vectors,
    )


def solution(mesh):
    blocks = P("seq", None, None)
    positions = P("seq", "head", None)
    return jax.shard_map(
        local,
        mesh=mesh,
        in_specs=(positions, positions, P("seq", None), P()) + (blocks,) * 6 + (P(),) * 3,
        out_specs=(positions, positions) + (blocks,) * 4 + (P(),) * 3,
        check_vma=False,
    )
```

```python
import functools

import jax
import jax.numpy as jnp
import numpy as np
from jax import lax
from jax.experimental import pallas as pl
from jax.experimental.pallas import tpu as pltpu
from jax.sharding import PartitionSpec as P

MODEL_WIDTH = 768
HEAD_TOTAL = 12
HEAD_SIZE = 64
FF = 3072
ROW_POSITIONS = 1024
B = 192
STEP = 10
NBLK = 192
PAIRS = HEAD_TOTAL // 2
LANES = 128
REST = B * B // LANES
QUARTER = REST // 4
CHUNKS = FF // MODEL_WIDTH
MEBI = 2**20

NORM_EPSILON = 1e-05
STAT_DECAY = 0.5
MOMENTUM_DECAY = 0.5
MATRIX_RATE = 1.0
WEIGHT_DECAY = 0.01
FIRST_DECAY = 0.9
SECOND_DECAY = 0.999
VECTOR_RATE = 0.3
ADAM_EPSILON = 1e-08

F32 = jnp.float32
BF16 = jnp.bfloat16
STARTS = (0, 48, 64, 128, 192)


def panel_of_block():
    panels = []
    for block in range(NBLK):
        if block < STARTS[1]:
            panels.append((block % 12) // 4 * 4 + block // 12)
        elif block < STARTS[2]:
            panels.append(12 + (block - STARTS[1]) // 4)
        elif block < STARTS[3]:
            inner = block - STARTS[2]
            panels.append(16 + (inner % 16) // 4 * 4 + inner // 16)
        else:
            panels.append(32 + (block - STARTS[3]) // 4)
    return np.array(panels, np.int32)


def cost(flops, moved, transcendentals=0):
    return pl.CostEstimate(flops=flops, bytes_accessed=moved, transcendentals=transcendentals)


def dot(left, right, contract=((1,), (0,))):
    return lax.dot_general(left, right, (contract, ((), ())), preferred_element_type=F32)


def low_lanes(rows):
    return lax.broadcasted_iota(jnp.int32, (rows, LANES), 1) < LANES // 2


def pack_kernel(order_ref, blocks_ref, packed_ref):
    count = blocks_ref.shape[0]
    first = pl.program_id(0) * count
    half = low_lanes(B // 2)
    low = low_lanes(B)
    for slot in range(count):
        left = blocks_ref[slot, :, :LANES]
        narrow = blocks_ref[slot, :, LANES:]
        right = jnp.concatenate([narrow, narrow], axis=1)
        turned = pltpu.roll(left, LANES // 2, 1)
        odd = order_ref[first + slot] % 2 == 1
        main = jnp.where(odd, jnp.where(low, turned, right), left)
        even_rest = jnp.where(half, right[: B // 2], right[B // 2 :])
        odd_rest = jnp.where(half, left[B // 2 :], turned[: B // 2])
        packed_ref[slot, :B, :] = main.astype(BF16)
        packed_ref[slot, B:, :] = jnp.where(odd, odd_rest, even_rest).astype(BF16)


def pack_blocks(order, blocks):
    count = blocks.shape[0]
    group = max(size for size in range(1, 7) if count % size == 0)
    return pl.pallas_call(
        pack_kernel,
        grid_spec=pltpu.PrefetchScalarGridSpec(
            num_scalar_prefetch=1,
            grid=(count // group,),
            in_specs=[pl.BlockSpec((group, B, B), lambda i, *_: (i, 0, 0))],
            out_specs=pl.BlockSpec((group, REST, LANES), lambda i, *_: (i, 0, 0)),
        ),
        out_shape=jax.ShapeDtypeStruct((count, REST, LANES), BF16),
        cost_estimate=cost(0, count * B * B * 6),
        name="pack_weight_blocks",
    )(order, blocks)


def permute_xor(value, axis, mask):
    size = lax.axis_size(axis)
    return lax.ppermute(value, axis, [(i, i ^ mask) for i in range(size)])


def gate_kernel(*refs):
    del refs


def gate(values, others):
    flat = list(values)
    shapes = [jax.ShapeDtypeStruct(value.shape, value.dtype) for value in flat]
    return pl.pallas_call(
        gate_kernel,
        in_specs=[ANYWHERE] * (len(flat) + len(others)),
        out_specs=[ANYWHERE] * len(flat),
        out_shape=shapes,
        input_output_aliases={i: i for i in range(len(flat))},
        cost_estimate=cost(0, 0),
        name="gate",
    )(*flat, *others)


ANYWHERE = pl.BlockSpec(memory_space=pl.ANY)


def gathered_slots(heads, chips, count):
    size, cut = count // heads, count // heads // 2
    slots = np.zeros((heads, chips, 2, NBLK), np.int32)
    for head in range(heads):
        for chip in range(chips):
            places = [(chip, slot) for slot in range(count)]
            for kinds in GROUP_KINDS:
                for mask in range(heads):
                    for chip_mask, half in kinds:
                        begin = (head ^ mask) * size + half * cut
                        places += [(chip ^ chip_mask, begin + slot) for slot in range(cut)]
            for core in range(2):
                slots[head, chip, core] = [
                    (c * 2 + which) * count + slot for which in (core, 1 - core) for c, slot in places
                ]
    return slots


GROUP_KINDS = (((1, 0), (1, 1)), ((2, 0), (3, 0)), ((2, 1), (3, 1)))


def gather_weights(packed, owner_order, early):
    heads = lax.axis_size("head")
    chips = lax.axis_size("seq") // 2
    count = packed.shape[0]
    head = lax.axis_index("head")
    seq = lax.axis_index("seq")
    chip, core = seq // 2, seq % 2
    if count % (2 * heads) or chips != 4:
        return [lax.all_gather(packed, "seq", axis=0, tiled=True)], owner_order, early
    size = count // heads
    cut = size // 2
    slots = jnp.asarray(gathered_slots(heads, chips, count).reshape(-1, NBLK))
    slots = lax.dynamic_index_in_dim(slots, (head * chips + chip) * 2 + core, 0, keepdims=False)
    whole = jnp.arange(NBLK, dtype=jnp.int32)
    numbers = jnp.sum(jnp.where(slots[:, None] == whole[None, :], owner_order[None, :], 0), axis=1)
    own = lax.dynamic_slice_in_dim(packed, head * size, size, 0)
    halves = own[:cut], own[cut:]
    over_z = lambda half, mask: permute_xor(half, "seq", 2 * mask)
    def first_hop(first, second):
        return [
            permute_xor(first, "head", 1),
            permute_xor(second, "head", 2),
            permute_xor(second, "head", 1),
            permute_xor(first, "head", 2),
        ]

    def second_hop(first_x, second_y, *_):
        return [permute_xor(first_x, "head", 2), permute_xor(second_y, "head", 1)]

    def swap_cores(pieces):
        return [permute_xor(piece, "seq", 1) for piece in pieces]

    def arranged(pieces, one, two):
        first_x, second_y, second_x, first_y = one
        return [*pieces, first_x, second_x, first_y, second_y, *two]

    near = [over_z(half, 1) for half in halves]
    halfway = [over_z(halves[0], 2), over_z(halves[0], 3)]
    swapped = swap_cores([packed])
    *near, late = gate([*near, halves[1]], [*swapped, numbers, *early[:-1]])
    near_one = first_hop(*near)
    last = [over_z(late, 2), over_z(late, 3)]
    gated = gate([*near_one[:2], *halfway], near_one[2:])
    near_one[:2], halfway = gated[:2], gated[2:]
    near_two = second_hop(*near_one)
    halfway_one = first_hop(*halfway)
    gated = gate([*halfway_one[:2], *last], [*halfway_one[2:], *near_two, early[-1]])
    halfway_one[:2], last = gated[:2], gated[2:]
    halfway_two = second_hop(*halfway_one)
    last_one = first_hop(*last)
    last_one[:2] = gate(last_one[:2], [*last_one[2:], *halfway_two])
    last_two = second_hop(*last_one)
    mine = [
        jnp.concatenate(arranged(near, near_one, near_two)),
        jnp.concatenate(arranged(halfway, halfway_one, halfway_two)),
        jnp.concatenate(arranged(last, last_one, ())),
        *last_two,
    ]
    return [packed, *mine, *swapped, *swap_cores(mine)], numbers, early


LOW_GROUP = (STARTS[0], STARTS[1])
HIGH_GROUP = (STARTS[1], STARTS[4])


def fetch_blocks(number_ref, sources, blocks, arrive, group):
    low, high = group
    first = 0
    for source in sources:

        def start(place, carry, source=source, first=first):
            number = number_ref[first + place]

            @pl.when((number >= low) & (number < high))
            def _():
                pltpu.make_async_copy(source.at[place], blocks.at[number - low], arrive).start()

            return carry

        count = source.shape[0]
        lax.fori_loop(0, count, start, 0, unroll=min(count, 4))
        first += count


def lay_out_blocks(panel_ref, blocks, sheet, group, begin, end):
    low = group[0]
    half = low_lanes(B // 2)

    def lay_out(index, carry):
        pair = low // 2 + index
        row = pl.multiple_of((panel_ref[pair] - low // 4) * B, B)
        lane = pl.multiple_of((pair % 2) * 384, LANES)
        even, odd = 2 * index, 2 * index + 1
        sheet[pl.ds(row, B), pl.ds(lane, LANES)] = blocks[even, :B, :]
        sheet[pl.ds(row, B), pl.ds(lane + 2 * LANES, LANES)] = blocks[odd, :B, :]
        even_rest = blocks[even, B:, :].astype(F32)
        odd_rest = blocks[odd, B:, :].astype(F32)
        turned = pltpu.roll(jnp.where(half, odd_rest, even_rest), LANES // 2, 1)
        center = jnp.concatenate([jnp.where(half, even_rest, odd_rest), turned], axis=0)
        sheet[pl.ds(row, B), pl.ds(lane + LANES, LANES)] = center.astype(BF16)
        return carry

    lax.fori_loop(begin, end, lay_out, 0, unroll=4)


def group_scratch(group):
    count = group[1] - group[0]
    return [
        pltpu.VMEM((count * 48, MODEL_WIDTH), BF16),
        pltpu.VMEM((count, REST, LANES), BF16),
        pltpu.SemaphoreType.DMA,
        pltpu.SemaphoreType.DMA,
    ]


def project_kernel(
    number_ref, panel_ref, x_ref, vec_ref, *refs
):
    sources = refs[:-6]
    projected_ref, sheet_out, sheet, blocks, arrive, leave = refs[-6:]
    fetch_blocks(number_ref, sources, blocks, arrive, LOW_GROUP)
    pltpu.make_async_copy(blocks, blocks, arrive).wait()
    lay_out_blocks(panel_ref, blocks, sheet, LOW_GROUP, 0, blocks.shape[0] // 2)
    copy = pltpu.make_async_copy(sheet, sheet_out, leave)
    copy.start()
    for panel in range(3):
        weight = sheet[panel * MODEL_WIDTH : (panel + 1) * MODEL_WIDTH, :]
        for tile in range(x_ref.shape[0] // 512):
            rows = slice(tile * 512, (tile + 1) * 512)
            value = dot(x_ref[rows, :], weight)
            if panel != 1:
                value = value + vec_ref[4 + panel // 2 : 5 + panel // 2, :]
            projected_ref[rows, panel * MODEL_WIDTH : (panel + 1) * MODEL_WIDTH] = value.astype(BF16)
    copy.wait()


def project(x, vectors, sources, numbers):
    rows = x.shape[0]
    whole = lambda shape: pl.BlockSpec(shape, lambda i, *_: (0,) * len(shape))
    anywhere = pl.BlockSpec(memory_space=pl.ANY)
    return pl.pallas_call(
        project_kernel,
        grid_spec=pltpu.PrefetchScalarGridSpec(
            num_scalar_prefetch=2,
            grid=(1,),
            in_specs=[whole(x.shape), whole(vectors.shape)] + [anywhere] * len(sources),
            out_specs=[whole((rows, 3 * MODEL_WIDTH)), anywhere],
            scratch_shapes=group_scratch(LOW_GROUP),
        ),
        out_shape=[
            jax.ShapeDtypeStruct((rows, 3 * MODEL_WIDTH), BF16),
            jax.ShapeDtypeStruct((STARTS[1] * 48, MODEL_WIDTH), BF16),
        ],
        compiler_params=pltpu.CompilerParams(vmem_limit_bytes=48 * MEBI),
        cost_estimate=cost(6 * rows * MODEL_WIDTH**2, 16 * MEBI),
        name="project_queries_keys_values",
    )(numbers, jnp.array(panel_of_block()[::2]), x, vectors, *sources)


FORWARD_TILES = (512, 256)
BACKWARD_TILES = (256, 128)


def key_tiles(labels, tile, key_tile):
    edges = labels.reshape(-1, tile)
    first, last = edges[:, 0], edges[:, -1]
    start = jnp.sum(labels[None, :] < first[:, None], axis=1, dtype=jnp.int32) // key_tile
    end = jnp.sum(labels[None, :] <= last[:, None], axis=1, dtype=jnp.int32)
    return start, (end + key_tile - 1) // key_tile - start


def over_tiles(tile, key_tile, start_ref, count_ref, run):
    def block(index, carry):
        rows = pl.ds(pl.multiple_of(index * tile, tile), tile)
        start = pl.multiple_of(start_ref[index] * key_tile, key_tile)
        for count in range(1, ROW_POSITIONS // key_tile + 1):
            keys = pl.ds(start, count * key_tile)
            pl.when(count_ref[index] == count)(functools.partial(run, rows, keys))
        return carry

    lax.fori_loop(0, ROW_POSITIONS // tile, block, 0)


def attention_forward_kernel(
    tile, key_tile, start_ref, count_ref, number_ref, panel_ref, row_ref, column_ref, q_ref, k_ref, v_ref, *refs
):
    sources = refs[:-8]
    out_ref, log_ref, sheet_out, vt_ref, sheet, blocks, arrive, leave = refs[-8:]
    groups = q_ref.shape[1] // LANES
    step, last = pl.program_id(0), pl.num_programs(0) - 1

    @pl.when(step == 0)
    def _():
        fetch_blocks(number_ref, sources, blocks, arrive, HIGH_GROUP)

    @pl.when(step == 1)
    def _():
        pltpu.make_async_copy(blocks, blocks, arrive).wait()
        lay_out_blocks(panel_ref, blocks, sheet, HIGH_GROUP, 0, blocks.shape[0] // 2)
        pltpu.make_async_copy(sheet, sheet_out, leave).start()

    vt_ref[...] = v_ref[...].T
    low = low_lanes(tile)

    def run(rows, keys):
        same = column_ref[keys, :] == row_ref[:, rows]
        for group in range(groups):
            lanes = slice(group * LANES, (group + 1) * LANES)
            queries = q_ref[rows, lanes] * jnp.bfloat16(HEAD_SIZE**-0.5)
            mixed = []
            for part in range(2):
                chosen = jnp.where(low if part == 0 else ~low, queries, jnp.zeros_like(queries))
                scores = dot(k_ref[keys, lanes], chosen, ((1,), (1,)))
                scores = jnp.where(same, scores, -1e30)
                peak = jnp.max(scores, axis=0, keepdims=True)
                exponents = jnp.exp(scores - peak)
                total = jnp.sum(exponents, axis=0, keepdims=True)
                probabilities = (exponents * (1.0 / total)).astype(BF16)
                first = group * LANES + part * HEAD_SIZE
                mixed.append(dot(vt_ref[first : first + HEAD_SIZE, keys], probabilities))
                log_ref[group, part : part + 1, rows] = peak + jnp.log(total)
            out_ref[rows, lanes] = jnp.concatenate(mixed, axis=0).T.astype(BF16)

    over_tiles(tile, key_tile, start_ref, count_ref, run)

    @pl.when(step == last)
    def _():
        pltpu.make_async_copy(sheet, sheet_out, leave).wait()


def attention_forward(projected, tiles, label_row, label_column, sources, numbers, groups=2):
    start, count = tiles
    width = groups * LANES
    steps = PAIRS // groups
    rows = ROW_POSITIONS
    anywhere = pl.BlockSpec(memory_space=pl.ANY)
    return pl.pallas_call(
        functools.partial(attention_forward_kernel, *FORWARD_TILES),
        grid_spec=pltpu.PrefetchScalarGridSpec(
            num_scalar_prefetch=4,
            grid=(steps,),
            in_specs=[
                pl.BlockSpec((1, rows), lambda h, *_: (0, 0)),
                pl.BlockSpec((rows, 1), lambda h, *_: (0, 0)),
                pl.BlockSpec((rows, width), lambda h, *_: (0, h)),
                pl.BlockSpec((rows, width), lambda h, *_: (0, steps + h)),
                pl.BlockSpec((rows, width), lambda h, *_: (0, 2 * steps + h)),
            ]
            + [anywhere] * len(sources),
            out_specs=[
                pl.BlockSpec((rows, width), lambda h, *_: (0, h)),
                pl.BlockSpec((groups, 8, rows), lambda h, *_: (h, 0, 0)),
                anywhere,
            ],
            scratch_shapes=[pltpu.VMEM((width, rows), BF16)] + group_scratch(HIGH_GROUP),
        ),
        out_shape=[
            jax.ShapeDtypeStruct((rows, MODEL_WIDTH), BF16),
            jax.ShapeDtypeStruct((PAIRS, 8, rows), F32),
            jax.ShapeDtypeStruct(((NBLK - STARTS[1]) * 48, MODEL_WIDTH), BF16),
        ],
        compiler_params=pltpu.CompilerParams(vmem_limit_bytes=56 * MEBI),
        cost_estimate=cost(16 * 10**9, 30 * MEBI),
        name="attention_forward",
    )(
        start,
        count,
        numbers,
        jnp.array(panel_of_block()[::2]),
        label_row,
        label_column,
        projected,
        projected,
        projected,
        *sources,
    )


def attention_backward_kernel(
    tile,
    key_tile,
    start_ref,
    count_ref,
    row_ref,
    column_ref,
    q_ref,
    k_ref,
    v_ref,
    d_ref,
    log_ref,
    *refs,
):
    out_ref, sum_ref, kt_ref, dk_ref, dv_ref = refs[-5:]
    groups = q_ref.shape[1] // LANES
    factor = HEAD_SIZE**-0.5
    kt_ref[...] = k_ref[...].T
    dk_ref[...] = jnp.zeros_like(dk_ref)
    dv_ref[...] = jnp.zeros_like(dv_ref)
    low = low_lanes(tile)

    def run(rows, keys):
        same = column_ref[keys, :] == row_ref[:, rows]
        for group in range(groups):
            lanes = slice(group * LANES, (group + 1) * LANES)
            queries = q_ref[rows, lanes] * jnp.bfloat16(factor)
            upstream = d_ref[rows, lanes]
            d_queries = []
            d_keys = d_values = 0.0
            for part in range(2):
                mask = low if part == 0 else ~low
                chosen = jnp.where(mask, queries, jnp.zeros_like(queries))
                d_chosen = jnp.where(mask, upstream, jnp.zeros_like(upstream))
                scores = dot(k_ref[keys, lanes], chosen, ((1,), (1,)))
                exponents = jnp.exp(scores - log_ref[group, part : part + 1, rows])
                probabilities = jnp.where(same, exponents, 0.0)
                d_probs = dot(v_ref[keys, lanes], d_chosen, ((1,), (1,)))
                inner = jnp.sum(probabilities * d_probs, axis=0, keepdims=True)
                d_scores = (probabilities * (d_probs - inner)).astype(BF16)
                d_values += dot(probabilities.astype(BF16), d_chosen)
                d_keys += dot(d_scores, chosen)
                first = group * LANES + part * HEAD_SIZE
                d_queries.append(dot(kt_ref[first : first + HEAD_SIZE, keys], d_scores))
            dk_ref[keys, lanes] += d_keys
            dv_ref[keys, lanes] += d_values
            out_ref[0, rows, lanes] = (jnp.concatenate(d_queries, axis=0).T * factor).astype(BF16)

    over_tiles(tile, key_tile, start_ref, count_ref, run)
    out_ref[1] = dk_ref[...].astype(BF16)
    out_ref[2] = dv_ref[...].astype(BF16)
    sum_ref[0:1, :] = jnp.sum(out_ref[0].astype(F32), axis=0, keepdims=True)
    sum_ref[1:2, :] = jnp.sum(out_ref[2].astype(F32), axis=0, keepdims=True)


def attention_backward(projected, tiles, label_row, label_column, d_attended, logs, first, others, groups=2):
    start, count = tiles
    width = groups * LANES
    steps = PAIRS // groups
    rows = ROW_POSITIONS
    return pl.pallas_call(
        functools.partial(attention_backward_kernel, *BACKWARD_TILES),
        grid_spec=pltpu.PrefetchScalarGridSpec(
            num_scalar_prefetch=2,
            grid=(1,),
            in_specs=[
                pl.BlockSpec((1, rows), lambda h, *_: (0, 0)),
                pl.BlockSpec((rows, 1), lambda h, *_: (0, 0)),
                pl.BlockSpec((rows, width), lambda h, *_: (0, first)),
                pl.BlockSpec((rows, width), lambda h, *_: (0, steps + first)),
                pl.BlockSpec((rows, width), lambda h, *_: (0, 2 * steps + first)),
                pl.BlockSpec((rows, width), lambda h, *_: (0, first)),
                pl.BlockSpec((groups, 8, rows), lambda h, *_: (first, 0, 0)),
            ]
            + [ANYWHERE] * len(others),
            out_specs=[
                pl.BlockSpec((3, rows, width), lambda h, *_: (0, 0, 0)),
                pl.BlockSpec((8, width), lambda h, *_: (0, 0)),
            ],
            scratch_shapes=[
                pltpu.VMEM((width, rows), BF16),
                pltpu.VMEM((rows, width), F32),
                pltpu.VMEM((rows, width), F32),
            ],
        ),
        out_shape=[
            jax.ShapeDtypeStruct((3, rows, width), BF16),
            jax.ShapeDtypeStruct((8, width), F32),
        ],
        compiler_params=pltpu.CompilerParams(vmem_limit_bytes=48 * MEBI),
        cost_estimate=cost(11 * 10**9, 6 * rows * MODEL_WIDTH),
        name="attention_backward",
    )(
        start,
        count,
        label_row,
        label_column,
        projected,
        projected,
        projected,
        d_attended,
        logs,
        *others,
    )


def mean(value):
    return jnp.sum(value, axis=1, keepdims=True) * (1.0 / MODEL_WIDTH)


def load_once(step, pairs, semaphores):
    copies = [pltpu.make_async_copy(source, held, semaphores.at[i]) for i, (source, held) in enumerate(pairs)]

    @pl.when(step == 0)
    def _():
        for copy in copies:
            copy.start()

    def wait(index):
        pl.when(step == 0)(copies[index].wait)

    return wait


def middle_kernel(
    head_ref,
    attended_ref,
    x_ref,
    piece0,
    piece1,
    piece2,
    piece3,
    vec_ref,
    sheet_ref,
    output_ref,
    normed_ref,
    activated_ref,
    d_before_ref,
    d_feed_ref,
    d_first_ref,
    d_branch_ref,
    d_attended_ref,
    sums_ref,
    out_weight,
    up_weight,
    down_weight,
    slope_ref,
    semaphores,
):
    width = MODEL_WIDTH
    step = pl.program_id(0)
    wait = load_once(
        step,
        [
            (sheet_ref.at[pl.ds(0, width), :], out_weight),
            (sheet_ref.at[pl.ds(width, FF), :], up_weight),
            (sheet_ref.at[pl.ds(width + FF, FF), :], down_weight),
        ],
        semaphores,
    )

    @pl.when(step == 0)
    def _():
        sums_ref[...] = jnp.zeros_like(sums_ref)

    def add_up(row, value):
        sums_ref[row : row + 1, :] += jnp.sum(value, axis=0, keepdims=True)

    def vector(row):
        return vec_ref[row : row + 1, :]

    wait(0)
    hidden = x_ref[...].astype(F32) + (dot(attended_ref[...], out_weight[...]) + vector(6))
    center = hidden - mean(hidden)
    first_scale = lax.rsqrt(mean(center * center) + NORM_EPSILON)
    first_normal = center * first_scale
    normed = first_normal * vector(0) + vector(1)
    normed_low = normed.astype(BF16)
    normed_ref[...] = normed_low
    wait(1)
    wait(2)
    feed_out = vector(7)
    for chunk in range(CHUNKS):
        part = slice(chunk * width, (chunk + 1) * width)
        before = dot(normed_low, up_weight[part, :]) + vector(8 + chunk)
        share = 0.5 + 0.5 * lax.erf(before * np.float32(np.sqrt(0.5)))
        density = jnp.exp(before * before * -0.5) * np.float32(1.0 / np.sqrt(2.0 * np.pi))
        slope_ref[:, part] = share + before * density
        activated = (before * share).astype(BF16)
        activated_ref[:, part] = activated
        feed_out = feed_out + dot(activated, down_weight[part, :])
    mixed = normed + feed_out
    center = mixed - mean(mixed)
    second_scale = lax.rsqrt(mean(center * center) + NORM_EPSILON)
    second_normal = center * second_scale
    output_ref[...] = (second_normal * vector(2) + vector(3)).astype(BF16)
    source = step ^ head_ref[0]
    upstream = jnp.where(source % 2 == 0, piece0[...], piece1[...])
    upstream = jnp.where(source < 2, upstream, jnp.where(source % 2 == 0, piece2[...], piece3[...]))
    upstream = upstream.astype(F32)
    add_up(2, upstream * second_normal)
    add_up(3, upstream)
    scaled = upstream * vector(2)
    d_mixed = second_scale * (scaled - mean(scaled) - second_normal * mean(scaled * second_normal))
    d_feed = d_mixed.astype(BF16)
    d_feed_ref[...] = d_feed
    add_up(7, d_feed.astype(F32))
    d_normed = d_mixed
    for chunk in range(CHUNKS):
        part = slice(chunk * width, (chunk + 1) * width)
        d_active = dot(d_feed, down_weight[part, :], ((1,), (1,)))
        d_before = (d_active * slope_ref[:, part]).astype(BF16)
        d_before_ref[:, part] = d_before
        add_up(8 + chunk, d_before.astype(F32))
        d_normed = d_normed + dot(d_before, up_weight[part, :], ((1,), (1,)))
    add_up(0, d_normed * first_normal)
    add_up(1, d_normed)
    scaled = d_normed * vector(0)
    d_first = first_scale * (scaled - mean(scaled) - first_normal * mean(scaled * first_normal))
    d_first_ref[...] = d_first
    d_branch = d_first.astype(BF16)
    d_branch_ref[...] = d_branch
    add_up(6, d_branch.astype(F32))
    d_attended_ref[...] = dot(d_branch, out_weight[...], ((1,), (1,))).astype(BF16)


def middle(attended, x, pieces, vectors, sheet):
    rows, width = x.shape
    tile = pieces[0].shape[0]
    by_tile = lambda columns: pl.BlockSpec((tile, columns), lambda i, *_: (i, 0))
    fixed = lambda count: pl.BlockSpec((count, width), lambda i, *_: (0, 0))
    outs = [(width, BF16), (width, BF16), (FF, BF16), (FF, BF16), (width, BF16), (width, F32)]
    outs += [(width, BF16), (width, BF16)]
    head = lax.axis_index("head").reshape(1).astype(jnp.int32)
    return pl.pallas_call(
        middle_kernel,
        grid_spec=pltpu.PrefetchScalarGridSpec(
            num_scalar_prefetch=1,
            grid=(rows // tile,),
            in_specs=[by_tile(width)] * 2 + [fixed(tile)] * 4 + [fixed(12), ANYWHERE],
            out_specs=[by_tile(columns) for columns, _ in outs] + [fixed(12)],
            scratch_shapes=[
                pltpu.VMEM((width, width), BF16),
                pltpu.VMEM((FF, width), BF16),
                pltpu.VMEM((FF, width), BF16),
                pltpu.VMEM((tile, FF), F32),
                pltpu.SemaphoreType.DMA((3,)),
            ],
        ),
        out_shape=[jax.ShapeDtypeStruct((rows, columns), dtype) for columns, dtype in outs]
        + [jax.ShapeDtypeStruct((12, width), F32)],
        compiler_params=pltpu.CompilerParams(vmem_limit_bytes=56 * MEBI),
        cost_estimate=cost(rows * width * (FF * 8 + width * 4), rows * width * 40),
        name="layer_middle",
    )(head, attended, x, *pieces, vectors, sheet)


def store_panels(value, core, kept_ref, sent_ref):
    for own in range(2):

        @pl.when(core == own)
        def _():
            for ref, half in ((kept_ref, own), (sent_ref, 1 - own)):
                for pair in range(2):
                    for quarter in range(4):
                        first = 2 * pair * B + quarter * 48 + half * 24
                        rows = [value[first : first + 24], value[first + B : first + B + 24]]
                        ref[quarter, pair] = jnp.concatenate(rows, axis=0).astype(BF16)


def gradient_kernel(pairs, core_ref, *refs):
    kept_ref, sent_ref = refs[-2:]
    step = pl.program_id(0)
    for low, high, left, rights in pairs:

        def run(left=refs[left], rights=[refs[right] for right in rights]):
            if len(rights) == 1:
                right = rights[0][...]
            else:
                right = jnp.concatenate([part[0] for part in rights], axis=1)
            store_panels(dot(left[...], right, ((0,), (0,))), core_ref[0], kept_ref, sent_ref)

        pl.when((step >= low) & (step < high))(run)


def gradient_call(steps, pairs, specs, values, name, others=()):
    core = (lax.axis_index("seq") % 2).reshape(1).astype(jnp.int32)
    shape = jax.ShapeDtypeStruct((4, 2 * steps, 48, MODEL_WIDTH), BF16)
    spec = pl.BlockSpec((4, 2, 48, MODEL_WIDTH), lambda i, *_: (0, i, 0, 0))
    return pl.pallas_call(
        functools.partial(gradient_kernel, pairs),
        grid_spec=pltpu.PrefetchScalarGridSpec(
            num_scalar_prefetch=1,
            grid=(steps,),
            in_specs=specs + [ANYWHERE] * len(others),
            out_specs=[spec, spec],
        ),
        out_shape=[shape, shape],
        compiler_params=pltpu.CompilerParams(vmem_limit_bytes=48 * MEBI),
        cost_estimate=cost(2 * ROW_POSITIONS * steps * MODEL_WIDTH**2, 4 * steps * MEBI),
        name=name,
    )(core, *values, *others)


FIXED_ROWS = pl.BlockSpec((ROW_POSITIONS, MODEL_WIDTH), lambda i, *_: (0, 0))
def feed_gradients(normed_low, d_before, activated, d_feed, others):
    pairs = [(0, CHUNKS, 0, [1]), (CHUNKS, 2 * CHUNKS, 2, [3])]
    moving = lambda first: pl.BlockSpec(
        (ROW_POSITIONS, MODEL_WIDTH), lambda i, *_: (0, jnp.clip(i - first, 0, CHUNKS - 1))
    )
    return gradient_call(
        2 * CHUNKS,
        pairs,
        [FIXED_ROWS, moving(0), moving(CHUNKS), FIXED_ROWS],
        (normed_low, d_before, activated, d_feed),
        "feed_gradients",
        others,
    )


def attention_gradients(x, attended, d_branch, d_projected, others):
    count = len(d_projected)
    pairs = [(0, 3, 0, list(range(3, 3 + count))), (3, 4, 1, [2])]
    third = lambda part: pl.BlockSpec(
        (1,) + part.shape[1:], lambda i, *_: (jnp.minimum(i, 2), 0, 0)
    )
    return gradient_call(
        CHUNKS,
        pairs,
        [FIXED_ROWS] * 3 + [third(part) for part in d_projected],
        (x, attended, d_branch) + tuple(d_projected),
        "attention_gradients",
        others,
    )


def input_gradient_kernel(count, sheet_ref, d_first_ref, *refs):
    parts, out_ref = refs[:count], refs[-1]
    value = d_first_ref[...]
    for third in range(3):
        weight = sheet_ref[third * MODEL_WIDTH : (third + 1) * MODEL_WIDTH, :]
        d_rows = jnp.concatenate([part[third] for part in parts], axis=1)
        value = value + dot(d_rows, weight, ((1,), (1,)))
    out_ref[...] = value.astype(BF16)


def input_gradient(d_projected, sheet, d_first, others, tile=512):
    rows = d_first.shape[0]
    by_tile = pl.BlockSpec((tile, MODEL_WIDTH), lambda i: (i, 0))
    return pl.pallas_call(
        functools.partial(input_gradient_kernel, len(d_projected)),
        grid=(rows // tile,),
        in_specs=[
            pl.BlockSpec((3 * MODEL_WIDTH, MODEL_WIDTH), lambda i: (0, 0), pipeline_mode=pl.Buffered(1)),
            by_tile,
        ]
        + [pl.BlockSpec((3, tile, part.shape[2]), lambda i: (0, i, 0)) for part in d_projected]
        + [ANYWHERE] * len(others),
        out_specs=by_tile,
        out_shape=jax.ShapeDtypeStruct((rows, MODEL_WIDTH), BF16),
        compiler_params=pltpu.CompilerParams(vmem_limit_bytes=48 * MEBI),
        cost_estimate=cost(6 * rows * MODEL_WIDTH**2, 14 * MEBI),
        name="input_gradient",
    )(sheet, d_first, *d_projected, *others)


def add_parts(*parts):
    return functools.reduce(jnp.add, [part.astype(F32) for part in parts]).astype(BF16)


def pick(value, index, axis=0):
    return lax.dynamic_index_in_dim(value, index, axis, keepdims=False)


def head_first_parts(*terms):
    head = lax.axis_index("head")
    x, y = head % 2, head // 2
    cut = terms[0].shape[1] // 2
    squares = [term.reshape((2, 2) + term.shape[1:]) for term in terms]
    first = lambda index: add_parts(*[pick(square[:, :, :cut], index, 1) for square in squares])
    second = lambda index: add_parts(*[pick(square[:, :, cut:], index, 0) for square in squares])
    return (first(1 - x), second(1 - y)), (first(x), second(y))


def head_first_send(sent):
    return permute_xor(sent[0], "head", 1), permute_xor(sent[1], "head", 2)


def head_second_parts(kept, arrived):
    head = lax.axis_index("head")
    x, y = head % 2, head // 2
    first, second = zip(kept, arrived)
    part = lambda terms, index: add_parts(*[pick(term, index) for term in terms])
    return (part(first, 1 - y), part(second, 1 - x)), (part(first, y), part(second, x))


def head_second_send(sent):
    return permute_xor(sent[0], "head", 2), permute_xor(sent[1], "head", 1)


def add_pairs(kept, arrived):
    return [add_parts(one, two) for one, two in zip(kept, arrived)]


TOGETHER = 4
BUNDLE = TOGETHER * 36


def owned_kernel(panel_ref, lane_ref, odd_ref, sheet_ref, carried_ref, out_ref, carried_out):
    del carried_ref, carried_out
    first = pl.program_id(0) * out_ref.shape[0] * TOGETHER
    half = low_lanes(24)

    def bundle(place, carry):
        mains, rests = [], []
        for index in range(TOGETHER):
            slot = first + place * TOGETHER + index
            panel, odd = panel_ref[slot], odd_ref[slot] == 1
            pair = panel // 2
            lane = pl.multiple_of(lane_ref[slot], LANES)
            main_lane = pl.multiple_of(lane + jnp.where(odd, 2 * LANES, 0), LANES)
            values = []
            for begin in (main_lane, pl.multiple_of(lane + LANES, LANES)):
                value = sheet_ref[pair, :, pl.ds(begin, LANES)].astype(F32)
                values.append(jnp.where(panel % 2 == 1, value[24:], value[:24]))
            mains.append(values[0])
            turn = odd if index % 2 == 0 else jnp.logical_not(odd)
            rests.append(jnp.where(turn, pltpu.roll(values[1], LANES // 2, 1), values[1]))
        rests = [jnp.where(half, rests[i], rests[i + 1]) for i in range(0, TOGETHER, 2)]
        out_ref[place] = jnp.concatenate(mains + rests, axis=0).astype(BF16)
        return carry

    lax.fori_loop(0, out_ref.shape[0], bundle, 0, unroll=2)


def by_owner(sheet_gradient, owner_order, carried):
    owners = lax.axis_size("seq")
    count = NBLK // owners
    bundles = -(-count // TOGETHER)
    slots = jnp.pad(owner_order.reshape(owners, count), ((0, 0), (0, bundles * TOGETHER - count)))
    slots = slots.reshape(-1)
    steps = 4 if owners * bundles % 4 == 0 else 1
    each = owners * bundles // steps
    panels = jnp.asarray(panel_of_block())
    whole = jnp.arange(NBLK, dtype=jnp.int32)
    panels = jnp.sum(jnp.where(slots[:, None] == whole[None, :], panels[None, :], 0), axis=1)
    gathered, carried = pl.pallas_call(
        owned_kernel,
        grid_spec=pltpu.PrefetchScalarGridSpec(
            num_scalar_prefetch=3,
            grid=(steps,),
            in_specs=[pl.BlockSpec(sheet_gradient.shape, lambda i, *_: (0, 0, 0)), ANYWHERE],
            out_specs=[pl.BlockSpec((each, BUNDLE, LANES), lambda i, *_: (i, 0, 0)), ANYWHERE],
        ),
        out_shape=[
            jax.ShapeDtypeStruct((owners * bundles, BUNDLE, LANES), BF16),
            jax.ShapeDtypeStruct(carried.shape, carried.dtype),
        ],
        input_output_aliases={4: 1},
        compiler_params=pltpu.CompilerParams(vmem_limit_bytes=24 * MEBI),
        cost_estimate=cost(0, 4 * MEBI),
        name="gradients_by_owner",
    )(panels, slots // 2 % 2 * 384, slots % 2, sheet_gradient, carried)
    return gathered.reshape(owners // 2, 2, bundles, BUNDLE, LANES), carried


def add_tree(terms):
    while len(terms) > 1:
        terms = [one + two for one, two in zip(terms[::2], terms[1::2])]
    return terms[0]


def two_parts(value):
    high = lax.reduce_precision(value, 8, 7)
    return high, lax.reduce_precision(value - high, 8, 7)


def sum_to_owners(parts, sums, others):
    chips = lax.axis_size("seq") // 2
    seq = lax.axis_index("seq")
    chip, core = seq // 2, seq % 2
    shape = parts.shape[2:]
    flat = lambda value: value.reshape((-1,) + shape[1:])

    def with_sums(value, total):
        high, low = two_parts(total)
        both = jnp.concatenate([high, low]).astype(BF16)
        return jnp.concatenate([flat(value), flat(both)])

    def split_sums(value):
        high, low = value[-1].astype(F32).reshape((2,) + sums.shape)
        return value[:-1], high + low

    packed = flat if sums is None else functools.partial(with_sums, total=sums)
    arrived = [packed(pick(parts, chip))]
    for mask in range(1, chips):
        arrived.append(permute_xor(packed(pick(parts, chip ^ mask)), "seq", 2 * mask))
    if others:
        arrived[1:] = gate(arrived[1:], others)
    if sums is not None:
        split = [split_sums(value) for value in arrived]
        arrived = [value for value, _ in split]
        sums = add_tree([total for _, total in split])
    mine = add_parts(*arrived).reshape((2,) + shape)
    packed = flat if sums is None else functools.partial(with_sums, total=sums)
    other = permute_xor(packed(pick(mine, 1 - core)), "seq", 1)
    if sums is not None:
        other, total = split_sums(other)
        high, low = two_parts(sums)
        sums = (high + low) + total
    return jnp.stack([pick(mine, core), other.reshape(shape)]), sums


def gather_quarters(part):
    return [part] + [permute_xor(part, "head", mask) for mask in (1, 2, 3)]


def shampoo_kernel(
    base,
    held,
    number_ref,
    place_ref,
    part0,
    part1,
    part2,
    part3,
    momentum_ref,
    left_ref,
    right_ref,
    root_left_ref,
    root_right_ref,
    master_ref,
    *refs,
):
    new_momentum_ref, new_left_ref, new_right_ref, new_master_ref, main_ref, rest_ref = refs[held:]
    count = momentum_ref.shape[0]
    first = (base + pl.program_id(0)) * count
    low = low_lanes(B)
    half = low_lanes(24)
    core = place_ref[4]
    for slot in range(count):
        odd = number_ref[first + slot] % 2 == 1
        for index, part in enumerate((part0, part1, part2, part3)):
            for which in range(2):
                row = pl.multiple_of(place_ref[index] * 48 + (which ^ core) * 24, 8)
                bundle = part[which, slot // TOGETHER].astype(F32)
                inside = slot % TOGETHER
                main_ref[pl.ds(row, 24), :] = bundle[inside * 24 : inside * 24 + 24]
                begin = TOGETHER * 24 + inside // 2 * 24
                rest_ref[pl.ds(row, 24), :] = bundle[begin : begin + 24]
        main = main_ref[...]
        rest = rest_ref[...]
        spun = pltpu.roll(main, LANES // 2, 1)
        rest_low = rest if slot % 2 == 0 else pltpu.roll(rest, LANES // 2, 1)
        left_lanes = jnp.where(odd, jnp.where(low, rest_low, spun), main)
        right_lanes = jnp.where(odd, spun, rest_low)
        gradient = jnp.concatenate([left_lanes, right_lanes[:, : LANES // 2]], axis=1)
        new_momentum = MOMENTUM_DECAY * momentum_ref[slot] + (1.0 - MOMENTUM_DECAY) * gradient
        new_momentum_ref[slot] = new_momentum
        grad_low = gradient.astype(BF16)
        new_left_ref[slot] = STAT_DECAY * left_ref[slot] + (1.0 - STAT_DECAY) * dot(
            grad_low, grad_low, ((1,), (1,))
        )
        new_right_ref[slot] = STAT_DECAY * right_ref[slot] + (1.0 - STAT_DECAY) * dot(
            grad_low, grad_low, ((0,), (0,))
        )
        leftward = dot(root_left_ref[slot].astype(BF16), new_momentum.astype(BF16))
        preconditioned = dot(leftward.astype(BF16), root_right_ref[slot].astype(BF16))
        master = master_ref[slot]
        new_master_ref[slot] = master - MATRIX_RATE * (preconditioned + WEIGHT_DECAY * master)


def shampoo(numbers, parts, states, first, earlier, others):
    group = TOGETHER if numbers.shape[0] % TOGETHER == 0 else numbers.shape[0]
    steps = parts[0].shape[1]
    base = first // group
    spec = pl.BlockSpec((group, B, B), lambda i, *_: (base + i, 0, 0))
    part_spec = pl.BlockSpec((2, 1, BUNDLE, LANES), lambda i, *_: (0, i, 0, 0))
    places = lax.axis_index("head") ^ jnp.arange(4, dtype=jnp.int32)
    places = jnp.concatenate([places, (lax.axis_index("seq") % 2).reshape(1).astype(jnp.int32)])
    return pl.pallas_call(
        functools.partial(shampoo_kernel, base, len(earlier) + len(others)),
        grid_spec=pltpu.PrefetchScalarGridSpec(
            num_scalar_prefetch=2,
            grid=(steps,),
            in_specs=[part_spec] * 4
            + [spec] * 6
            + [ANYWHERE] * (len(earlier) + len(others)),
            out_specs=[spec] * 4,
            scratch_shapes=[pltpu.VMEM((B, LANES), F32), pltpu.VMEM((B, LANES), F32)],
        ),
        out_shape=[jax.ShapeDtypeStruct((numbers.shape[0], B, B), F32)] * 4,
        input_output_aliases={12 + i: i for i in range(len(earlier))},
        compiler_params=pltpu.CompilerParams(vmem_limit_bytes=48 * MEBI),
        cost_estimate=cost(8 * steps * group * B**3, 10 * steps * group * B * B * 4),
        name="shampoo_blocks",
    )(numbers, places, *parts, *states, *earlier, *others)


def adam_step(vector_grad, vec_first, vec_second, vectors):
    new_first = FIRST_DECAY * vec_first + (1.0 - FIRST_DECAY) * vector_grad
    new_second = SECOND_DECAY * vec_second + (1.0 - SECOND_DECAY) * vector_grad * vector_grad
    corrected_first = new_first / (1.0 - FIRST_DECAY**STEP)
    corrected_second = new_second / (1.0 - SECOND_DECAY**STEP)
    new_vectors = vectors - VECTOR_RATE * corrected_first / (
        jnp.sqrt(corrected_second) + ADAM_EPSILON
    )
    return (new_first, new_second, new_vectors)


def exchange_rows(value):
    return lax.all_to_all(value, "head", split_axis=0, concat_axis=0, tiled=True)


def parts_to_send(value):
    head = lax.axis_index("head")
    return [pick(value, head ^ mask) for mask in (1, 2, 3)]


def send_rows(parts):
    return [permute_xor(part, "head", mask) for mask, part in enumerate(parts, 1)]


def arrange_rows(value, arrived):
    head = lax.axis_index("head")
    result = value
    for mask, piece in enumerate(arrived, 1):
        result = lax.dynamic_update_index_in_dim(result, piece, head ^ mask, 0)
    return result


def local(
    tokens,
    cotangent,
    segment_ids,
    owner_order,
    master_blocks,
    momentum,
    stat_left,
    stat_right,
    root_left,
    root_right,
    vectors,
    vec_first,
    vec_second,
):
    width = MODEL_WIDTH
    count = master_blocks.shape[0]
    head = lax.axis_index("head")
    numbers = lax.dynamic_slice_in_dim(owner_order, lax.axis_index("seq") * count, count, 0)
    sheet_vectors = vectors.reshape(12, width)

    labels = lax.dynamic_index_in_dim(segment_ids, head, 0, keepdims=False)
    early = [sheet_vectors, labels.reshape(1, -1), labels.reshape(-1, 1)]
    early += [*key_tiles(labels, *FORWARD_TILES), *key_tiles(labels, *BACKWARD_TILES)]
    early += [exchange_rows(tokens).reshape(ROW_POSITIONS, width)]
    packed = pack_blocks(numbers, master_blocks)
    blocks, source_numbers, early = gather_weights(packed, owner_order, early)
    sheet_vectors, label_row, label_column = early[:3]
    wide_tiles, tiles, x = early[3:5], early[5:7], early[7]
    upstream = [pick(cotangent, head), *send_rows(parts_to_send(cotangent))]

    projected, input_sheet = project(x, sheet_vectors, blocks, source_numbers)
    attended, logs, sheet = attention_forward(
        projected, wide_tiles, label_row, label_column, blocks, source_numbers
    )
    upstream[1:] = gate(upstream[1:], [attended])
    (
        output,
        normed_low,
        activated,
        d_before,
        d_feed,
        d_first,
        d_branch,
        d_attended,
        sums,
    ) = middle(attended, x, upstream, sheet_vectors, sheet)
    def backward(index, *others):
        return attention_backward(
            projected, tiles, label_row, label_column, d_attended, logs, index, others
        )

    output = output.reshape(tokens.shape)
    output_sent = parts_to_send(output)
    feed, feed_sent = feed_gradients(normed_low, d_before, activated, d_feed, [])
    parts = [backward(0, feed, feed_sent, *output_sent)]
    feed = add_parts(feed, *gate([permute_xor(feed_sent, "seq", 1)], parts[0][:1]))
    feed_sent, feed = head_first_parts(feed)
    output_arrived = gate(send_rows(output_sent), feed_sent)
    parts.append(backward(1, parts[0][0], *feed_sent, *output_arrived))
    parts.append(backward(2, parts[1][0]))
    feed_sent, feed = head_second_parts(feed, gate(head_first_send(feed_sent), parts[2][:1]))
    d_projected = [part[0] for part in parts]
    rest, rest_sent = attention_gradients(x, attended, d_branch, d_projected, feed_sent)
    feed = jnp.concatenate(add_pairs(feed, gate(head_second_send(feed_sent), [rest])))
    rest_sent, rest = head_first_parts(
        rest, *gate([permute_xor(rest_sent, "seq", 1)], [feed])
    )
    bias_sums = jnp.concatenate([part[1] for part in parts], axis=1)
    sums = jnp.concatenate([sums[:4], bias_sums[:2], sums[6:]])
    input_grad = input_gradient(d_projected, input_sheet, d_first, rest_sent)
    arrived = [permute_xor(sums, "head", mask) for mask in (1, 2, 3)]
    sums = add_tree([sums, *gate(arrived, [input_grad])])
    rest_sent, rest = head_second_parts(rest, gate(head_first_send(rest_sent), [input_grad]))
    rest = jnp.concatenate(add_pairs(rest, head_second_send(rest_sent)))
    owned, input_grad = by_owner(jnp.concatenate([rest, feed]), owner_order, input_grad)
    input_grad = exchange_rows(input_grad.reshape(tokens.shape))
    output = arrange_rows(output, output_arrived)
    bundles = owned.shape[2]
    halves = 2 if bundles % 2 == 0 else 1
    each = bundles // halves
    states = (momentum, stat_left, stat_right, root_left, root_right, master_blocks)
    if halves == 1:
        part, total = sum_to_owners(owned, sums, [])
        blocks = shampoo(numbers, gather_quarters(part), states, 0, (), [])
        input_grad = input_grad.astype(F32)
    else:
        part, _ = sum_to_owners(owned[:, :, :each], None, [])
        quarters = gather_quarters(part)
        part, total = sum_to_owners(owned[:, :, each:], sums, [*quarters[1:], input_grad])
        input_grad = input_grad.astype(F32)
        blocks = shampoo(numbers, quarters, states, 0, (), [part])
        quarters = gather_quarters(part)
        blocks = shampoo(numbers, quarters, states, each * TOGETHER, blocks, [input_grad, output])
    new_first, new_second, new_vectors = adam_step(total.reshape(-1), vec_first, vec_second, vectors)

    new_momentum, new_left, new_right, new_master = blocks
    return (
        output,
        input_grad,
        new_momentum,
        new_left,
        new_right,
        new_master,
        new_first,
        new_second,
        new_vectors,
    )


def solution(mesh):
    blocks = P("seq", None, None)
    positions = P("seq", "head", None)
    return jax.shard_map(
        local,
        mesh=mesh,
        in_specs=(positions, positions, P("seq", None), P()) + (blocks,) * 6 + (P(),) * 3,
        out_specs=(positions, positions) + (blocks,) * 4 + (P(),) * 3,
        check_vma=False,
    )
```

```python
import functools

import jax
import jax.numpy as jnp
import numpy as np
from jax import lax
from jax.experimental import pallas as pl
from jax.experimental.pallas import tpu as pltpu
from jax.sharding import PartitionSpec as P

MODEL_WIDTH = 768
HEAD_TOTAL = 12
HEAD_SIZE = 64
FF = 3072
ROW_POSITIONS = 1024
B = 192
STEP = 10
NBLK = 192
PAIRS = HEAD_TOTAL // 2
LANES = 128
REST = B * B // LANES
QUARTER = REST // 4
CHUNKS = FF // MODEL_WIDTH
MEBI = 2**20

NORM_EPSILON = 1e-05
STAT_DECAY = 0.5
MOMENTUM_DECAY = 0.5
MATRIX_RATE = 1.0
WEIGHT_DECAY = 0.01
FIRST_DECAY = 0.9
SECOND_DECAY = 0.999
VECTOR_RATE = 0.3
ADAM_EPSILON = 1e-08

F32 = jnp.float32
BF16 = jnp.bfloat16
STARTS = (0, 48, 64, 128, 192)


def panel_of_block():
    panels = []
    for block in range(NBLK):
        if block < STARTS[1]:
            panels.append((block % 12) // 4 * 4 + block // 12)
        elif block < STARTS[2]:
            panels.append(12 + (block - STARTS[1]) // 4)
        elif block < STARTS[3]:
            inner = block - STARTS[2]
            panels.append(16 + (inner % 16) // 4 * 4 + inner // 16)
        else:
            panels.append(32 + (block - STARTS[3]) // 4)
    return np.array(panels, np.int32)


def cost(flops, moved, transcendentals=0):
    return pl.CostEstimate(flops=flops, bytes_accessed=moved, transcendentals=transcendentals)


def dot(left, right, contract=((1,), (0,))):
    return lax.dot_general(left, right, (contract, ((), ())), preferred_element_type=F32)


def low_lanes(rows):
    return lax.broadcasted_iota(jnp.int32, (rows, LANES), 1) < LANES // 2


def pack_kernel(order_ref, blocks_ref, packed_ref):
    count = blocks_ref.shape[0]
    first = pl.program_id(0) * count
    half = low_lanes(B // 2)
    low = low_lanes(B)
    for slot in range(count):
        left = blocks_ref[slot, :, :LANES]
        narrow = blocks_ref[slot, :, LANES:]
        right = jnp.concatenate([narrow, narrow], axis=1)
        turned = pltpu.roll(left, LANES // 2, 1)
        odd = order_ref[first + slot] % 2 == 1
        main = jnp.where(odd, jnp.where(low, turned, right), left)
        even_rest = jnp.where(half, right[: B // 2], right[B // 2 :])
        odd_rest = jnp.where(half, left[B // 2 :], turned[: B // 2])
        packed_ref[slot, :B, :] = main.astype(BF16)
        packed_ref[slot, B:, :] = jnp.where(odd, odd_rest, even_rest).astype(BF16)


def pack_blocks(order, blocks):
    count = blocks.shape[0]
    group = max(size for size in range(1, 7) if count % size == 0)
    return pl.pallas_call(
        pack_kernel,
        grid_spec=pltpu.PrefetchScalarGridSpec(
            num_scalar_prefetch=1,
            grid=(count // group,),
            in_specs=[pl.BlockSpec((group, B, B), lambda i, *_: (i, 0, 0))],
            out_specs=pl.BlockSpec((group, REST, LANES), lambda i, *_: (i, 0, 0)),
        ),
        out_shape=jax.ShapeDtypeStruct((count, REST, LANES), BF16),
        cost_estimate=cost(0, count * B * B * 6),
        name="pack_weight_blocks",
    )(order, blocks)


def permute_xor(value, axis, mask):
    size = lax.axis_size(axis)
    return lax.ppermute(value, axis, [(i, i ^ mask) for i in range(size)])


def gate_kernel(*refs):
    del refs


def gate(values, others):
    flat = list(values)
    shapes = [jax.ShapeDtypeStruct(value.shape, value.dtype) for value in flat]
    return pl.pallas_call(
        gate_kernel,
        in_specs=[ANYWHERE] * (len(flat) + len(others)),
        out_specs=[ANYWHERE] * len(flat),
        out_shape=shapes,
        input_output_aliases={i: i for i in range(len(flat))},
        cost_estimate=cost(0, 0),
        name="gate",
    )(*flat, *others)


ANYWHERE = pl.BlockSpec(memory_space=pl.ANY)


def gathered_slots(heads, chips, count):
    size, cut = count // heads, count // heads // 2
    slots = np.zeros((heads, chips, 2, NBLK), np.int32)
    for head in range(heads):
        for chip in range(chips):
            places = [(chip, slot) for slot in range(count)]
            for kinds in GROUP_KINDS:
                for mask in range(heads):
                    for chip_mask, half in kinds:
                        begin = (head ^ mask) * size + half * cut
                        places += [(chip ^ chip_mask, begin + slot) for slot in range(cut)]
            for core in range(2):
                slots[head, chip, core] = [
                    (c * 2 + which) * count + slot for which in (core, 1 - core) for c, slot in places
                ]
    return slots


GROUP_KINDS = (((1, 0), (1, 1)), ((2, 0), (3, 0)), ((2, 1), (3, 1)))


def gather_weights(packed, owner_order, early):
    heads = lax.axis_size("head")
    chips = lax.axis_size("seq") // 2
    count = packed.shape[0]
    head = lax.axis_index("head")
    seq = lax.axis_index("seq")
    chip, core = seq // 2, seq % 2
    if count % (2 * heads) or chips != 4:
        return [lax.all_gather(packed, "seq", axis=0, tiled=True)], owner_order, early
    size = count // heads
    cut = size // 2
    slots = jnp.asarray(gathered_slots(heads, chips, count).reshape(-1, NBLK))
    slots = lax.dynamic_index_in_dim(slots, (head * chips + chip) * 2 + core, 0, keepdims=False)
    whole = jnp.arange(NBLK, dtype=jnp.int32)
    numbers = jnp.sum(jnp.where(slots[:, None] == whole[None, :], owner_order[None, :], 0), axis=1)
    own = lax.dynamic_slice_in_dim(packed, head * size, size, 0)
    halves = own[:cut], own[cut:]
    over_z = lambda half, mask: permute_xor(half, "seq", 2 * mask)
    def first_hop(first, second):
        return [
            permute_xor(first, "head", 1),
            permute_xor(second, "head", 2),
            permute_xor(second, "head", 1),
            permute_xor(first, "head", 2),
        ]

    def second_hop(first_x, second_y, *_):
        return [permute_xor(first_x, "head", 2), permute_xor(second_y, "head", 1)]

    def swap_cores(pieces):
        return [permute_xor(piece, "seq", 1) for piece in pieces]

    def arranged(pieces, one, two):
        first_x, second_y, second_x, first_y = one
        return [*pieces, first_x, second_x, first_y, second_y, *two]

    near = [over_z(half, 1) for half in halves]
    halfway = [over_z(halves[0], 2), over_z(halves[0], 3)]
    swapped = swap_cores([packed])
    *near, late = gate([*near, halves[1]], [*swapped, numbers, *early[:-1]])
    near_one = first_hop(*near)
    last = [over_z(late, 2), over_z(late, 3)]
    gated = gate([*near_one[:2], *halfway], near_one[2:])
    near_one[:2], halfway = gated[:2], gated[2:]
    near_two = second_hop(*near_one)
    halfway_one = first_hop(*halfway)
    gated = gate([*halfway_one[:2], *last], [*halfway_one[2:], *near_two, early[-1]])
    halfway_one[:2], last = gated[:2], gated[2:]
    halfway_two = second_hop(*halfway_one)
    last_one = first_hop(*last)
    last_one[:2] = gate(last_one[:2], [*last_one[2:], *halfway_two])
    last_two = second_hop(*last_one)
    mine = [
        jnp.concatenate(arranged(near, near_one, near_two)),
        jnp.concatenate(arranged(halfway, halfway_one, halfway_two)),
        jnp.concatenate(arranged(last, last_one, ())),
        *last_two,
    ]
    return [packed, *mine, *swapped, *swap_cores(mine)], numbers, early


LOW_GROUP = (STARTS[0], STARTS[1])
HIGH_GROUP = (STARTS[1], STARTS[4])


def fetch_blocks(number_ref, sources, blocks, arrive, group):
    low, high = group
    first = 0
    for source in sources:

        def start(place, carry, source=source, first=first):
            number = number_ref[first + place]

            @pl.when((number >= low) & (number < high))
            def _():
                pltpu.make_async_copy(source.at[place], blocks.at[number - low], arrive).start()

            return carry

        count = source.shape[0]
        lax.fori_loop(0, count, start, 0, unroll=min(count, 4))
        first += count


def lay_out_blocks(panel_ref, blocks, sheet, group, begin, end):
    low = group[0]
    half = low_lanes(B // 2)

    def lay_out(index, carry):
        pair = low // 2 + index
        row = pl.multiple_of((panel_ref[pair] - low // 4) * B, B)
        lane = pl.multiple_of((pair % 2) * 384, LANES)
        even, odd = 2 * index, 2 * index + 1
        sheet[pl.ds(row, B), pl.ds(lane, LANES)] = blocks[even, :B, :]
        sheet[pl.ds(row, B), pl.ds(lane + 2 * LANES, LANES)] = blocks[odd, :B, :]
        even_rest = blocks[even, B:, :].astype(F32)
        odd_rest = blocks[odd, B:, :].astype(F32)
        turned = pltpu.roll(jnp.where(half, odd_rest, even_rest), LANES // 2, 1)
        center = jnp.concatenate([jnp.where(half, even_rest, odd_rest), turned], axis=0)
        sheet[pl.ds(row, B), pl.ds(lane + LANES, LANES)] = center.astype(BF16)
        return carry

    lax.fori_loop(begin, end, lay_out, 0, unroll=8)


def group_scratch(group):
    count = group[1] - group[0]
    return [
        pltpu.VMEM((count * 48, MODEL_WIDTH), BF16),
        pltpu.VMEM((count, REST, LANES), BF16),
        pltpu.SemaphoreType.DMA,
        pltpu.SemaphoreType.DMA,
    ]


def project_kernel(
    number_ref, panel_ref, x_ref, vec_ref, *refs
):
    sources = refs[:-6]
    projected_ref, sheet_out, sheet, blocks, arrive, leave = refs[-6:]
    fetch_blocks(number_ref, sources, blocks, arrive, LOW_GROUP)
    pltpu.make_async_copy(blocks, blocks, arrive).wait()
    lay_out_blocks(panel_ref, blocks, sheet, LOW_GROUP, 0, blocks.shape[0] // 2)
    copy = pltpu.make_async_copy(sheet, sheet_out, leave)
    copy.start()
    for panel in range(3):
        weight = sheet[panel * MODEL_WIDTH : (panel + 1) * MODEL_WIDTH, :]
        for tile in range(x_ref.shape[0] // 512):
            rows = slice(tile * 512, (tile + 1) * 512)
            value = dot(x_ref[rows, :], weight)
            if panel != 1:
                value = value + vec_ref[4 + panel // 2 : 5 + panel // 2, :]
            projected_ref[rows, panel * MODEL_WIDTH : (panel + 1) * MODEL_WIDTH] = value.astype(BF16)
    copy.wait()


def project(x, vectors, sources, numbers):
    rows = x.shape[0]
    whole = lambda shape: pl.BlockSpec(shape, lambda i, *_: (0,) * len(shape))
    anywhere = pl.BlockSpec(memory_space=pl.ANY)
    return pl.pallas_call(
        project_kernel,
        grid_spec=pltpu.PrefetchScalarGridSpec(
            num_scalar_prefetch=2,
            grid=(1,),
            in_specs=[whole(x.shape), whole(vectors.shape)] + [anywhere] * len(sources),
            out_specs=[whole((rows, 3 * MODEL_WIDTH)), anywhere],
            scratch_shapes=group_scratch(LOW_GROUP),
        ),
        out_shape=[
            jax.ShapeDtypeStruct((rows, 3 * MODEL_WIDTH), BF16),
            jax.ShapeDtypeStruct((STARTS[1] * 48, MODEL_WIDTH), BF16),
        ],
        compiler_params=pltpu.CompilerParams(vmem_limit_bytes=48 * MEBI),
        cost_estimate=cost(6 * rows * MODEL_WIDTH**2, 16 * MEBI),
        name="project_queries_keys_values",
    )(numbers, jnp.array(panel_of_block()[::2]), x, vectors, *sources)


FORWARD_TILES = (512, 256)
BACKWARD_TILES = (256, 128)


def key_tiles(labels, tile, key_tile):
    edges = labels.reshape(-1, tile)
    first, last = edges[:, 0], edges[:, -1]
    start = jnp.sum(labels[None, :] < first[:, None], axis=1, dtype=jnp.int32) // key_tile
    end = jnp.sum(labels[None, :] <= last[:, None], axis=1, dtype=jnp.int32)
    return start, (end + key_tile - 1) // key_tile - start


def over_tiles(tile, key_tile, start_ref, count_ref, run):
    def block(index, carry):
        rows = pl.ds(pl.multiple_of(index * tile, tile), tile)
        start = pl.multiple_of(start_ref[index] * key_tile, key_tile)
        for count in range(1, ROW_POSITIONS // key_tile + 1):
            keys = pl.ds(start, count * key_tile)
            pl.when(count_ref[index] == count)(functools.partial(run, rows, keys))
        return carry

    lax.fori_loop(0, ROW_POSITIONS // tile, block, 0)


def attention_forward_kernel(
    tile, key_tile, start_ref, count_ref, number_ref, panel_ref, row_ref, column_ref, q_ref, k_ref, v_ref, *refs
):
    sources = refs[:-8]
    out_ref, log_ref, sheet_out, vt_ref, sheet, blocks, arrive, leave = refs[-8:]
    groups = q_ref.shape[1] // LANES
    step, last = pl.program_id(0), pl.num_programs(0) - 1

    @pl.when(step == 0)
    def _():
        fetch_blocks(number_ref, sources, blocks, arrive, HIGH_GROUP)

    @pl.when(step == 1)
    def _():
        pltpu.make_async_copy(blocks, blocks, arrive).wait()
        lay_out_blocks(panel_ref, blocks, sheet, HIGH_GROUP, 0, blocks.shape[0] // 2)
        pltpu.make_async_copy(sheet, sheet_out, leave).start()

    vt_ref[...] = v_ref[...].T
    low = low_lanes(tile)

    def run(rows, keys):
        same = column_ref[keys, :] == row_ref[:, rows]
        for group in range(groups):
            lanes = slice(group * LANES, (group + 1) * LANES)
            queries = q_ref[rows, lanes] * jnp.bfloat16(HEAD_SIZE**-0.5)
            mixed = []
            for part in range(2):
                chosen = jnp.where(low if part == 0 else ~low, queries, jnp.zeros_like(queries))
                scores = dot(k_ref[keys, lanes], chosen, ((1,), (1,)))
                scores = jnp.where(same, scores, -1e30)
                peak = jnp.max(scores, axis=0, keepdims=True)
                exponents = jnp.exp(scores - peak)
                total = jnp.sum(exponents, axis=0, keepdims=True)
                probabilities = (exponents * (1.0 / total)).astype(BF16)
                first = group * LANES + part * HEAD_SIZE
                mixed.append(dot(vt_ref[first : first + HEAD_SIZE, keys], probabilities))
                log_ref[group, part : part + 1, rows] = peak + jnp.log(total)
            out_ref[rows, lanes] = jnp.concatenate(mixed, axis=0).T.astype(BF16)

    over_tiles(tile, key_tile, start_ref, count_ref, run)

    @pl.when(step == last)
    def _():
        pltpu.make_async_copy(sheet, sheet_out, leave).wait()


def attention_forward(projected, tiles, label_row, label_column, sources, numbers, groups=2):
    start, count = tiles
    width = groups * LANES
    steps = PAIRS // groups
    rows = ROW_POSITIONS
    anywhere = pl.BlockSpec(memory_space=pl.ANY)
    return pl.pallas_call(
        functools.partial(attention_forward_kernel, *FORWARD_TILES),
        grid_spec=pltpu.PrefetchScalarGridSpec(
            num_scalar_prefetch=4,
            grid=(steps,),
            in_specs=[
                pl.BlockSpec((1, rows), lambda h, *_: (0, 0)),
                pl.BlockSpec((rows, 1), lambda h, *_: (0, 0)),
                pl.BlockSpec((rows, width), lambda h, *_: (0, h)),
                pl.BlockSpec((rows, width), lambda h, *_: (0, steps + h)),
                pl.BlockSpec((rows, width), lambda h, *_: (0, 2 * steps + h)),
            ]
            + [anywhere] * len(sources),
            out_specs=[
                pl.BlockSpec((rows, width), lambda h, *_: (0, h)),
                pl.BlockSpec((groups, 8, rows), lambda h, *_: (h, 0, 0)),
                anywhere,
            ],
            scratch_shapes=[pltpu.VMEM((width, rows), BF16)] + group_scratch(HIGH_GROUP),
        ),
        out_shape=[
            jax.ShapeDtypeStruct((rows, MODEL_WIDTH), BF16),
            jax.ShapeDtypeStruct((PAIRS, 8, rows), F32),
            jax.ShapeDtypeStruct(((NBLK - STARTS[1]) * 48, MODEL_WIDTH), BF16),
        ],
        compiler_params=pltpu.CompilerParams(vmem_limit_bytes=56 * MEBI),
        cost_estimate=cost(16 * 10**9, 30 * MEBI),
        name="attention_forward",
    )(
        start,
        count,
        numbers,
        jnp.array(panel_of_block()[::2]),
        label_row,
        label_column,
        projected,
        projected,
        projected,
        *sources,
    )


def attention_backward_kernel(
    tile,
    key_tile,
    start_ref,
    count_ref,
    row_ref,
    column_ref,
    q_ref,
    k_ref,
    v_ref,
    d_ref,
    log_ref,
    *refs,
):
    out_ref, sum_ref, kt_ref, dk_ref, dv_ref = refs[-5:]
    groups = q_ref.shape[1] // LANES
    factor = HEAD_SIZE**-0.5
    kt_ref[...] = k_ref[...].T
    dk_ref[...] = jnp.zeros_like(dk_ref)
    dv_ref[...] = jnp.zeros_like(dv_ref)
    low = low_lanes(tile)

    def run(rows, keys):
        same = column_ref[keys, :] == row_ref[:, rows]
        for group in range(groups):
            lanes = slice(group * LANES, (group + 1) * LANES)
            queries = q_ref[rows, lanes] * jnp.bfloat16(factor)
            upstream = d_ref[rows, lanes]
            d_queries = []
            d_keys = d_values = 0.0
            for part in range(2):
                mask = low if part == 0 else ~low
                chosen = jnp.where(mask, queries, jnp.zeros_like(queries))
                d_chosen = jnp.where(mask, upstream, jnp.zeros_like(upstream))
                scores = dot(k_ref[keys, lanes], chosen, ((1,), (1,)))
                exponents = jnp.exp(scores - log_ref[group, part : part + 1, rows])
                probabilities = jnp.where(same, exponents, 0.0)
                d_probs = dot(v_ref[keys, lanes], d_chosen, ((1,), (1,)))
                inner = jnp.sum(probabilities * d_probs, axis=0, keepdims=True)
                d_scores = (probabilities * (d_probs - inner)).astype(BF16)
                d_values += dot(probabilities.astype(BF16), d_chosen)
                d_keys += dot(d_scores, chosen)
                first = group * LANES + part * HEAD_SIZE
                d_queries.append(dot(kt_ref[first : first + HEAD_SIZE, keys], d_scores))
            dk_ref[keys, lanes] += d_keys
            dv_ref[keys, lanes] += d_values
            out_ref[0, rows, lanes] = (jnp.concatenate(d_queries, axis=0).T * factor).astype(BF16)

    over_tiles(tile, key_tile, start_ref, count_ref, run)
    out_ref[1] = dk_ref[...].astype(BF16)
    out_ref[2] = dv_ref[...].astype(BF16)
    sum_ref[0:1, :] = jnp.sum(out_ref[0].astype(F32), axis=0, keepdims=True)
    sum_ref[1:2, :] = jnp.sum(out_ref[2].astype(F32), axis=0, keepdims=True)


def attention_backward(projected, tiles, label_row, label_column, d_attended, logs, first, others, groups=2):
    start, count = tiles
    width = groups * LANES
    steps = PAIRS // groups
    rows = ROW_POSITIONS
    return pl.pallas_call(
        functools.partial(attention_backward_kernel, *BACKWARD_TILES),
        grid_spec=pltpu.PrefetchScalarGridSpec(
            num_scalar_prefetch=2,
            grid=(1,),
            in_specs=[
                pl.BlockSpec((1, rows), lambda h, *_: (0, 0)),
                pl.BlockSpec((rows, 1), lambda h, *_: (0, 0)),
                pl.BlockSpec((rows, width), lambda h, *_: (0, first)),
                pl.BlockSpec((rows, width), lambda h, *_: (0, steps + first)),
                pl.BlockSpec((rows, width), lambda h, *_: (0, 2 * steps + first)),
                pl.BlockSpec((rows, width), lambda h, *_: (0, first)),
                pl.BlockSpec((groups, 8, rows), lambda h, *_: (first, 0, 0)),
            ]
            + [ANYWHERE] * len(others),
            out_specs=[
                pl.BlockSpec((3, rows, width), lambda h, *_: (0, 0, 0)),
                pl.BlockSpec((8, width), lambda h, *_: (0, 0)),
            ],
            scratch_shapes=[
                pltpu.VMEM((width, rows), BF16),
                pltpu.VMEM((rows, width), F32),
                pltpu.VMEM((rows, width), F32),
            ],
        ),
        out_shape=[
            jax.ShapeDtypeStruct((3, rows, width), BF16),
            jax.ShapeDtypeStruct((8, width), F32),
        ],
        compiler_params=pltpu.CompilerParams(vmem_limit_bytes=48 * MEBI),
        cost_estimate=cost(11 * 10**9, 6 * rows * MODEL_WIDTH),
        name="attention_backward",
    )(
        start,
        count,
        label_row,
        label_column,
        projected,
        projected,
        projected,
        d_attended,
        logs,
        *others,
    )


def mean(value):
    return jnp.sum(value, axis=1, keepdims=True) * (1.0 / MODEL_WIDTH)


def load_once(step, pairs, semaphores):
    copies = [pltpu.make_async_copy(source, held, semaphores.at[i]) for i, (source, held) in enumerate(pairs)]

    @pl.when(step == 0)
    def _():
        for copy in copies:
            copy.start()

    def wait(index):
        pl.when(step == 0)(copies[index].wait)

    return wait


def middle_kernel(
    head_ref,
    attended_ref,
    x_ref,
    piece0,
    piece1,
    piece2,
    piece3,
    vec_ref,
    sheet_ref,
    output_ref,
    normed_ref,
    activated_ref,
    d_before_ref,
    d_feed_ref,
    d_first_ref,
    d_branch_ref,
    d_attended_ref,
    sums_ref,
    out_weight,
    up_weight,
    down_weight,
    slope_ref,
    semaphores,
):
    width = MODEL_WIDTH
    step = pl.program_id(0)
    wait = load_once(
        step,
        [
            (sheet_ref.at[pl.ds(0, width), :], out_weight),
            (sheet_ref.at[pl.ds(width, FF), :], up_weight),
            (sheet_ref.at[pl.ds(width + FF, FF), :], down_weight),
        ],
        semaphores,
    )

    @pl.when(step == 0)
    def _():
        sums_ref[...] = jnp.zeros_like(sums_ref)

    def add_up(row, value):
        sums_ref[row : row + 1, :] += jnp.sum(value, axis=0, keepdims=True)

    def vector(row):
        return vec_ref[row : row + 1, :]

    wait(0)
    hidden = x_ref[...].astype(F32) + (dot(attended_ref[...], out_weight[...]) + vector(6))
    center = hidden - mean(hidden)
    first_scale = lax.rsqrt(mean(center * center) + NORM_EPSILON)
    first_normal = center * first_scale
    normed = first_normal * vector(0) + vector(1)
    normed_low = normed.astype(BF16)
    normed_ref[...] = normed_low
    wait(1)
    wait(2)
    feed_out = vector(7)
    for chunk in range(CHUNKS):
        part = slice(chunk * width, (chunk + 1) * width)
        before = dot(normed_low, up_weight[part, :]) + vector(8 + chunk)
        share = 0.5 + 0.5 * lax.erf(before * np.float32(np.sqrt(0.5)))
        density = jnp.exp(before * before * -0.5) * np.float32(1.0 / np.sqrt(2.0 * np.pi))
        slope_ref[:, part] = share + before * density
        activated = (before * share).astype(BF16)
        activated_ref[:, part] = activated
        feed_out = feed_out + dot(activated, down_weight[part, :])
    mixed = normed + feed_out
    center = mixed - mean(mixed)
    second_scale = lax.rsqrt(mean(center * center) + NORM_EPSILON)
    second_normal = center * second_scale
    output_ref[...] = (second_normal * vector(2) + vector(3)).astype(BF16)
    source = step ^ head_ref[0]
    upstream = jnp.where(source % 2 == 0, piece0[...], piece1[...])
    upstream = jnp.where(source < 2, upstream, jnp.where(source % 2 == 0, piece2[...], piece3[...]))
    upstream = upstream.astype(F32)
    add_up(2, upstream * second_normal)
    add_up(3, upstream)
    scaled = upstream * vector(2)
    d_mixed = second_scale * (scaled - mean(scaled) - second_normal * mean(scaled * second_normal))
    d_feed = d_mixed.astype(BF16)
    d_feed_ref[...] = d_feed
    add_up(7, d_feed.astype(F32))
    d_normed = d_mixed
    for chunk in range(CHUNKS):
        part = slice(chunk * width, (chunk + 1) * width)
        d_active = dot(d_feed, down_weight[part, :], ((1,), (1,)))
        d_before = (d_active * slope_ref[:, part]).astype(BF16)
        d_before_ref[:, part] = d_before
        add_up(8 + chunk, d_before.astype(F32))
        d_normed = d_normed + dot(d_before, up_weight[part, :], ((1,), (1,)))
    add_up(0, d_normed * first_normal)
    add_up(1, d_normed)
    scaled = d_normed * vector(0)
    d_first = first_scale * (scaled - mean(scaled) - first_normal * mean(scaled * first_normal))
    d_first_ref[...] = d_first
    d_branch = d_first.astype(BF16)
    d_branch_ref[...] = d_branch
    add_up(6, d_branch.astype(F32))
    d_attended_ref[...] = dot(d_branch, out_weight[...], ((1,), (1,))).astype(BF16)


def middle(attended, x, pieces, vectors, sheet):
    rows, width = x.shape
    tile = pieces[0].shape[0]
    by_tile = lambda columns: pl.BlockSpec((tile, columns), lambda i, *_: (i, 0))
    fixed = lambda count: pl.BlockSpec((count, width), lambda i, *_: (0, 0))
    outs = [(width, BF16), (width, BF16), (FF, BF16), (FF, BF16), (width, BF16), (width, F32)]
    outs += [(width, BF16), (width, BF16)]
    head = lax.axis_index("head").reshape(1).astype(jnp.int32)
    return pl.pallas_call(
        middle_kernel,
        grid_spec=pltpu.PrefetchScalarGridSpec(
            num_scalar_prefetch=1,
            grid=(rows // tile,),
            in_specs=[by_tile(width)] * 2 + [fixed(tile)] * 4 + [fixed(12), ANYWHERE],
            out_specs=[by_tile(columns) for columns, _ in outs] + [fixed(12)],
            scratch_shapes=[
                pltpu.VMEM((width, width), BF16),
                pltpu.VMEM((FF, width), BF16),
                pltpu.VMEM((FF, width), BF16),
                pltpu.VMEM((tile, FF), F32),
                pltpu.SemaphoreType.DMA((3,)),
            ],
        ),
        out_shape=[jax.ShapeDtypeStruct((rows, columns), dtype) for columns, dtype in outs]
        + [jax.ShapeDtypeStruct((12, width), F32)],
        compiler_params=pltpu.CompilerParams(vmem_limit_bytes=56 * MEBI),
        cost_estimate=cost(rows * width * (FF * 8 + width * 4), rows * width * 40),
        name="layer_middle",
    )(head, attended, x, *pieces, vectors, sheet)


def store_panels(value, core, kept_ref, sent_ref):
    for own in range(2):

        @pl.when(core == own)
        def _():
            for ref, half in ((kept_ref, own), (sent_ref, 1 - own)):
                for pair in range(2):
                    for quarter in range(4):
                        first = 2 * pair * B + quarter * 48 + half * 24
                        rows = [value[first : first + 24], value[first + B : first + B + 24]]
                        ref[quarter, pair] = jnp.concatenate(rows, axis=0).astype(BF16)


def gradient_kernel(pairs, core_ref, *refs):
    kept_ref, sent_ref = refs[-2:]
    step = pl.program_id(0)
    for low, high, left, rights in pairs:

        def run(left=refs[left], rights=[refs[right] for right in rights]):
            if len(rights) == 1:
                right = rights[0][...]
            else:
                right = jnp.concatenate([part[0] for part in rights], axis=1)
            store_panels(dot(left[...], right, ((0,), (0,))), core_ref[0], kept_ref, sent_ref)

        pl.when((step >= low) & (step < high))(run)


def gradient_call(steps, pairs, specs, values, name, others=()):
    core = (lax.axis_index("seq") % 2).reshape(1).astype(jnp.int32)
    shape = jax.ShapeDtypeStruct((4, 2 * steps, 48, MODEL_WIDTH), BF16)
    spec = pl.BlockSpec((4, 2, 48, MODEL_WIDTH), lambda i, *_: (0, i, 0, 0))
    return pl.pallas_call(
        functools.partial(gradient_kernel, pairs),
        grid_spec=pltpu.PrefetchScalarGridSpec(
            num_scalar_prefetch=1,
            grid=(steps,),
            in_specs=specs + [ANYWHERE] * len(others),
            out_specs=[spec, spec],
        ),
        out_shape=[shape, shape],
        compiler_params=pltpu.CompilerParams(vmem_limit_bytes=48 * MEBI),
        cost_estimate=cost(2 * ROW_POSITIONS * steps * MODEL_WIDTH**2, 4 * steps * MEBI),
        name=name,
    )(core, *values, *others)


FIXED_ROWS = pl.BlockSpec((ROW_POSITIONS, MODEL_WIDTH), lambda i, *_: (0, 0))
def feed_gradients(normed_low, d_before, activated, d_feed, others):
    pairs = [(0, CHUNKS, 0, [1]), (CHUNKS, 2 * CHUNKS, 2, [3])]
    moving = lambda first: pl.BlockSpec(
        (ROW_POSITIONS, MODEL_WIDTH), lambda i, *_: (0, jnp.clip(i - first, 0, CHUNKS - 1))
    )
    return gradient_call(
        2 * CHUNKS,
        pairs,
        [FIXED_ROWS, moving(0), moving(CHUNKS), FIXED_ROWS],
        (normed_low, d_before, activated, d_feed),
        "feed_gradients",
        others,
    )


def attention_gradients(x, attended, d_branch, d_projected, others):
    count = len(d_projected)
    pairs = [(0, 3, 0, list(range(3, 3 + count))), (3, 4, 1, [2])]
    third = lambda part: pl.BlockSpec(
        (1,) + part.shape[1:], lambda i, *_: (jnp.minimum(i, 2), 0, 0)
    )
    return gradient_call(
        CHUNKS,
        pairs,
        [FIXED_ROWS] * 3 + [third(part) for part in d_projected],
        (x, attended, d_branch) + tuple(d_projected),
        "attention_gradients",
        others,
    )


def input_gradient_kernel(count, sheet_ref, d_first_ref, *refs):
    parts, out_ref = refs[:count], refs[-1]
    value = d_first_ref[...]
    for third in range(3):
        weight = sheet_ref[third * MODEL_WIDTH : (third + 1) * MODEL_WIDTH, :]
        d_rows = jnp.concatenate([part[third] for part in parts], axis=1)
        value = value + dot(d_rows, weight, ((1,), (1,)))
    out_ref[...] = value.astype(BF16)


def input_gradient(d_projected, sheet, d_first, others, tile=512):
    rows = d_first.shape[0]
    by_tile = pl.BlockSpec((tile, MODEL_WIDTH), lambda i: (i, 0))
    return pl.pallas_call(
        functools.partial(input_gradient_kernel, len(d_projected)),
        grid=(rows // tile,),
        in_specs=[
            pl.BlockSpec((3 * MODEL_WIDTH, MODEL_WIDTH), lambda i: (0, 0), pipeline_mode=pl.Buffered(1)),
            by_tile,
        ]
        + [pl.BlockSpec((3, tile, part.shape[2]), lambda i: (0, i, 0)) for part in d_projected]
        + [ANYWHERE] * len(others),
        out_specs=by_tile,
        out_shape=jax.ShapeDtypeStruct((rows, MODEL_WIDTH), BF16),
        compiler_params=pltpu.CompilerParams(vmem_limit_bytes=48 * MEBI),
        cost_estimate=cost(6 * rows * MODEL_WIDTH**2, 14 * MEBI),
        name="input_gradient",
    )(sheet, d_first, *d_projected, *others)


def add_parts(*parts):
    return functools.reduce(jnp.add, [part.astype(F32) for part in parts]).astype(BF16)


def pick(value, index, axis=0):
    return lax.dynamic_index_in_dim(value, index, axis, keepdims=False)


def head_first_parts(*terms):
    head = lax.axis_index("head")
    x, y = head % 2, head // 2
    cut = terms[0].shape[1] // 2
    squares = [term.reshape((2, 2) + term.shape[1:]) for term in terms]
    first = lambda index: add_parts(*[pick(square[:, :, :cut], index, 1) for square in squares])
    second = lambda index: add_parts(*[pick(square[:, :, cut:], index, 0) for square in squares])
    return (first(1 - x), second(1 - y)), (first(x), second(y))


def head_first_send(sent):
    return permute_xor(sent[0], "head", 1), permute_xor(sent[1], "head", 2)


def head_second_parts(kept, arrived):
    head = lax.axis_index("head")
    x, y = head % 2, head // 2
    first, second = zip(kept, arrived)
    part = lambda terms, index: add_parts(*[pick(term, index) for term in terms])
    return (part(first, 1 - y), part(second, 1 - x)), (part(first, y), part(second, x))


def head_second_send(sent):
    return permute_xor(sent[0], "head", 2), permute_xor(sent[1], "head", 1)


def add_pairs(kept, arrived):
    return [add_parts(one, two) for one, two in zip(kept, arrived)]


TOGETHER = 4
BUNDLE = TOGETHER * 36


def owned_kernel(panel_ref, lane_ref, odd_ref, sheet_ref, carried_ref, out_ref, carried_out):
    del carried_ref, carried_out
    first = pl.program_id(0) * out_ref.shape[0] * TOGETHER
    half = low_lanes(24)

    def bundle(place, carry):
        mains, rests = [], []
        for index in range(TOGETHER):
            slot = first + place * TOGETHER + index
            panel, odd = panel_ref[slot], odd_ref[slot] == 1
            pair = panel // 2
            lane = pl.multiple_of(lane_ref[slot], LANES)
            main_lane = pl.multiple_of(lane + jnp.where(odd, 2 * LANES, 0), LANES)
            values = []
            for begin in (main_lane, pl.multiple_of(lane + LANES, LANES)):
                value = sheet_ref[pair, :, pl.ds(begin, LANES)].astype(F32)
                values.append(jnp.where(panel % 2 == 1, value[24:], value[:24]))
            mains.append(values[0])
            turn = odd if index % 2 == 0 else jnp.logical_not(odd)
            rests.append(jnp.where(turn, pltpu.roll(values[1], LANES // 2, 1), values[1]))
        rests = [jnp.where(half, rests[i], rests[i + 1]) for i in range(0, TOGETHER, 2)]
        out_ref[place] = jnp.concatenate(mains + rests, axis=0).astype(BF16)
        return carry

    lax.fori_loop(0, out_ref.shape[0], bundle, 0, unroll=2)


def by_owner(sheet_gradient, owner_order, carried):
    owners = lax.axis_size("seq")
    count = NBLK // owners
    bundles = -(-count // TOGETHER)
    slots = jnp.pad(owner_order.reshape(owners, count), ((0, 0), (0, bundles * TOGETHER - count)))
    slots = slots.reshape(-1)
    steps = 4 if owners * bundles % 4 == 0 else 1
    each = owners * bundles // steps
    panels = jnp.asarray(panel_of_block())
    whole = jnp.arange(NBLK, dtype=jnp.int32)
    panels = jnp.sum(jnp.where(slots[:, None] == whole[None, :], panels[None, :], 0), axis=1)
    gathered, carried = pl.pallas_call(
        owned_kernel,
        grid_spec=pltpu.PrefetchScalarGridSpec(
            num_scalar_prefetch=3,
            grid=(steps,),
            in_specs=[pl.BlockSpec(sheet_gradient.shape, lambda i, *_: (0, 0, 0)), ANYWHERE],
            out_specs=[pl.BlockSpec((each, BUNDLE, LANES), lambda i, *_: (i, 0, 0)), ANYWHERE],
        ),
        out_shape=[
            jax.ShapeDtypeStruct((owners * bundles, BUNDLE, LANES), BF16),
            jax.ShapeDtypeStruct(carried.shape, carried.dtype),
        ],
        input_output_aliases={4: 1},
        compiler_params=pltpu.CompilerParams(vmem_limit_bytes=24 * MEBI),
        cost_estimate=cost(0, 4 * MEBI),
        name="gradients_by_owner",
    )(panels, slots // 2 % 2 * 384, slots % 2, sheet_gradient, carried)
    return gathered.reshape(owners // 2, 2, bundles, BUNDLE, LANES), carried


def add_tree(terms):
    while len(terms) > 1:
        terms = [one + two for one, two in zip(terms[::2], terms[1::2])]
    return terms[0]


def two_parts(value):
    high = lax.reduce_precision(value, 8, 7)
    return high, lax.reduce_precision(value - high, 8, 7)


def sum_to_owners(parts, sums, others):
    chips = lax.axis_size("seq") // 2
    seq = lax.axis_index("seq")
    chip, core = seq // 2, seq % 2
    shape = parts.shape[2:]
    flat = lambda value: value.reshape((-1,) + shape[1:])

    def with_sums(value, total):
        high, low = two_parts(total)
        both = jnp.concatenate([high, low]).astype(BF16)
        return jnp.concatenate([flat(value), flat(both)])

    def split_sums(value):
        high, low = value[-1].astype(F32).reshape((2,) + sums.shape)
        return value[:-1], high + low

    packed = flat if sums is None else functools.partial(with_sums, total=sums)
    arrived = [packed(pick(parts, chip))]
    for mask in range(1, chips):
        arrived.append(permute_xor(packed(pick(parts, chip ^ mask)), "seq", 2 * mask))
    if others:
        arrived[1:] = gate(arrived[1:], others)
    if sums is not None:
        split = [split_sums(value) for value in arrived]
        arrived = [value for value, _ in split]
        sums = add_tree([total for _, total in split])
    mine = add_parts(*arrived).reshape((2,) + shape)
    packed = flat if sums is None else functools.partial(with_sums, total=sums)
    other = permute_xor(packed(pick(mine, 1 - core)), "seq", 1)
    if sums is not None:
        other, total = split_sums(other)
        high, low = two_parts(sums)
        sums = (high + low) + total
    return jnp.stack([pick(mine, core), other.reshape(shape)]), sums


def gather_quarters(part):
    return [part] + [permute_xor(part, "head", mask) for mask in (1, 2, 3)]


def shampoo_kernel(
    base,
    held,
    number_ref,
    place_ref,
    part0,
    part1,
    part2,
    part3,
    momentum_ref,
    left_ref,
    right_ref,
    root_left_ref,
    root_right_ref,
    master_ref,
    *refs,
):
    new_momentum_ref, new_left_ref, new_right_ref, new_master_ref, main_ref, rest_ref = refs[held:]
    count = momentum_ref.shape[0]
    first = (base + pl.program_id(0)) * count
    low = low_lanes(B)
    half = low_lanes(24)
    core = place_ref[4]
    for slot in range(count):
        odd = number_ref[first + slot] % 2 == 1
        for index, part in enumerate((part0, part1, part2, part3)):
            for which in range(2):
                row = pl.multiple_of(place_ref[index] * 48 + (which ^ core) * 24, 8)
                bundle = part[which, slot // TOGETHER].astype(F32)
                inside = slot % TOGETHER
                main_ref[pl.ds(row, 24), :] = bundle[inside * 24 : inside * 24 + 24]
                begin = TOGETHER * 24 + inside // 2 * 24
                rest_ref[pl.ds(row, 24), :] = bundle[begin : begin + 24]
        main = main_ref[...]
        rest = rest_ref[...]
        spun = pltpu.roll(main, LANES // 2, 1)
        rest_low = rest if slot % 2 == 0 else pltpu.roll(rest, LANES // 2, 1)
        left_lanes = jnp.where(odd, jnp.where(low, rest_low, spun), main)
        right_lanes = jnp.where(odd, spun, rest_low)
        gradient = jnp.concatenate([left_lanes, right_lanes[:, : LANES // 2]], axis=1)
        new_momentum = MOMENTUM_DECAY * momentum_ref[slot] + (1.0 - MOMENTUM_DECAY) * gradient
        new_momentum_ref[slot] = new_momentum
        grad_low = gradient.astype(BF16)
        new_left_ref[slot] = STAT_DECAY * left_ref[slot] + (1.0 - STAT_DECAY) * dot(
            grad_low, grad_low, ((1,), (1,))
        )
        new_right_ref[slot] = STAT_DECAY * right_ref[slot] + (1.0 - STAT_DECAY) * dot(
            grad_low, grad_low, ((0,), (0,))
        )
        leftward = dot(root_left_ref[slot].astype(BF16), new_momentum.astype(BF16))
        preconditioned = dot(leftward.astype(BF16), root_right_ref[slot].astype(BF16))
        master = master_ref[slot]
        new_master_ref[slot] = master - MATRIX_RATE * (preconditioned + WEIGHT_DECAY * master)


def shampoo(numbers, parts, states, first, earlier, others):
    group = TOGETHER if numbers.shape[0] % TOGETHER == 0 else numbers.shape[0]
    steps = parts[0].shape[1]
    base = first // group
    spec = pl.BlockSpec((group, B, B), lambda i, *_: (base + i, 0, 0))
    part_spec = pl.BlockSpec((2, 1, BUNDLE, LANES), lambda i, *_: (0, i, 0, 0))
    places = lax.axis_index("head") ^ jnp.arange(4, dtype=jnp.int32)
    places = jnp.concatenate([places, (lax.axis_index("seq") % 2).reshape(1).astype(jnp.int32)])
    return pl.pallas_call(
        functools.partial(shampoo_kernel, base, len(earlier) + len(others)),
        grid_spec=pltpu.PrefetchScalarGridSpec(
            num_scalar_prefetch=2,
            grid=(steps,),
            in_specs=[part_spec] * 4
            + [spec] * 6
            + [ANYWHERE] * (len(earlier) + len(others)),
            out_specs=[spec] * 4,
            scratch_shapes=[pltpu.VMEM((B, LANES), F32), pltpu.VMEM((B, LANES), F32)],
        ),
        out_shape=[jax.ShapeDtypeStruct((numbers.shape[0], B, B), F32)] * 4,
        input_output_aliases={12 + i: i for i in range(len(earlier))},
        compiler_params=pltpu.CompilerParams(vmem_limit_bytes=48 * MEBI),
        cost_estimate=cost(8 * steps * group * B**3, 10 * steps * group * B * B * 4),
        name="shampoo_blocks",
    )(numbers, places, *parts, *states, *earlier, *others)


def adam_step(vector_grad, vec_first, vec_second, vectors):
    new_first = FIRST_DECAY * vec_first + (1.0 - FIRST_DECAY) * vector_grad
    new_second = SECOND_DECAY * vec_second + (1.0 - SECOND_DECAY) * vector_grad * vector_grad
    corrected_first = new_first / (1.0 - FIRST_DECAY**STEP)
    corrected_second = new_second / (1.0 - SECOND_DECAY**STEP)
    new_vectors = vectors - VECTOR_RATE * corrected_first / (
        jnp.sqrt(corrected_second) + ADAM_EPSILON
    )
    return (new_first, new_second, new_vectors)


def exchange_rows(value):
    return lax.all_to_all(value, "head", split_axis=0, concat_axis=0, tiled=True)


def parts_to_send(value):
    head = lax.axis_index("head")
    return [pick(value, head ^ mask) for mask in (1, 2, 3)]


def send_rows(parts):
    return [permute_xor(part, "head", mask) for mask, part in enumerate(parts, 1)]


def arrange_rows(value, arrived):
    head = lax.axis_index("head")
    result = value
    for mask, piece in enumerate(arrived, 1):
        result = lax.dynamic_update_index_in_dim(result, piece, head ^ mask, 0)
    return result


def local(
    tokens,
    cotangent,
    segment_ids,
    owner_order,
    master_blocks,
    momentum,
    stat_left,
    stat_right,
    root_left,
    root_right,
    vectors,
    vec_first,
    vec_second,
):
    width = MODEL_WIDTH
    count = master_blocks.shape[0]
    head = lax.axis_index("head")
    numbers = lax.dynamic_slice_in_dim(owner_order, lax.axis_index("seq") * count, count, 0)
    sheet_vectors = vectors.reshape(12, width)

    labels = lax.dynamic_index_in_dim(segment_ids, head, 0, keepdims=False)
    early = [sheet_vectors, labels.reshape(1, -1), labels.reshape(-1, 1)]
    early += [*key_tiles(labels, *FORWARD_TILES), *key_tiles(labels, *BACKWARD_TILES)]
    early += [exchange_rows(tokens).reshape(ROW_POSITIONS, width)]
    packed = pack_blocks(numbers, master_blocks)
    blocks, source_numbers, early = gather_weights(packed, owner_order, early)
    sheet_vectors, label_row, label_column = early[:3]
    wide_tiles, tiles, x = early[3:5], early[5:7], early[7]
    upstream = [pick(cotangent, head), *send_rows(parts_to_send(cotangent))]

    projected, input_sheet = project(x, sheet_vectors, blocks, source_numbers)
    attended, logs, sheet = attention_forward(
        projected, wide_tiles, label_row, label_column, blocks, source_numbers
    )
    upstream[1:] = gate(upstream[1:], [attended])
    (
        output,
        normed_low,
        activated,
        d_before,
        d_feed,
        d_first,
        d_branch,
        d_attended,
        sums,
    ) = middle(attended, x, upstream, sheet_vectors, sheet)
    def backward(index, *others):
        return attention_backward(
            projected, tiles, label_row, label_column, d_attended, logs, index, others
        )

    output = output.reshape(tokens.shape)
    output_sent = parts_to_send(output)
    feed, feed_sent = feed_gradients(normed_low, d_before, activated, d_feed, [])
    parts = [backward(0, feed, feed_sent, *output_sent)]
    feed = add_parts(feed, *gate([permute_xor(feed_sent, "seq", 1)], parts[0][:1]))
    feed_sent, feed = head_first_parts(feed)
    output_arrived = gate(send_rows(output_sent), feed_sent)
    parts.append(backward(1, parts[0][0], *feed_sent, *output_arrived))
    parts.append(backward(2, parts[1][0]))
    feed_sent, feed = head_second_parts(feed, gate(head_first_send(feed_sent), parts[2][:1]))
    d_projected = [part[0] for part in parts]
    rest, rest_sent = attention_gradients(x, attended, d_branch, d_projected, feed_sent)
    feed = jnp.concatenate(add_pairs(feed, gate(head_second_send(feed_sent), [rest])))
    rest_sent, rest = head_first_parts(
        rest, *gate([permute_xor(rest_sent, "seq", 1)], [feed])
    )
    bias_sums = jnp.concatenate([part[1] for part in parts], axis=1)
    sums = jnp.concatenate([sums[:4], bias_sums[:2], sums[6:]])
    input_grad = input_gradient(d_projected, input_sheet, d_first, rest_sent)
    arrived = [permute_xor(sums, "head", mask) for mask in (1, 2, 3)]
    sums = add_tree([sums, *gate(arrived, [input_grad])])
    rest_sent, rest = head_second_parts(rest, gate(head_first_send(rest_sent), [input_grad]))
    rest = jnp.concatenate(add_pairs(rest, head_second_send(rest_sent)))
    owned, input_grad = by_owner(jnp.concatenate([rest, feed]), owner_order, input_grad)
    input_grad = exchange_rows(input_grad.reshape(tokens.shape))
    output = arrange_rows(output, output_arrived)
    bundles = owned.shape[2]
    halves = 2 if bundles % 2 == 0 else 1
    each = bundles // halves
    states = (momentum, stat_left, stat_right, root_left, root_right, master_blocks)
    if halves == 1:
        part, total = sum_to_owners(owned, sums, [])
        blocks = shampoo(numbers, gather_quarters(part), states, 0, (), [])
        input_grad = input_grad.astype(F32)
    else:
        part, _ = sum_to_owners(owned[:, :, :each], None, [])
        quarters = gather_quarters(part)
        part, total = sum_to_owners(owned[:, :, each:], sums, [*quarters[1:], input_grad])
        input_grad = input_grad.astype(F32)
        blocks = shampoo(numbers, quarters, states, 0, (), [part])
        quarters = gather_quarters(part)
        blocks = shampoo(numbers, quarters, states, each * TOGETHER, blocks, [input_grad, output])
    new_first, new_second, new_vectors = adam_step(total.reshape(-1), vec_first, vec_second, vectors)

    new_momentum, new_left, new_right, new_master = blocks
    return (
        output,
        input_grad,
        new_momentum,
        new_left,
        new_right,
        new_master,
        new_first,
        new_second,
        new_vectors,
    )


def solution(mesh):
    blocks = P("seq", None, None)
    positions = P("seq", "head", None)
    return jax.shard_map(
        local,
        mesh=mesh,
        in_specs=(positions, positions, P("seq", None), P()) + (blocks,) * 6 + (P(),) * 3,
        out_specs=(positions, positions) + (blocks,) * 4 + (P(),) * 3,
        check_vma=False,
    )
```
